1024 devices in a mesh: comp: 2 (over core), gy: 8 (over y, x_hi), gx: 64 (over x_lo, z).
Axes of the slice: x: 4 (x_hi: 2, x_lo: 2; x = x_hi * 2 + x_lo), y: 4, z: 32, core: 2. Of those that a mesh axis runs over, the one named last changes fastest.
Arguments:
- ocean_state: float32 [16, 8, 256, 1024], P('comp', None, 'gx', 'gy'), may hold values from -4 to 4, as said below
- irradiance: float32 [256, 1024], P('gx', 'gy'), may hold values from 0.5 to 4
- land_mask: int32 [256, 1024], P('gx', 'gy'), may hold values 0 or 1
- bottom_level: int32 [256, 1024], P('gx', 'gy'), may hold values from 1 to 8
Outputs:
- new_state: float32 [16, 8, 256, 1024], P('comp', None, 'gx', 'gy')
The draws below stay inside these ranges and needn't reach their ends.
Inputs may be any that keep to these rules, and one draw needn't show every extreme that they name: `ocean_state`: channels 0 to 3 hold velocity along x, velocity along y, temperature and salinity now, channels 4 to 7 the same one step earlier; the 8 tracer channels are positive.
All inputs are finite; a program needn't handle non-finite values. No bound on the sum of `land_mask` on one device may be relied on, other than what follows from the above.
Results may differ from the reference program's by a relative error of at most 0.0003.
Values sent between devices are 32-bit elements; how exact they have to be, the bound alone decides.
A program may use at most 32 MiB of HBM per device.

```python
import math
import jax
import jax.numpy as jnp
from jax import lax

TRACERS = 8
LEV = 8
CX = 4
STEPS = 2
NX = 256
NY = 1024


def draw_ocean_state(key, part):
    shape = (TRACERS, LEV, NX, NY)
    key_flow = jax.random.fold_in(key, 11)
    key_bgc = jax.random.fold_in(key, 12)
    dynamics = jnp.clip(jax.random.normal(key_flow, shape, jnp.float32), -4.0, 4.0)
    tracers = jnp.exp(jax.random.uniform(key_bgc, shape, jnp.float32, math.log(0.1), math.log(3.0)))
    return jnp.concatenate([dynamics, tracers], axis=0)


def plant(entries, own_key, low, high):
    index_at = [jax.random.randint(jax.random.fold_in(own_key, axis), (), 0, length) for axis, length in enumerate(entries.shape)]
    longest = entries.shape.index(max(entries.shape))
    beside = index_at[:longest] + [(index_at[longest] + 1) % entries.shape[longest]] + index_at[longest + 1:]
    return entries.at[tuple(index_at)].set(low).at[tuple(beside)].set(high)


def level_of(stream_key, shape, pieces, least, top_value):
    gain = 1.0
    for position, parts in pieces:
        heights = jax.random.uniform(jax.random.fold_in(jax.random.fold_in(stream_key, 6), position), (parts,), jnp.float32, least / len(pieces), top_value / len(pieces))
        gain = gain * jnp.repeat(jnp.exp(heights), shape[position] // parts).reshape((-1,) + (1,) * (len(shape) - 1 - position))
    return gain


def setup_inputs(seed: int = 0) -> dict:
    arg_keys = jax.random.split(jax.random.key(seed), 5)
    ocean_state = draw_ocean_state(jax.random.fold_in(arg_keys[4], 71), 0)
    irradiance = jnp.clip(jnp.exp(math.log(4.0) - 2.0794415 * jax.random.uniform(arg_keys[1], (NX, NY), jnp.float32) ** level_of(arg_keys[1], (NX, NY), ((0, 64), (1, 8)), -0.2, 0.2)), 0.5, 4.0)
    land_mask = plant((jax.random.randint(arg_keys[2], (NX, NY), 0, 8) < 7).astype(jnp.int32), jax.random.fold_in(arg_keys[2], 1), 0, 1)
    bottom_level = plant(jax.random.randint(arg_keys[3], (NX, NY), 1, LEV + 1), jax.random.fold_in(arg_keys[3], 1), 1, LEV).astype(jnp.int32)
    return dict(ocean_state=ocean_state, irradiance=irradiance, land_mask=land_mask, bottom_level=bottom_level)


TIME_STEP = 0.1
VISCOSITY = 0.2
DIFFUSION = 0.2
ASSELIN_GAIN = 0.1
THERMAL_EXPAND = 0.2
HALINE_CONTRACT = 0.8
GRAVITY_STEP = 0.1
CORIOLIS_BASE = 0.3
CORIOLIS_SLOPE = 0.4
MIXING_FLOOR = 0.05
MIXING_SPAN = 1.0
STRATIFICATION = 4.0
HEATING_GAIN = 3.0
WATER_ABSORB = 0.08
PIGMENT_ABSORB = 0.05
LIGHT_HALF = 0.5
THERMAL_GAIN_PER = 0.06
GROWTH_SMALL = 0.6
GROWTH_LARGE = 0.9
NUTRIENT_HALF_SMALL = 0.2
NUTRIENT_HALF_LARGE = 0.8
GRAZING_RATE = 0.8
GRAZING_HALF = 1.0
PHYTO_DEATH = 0.1
ZOOPLANKTON_DEATH = 0.15
EXCRETION = 0.1
ASSIMILATION = 0.7
REMINERAL_SMALL = 0.3
REMINERAL_LARGE = 0.1
NITRIFICATION = 0.2
OXYGEN_YIELD = 1.3
OXYGEN_DEMAND = 1.0


def interior(field_in):
    return field_in[..., 1:-1, 1:-1]


def neighbours(field_in):
    return (field_in[..., 2:, 1:-1], field_in[..., :-2, 1:-1], field_in[..., 1:-1, 2:], field_in[..., 1:-1, :-2])


def laplacian(field_in, entire_ocean_indicator):
    centre = interior(field_in)
    total = jnp.zeros_like(centre)
    for other, wet_other in zip(neighbours(field_in), neighbours(entire_ocean_indicator)):
        total = total + wet_other * (other - centre)
    return total * interior(entire_ocean_indicator)


def advection(east_speed, north_speed, field_in, entire_ocean_indicator):
    centre = interior(field_in)
    wet_centre = interior(entire_ocean_indicator)
    east_centre = interior(east_speed)
    north_centre = interior(north_speed)
    field_near = neighbours(field_in)
    wet_near = neighbours(entire_ocean_indicator)
    east_near = neighbours(east_speed)
    north_near = neighbours(north_speed)
    flux_east = 0.25 * (east_centre + east_near[0]) * (centre + field_near[0]) * wet_centre * wet_near[0]
    flux_west = 0.25 * (east_centre + east_near[1]) * (centre + field_near[1]) * wet_centre * wet_near[1]
    flux_north = 0.25 * (north_centre + north_near[2]) * (centre + field_near[2]) * wet_centre * wet_near[2]
    flux_south = 0.25 * (north_centre + north_near[3]) * (centre + field_near[3]) * wet_centre * wet_near[3]
    return flux_east - flux_west + flux_north - flux_south


def pressure_force(pressure, entire_ocean_indicator):
    centre = interior(pressure)
    wet_centre = interior(entire_ocean_indicator)
    near = neighbours(pressure)
    wet_near = neighbours(entire_ocean_indicator)
    force_east = 0.5 * wet_centre * (wet_near[0] * (near[0] - centre) + wet_near[1] * (centre - near[1]))
    force_north = 0.5 * wet_centre * (wet_near[2] * (near[2] - centre) + wet_near[3] * (centre - near[3]))
    return force_east, force_north


def ocean_water_mass_per_volume(thermal_state_grid, salt_content_grid, entire_ocean_indicator):
    return (HALINE_CONTRACT * salt_content_grid - THERMAL_EXPAND * thermal_state_grid) * entire_ocean_indicator


def make_flow(dynamics_full, entire_ocean_indicator):
    density = ocean_water_mass_per_volume(dynamics_full[2], dynamics_full[3], entire_ocean_indicator)
    below = jnp.concatenate([density[1:], density[-1:]], axis=0)
    wet_below = jnp.concatenate([entire_ocean_indicator[1:], jnp.zeros_like(entire_ocean_indicator[:1])], axis=0)
    strat = jnp.maximum(below - density, 0.0)
    mixing = (MIXING_FLOOR + MIXING_SPAN / (1.0 + STRATIFICATION * strat)) * entire_ocean_indicator * wet_below
    return jnp.stack([dynamics_full[0], dynamics_full[1], dynamics_full[2], mixing], axis=0)


def absorption(arriving_constituents, lit_in):
    wet_centre = (lit_in > 0).astype(jnp.float32)
    surface = lit_in[0]
    pigment = jnp.abs(arriving_constituents[2]) + jnp.abs(arriving_constituents[3])
    absorb = WATER_ABSORB + PIGMENT_ABSORB * pigment
    column = jnp.cumsum(absorb, axis=0)
    heating = surface * (jnp.exp(absorb - column) - jnp.exp(-column)) * wet_centre
    middle = surface * jnp.exp(0.5 * absorb - column)
    return heating, middle


def biotic_source_terms(arriving_constituents, thermal_state_grid, layer_centre_irradiance):
    nitrate, ammonium, small_phyto, large_phyto = arriving_constituents[0], arriving_constituents[1], arriving_constituents[2], arriving_constituents[3]
    grazers, small_detritus, large_detritus = arriving_constituents[4], arriving_constituents[5], arriving_constituents[6]
    nitrate_size = jnp.abs(nitrate)
    ammonium_size = jnp.abs(ammonium)
    light_limit = layer_centre_irradiance / (layer_centre_irradiance + LIGHT_HALF)
    thermal_change_per_step = jnp.exp(THERMAL_GAIN_PER * thermal_state_grid)
    small_common = GROWTH_SMALL * thermal_change_per_step * light_limit * small_phyto / (NUTRIENT_HALF_SMALL + nitrate_size + ammonium_size)
    large_common = GROWTH_LARGE * thermal_change_per_step * light_limit * large_phyto / (NUTRIENT_HALF_LARGE + nitrate_size + ammonium_size)
    small_nitrate = small_common * nitrate_size
    small_ammonium = small_common * ammonium_size
    large_nitrate = large_common * nitrate_size
    large_ammonium = large_common * ammonium_size
    prey = jnp.abs(small_phyto) + jnp.abs(large_phyto)
    graze_factor = GRAZING_RATE * grazers / (GRAZING_HALF + prey)
    graze_small = graze_factor * small_phyto
    graze_large = graze_factor * large_phyto
    remin = REMINERAL_SMALL * small_detritus + REMINERAL_LARGE * large_detritus
    nitrify = NITRIFICATION * ammonium
    growth = small_nitrate + small_ammonium + large_nitrate + large_ammonium
    tend_nitrate = nitrify - small_nitrate - large_nitrate
    tend_ammonium = remin + EXCRETION * grazers - nitrify - small_ammonium - large_ammonium
    tend_small = small_nitrate + small_ammonium - graze_small - PHYTO_DEATH * small_phyto
    tend_large = large_nitrate + large_ammonium - graze_large - PHYTO_DEATH * large_phyto
    tend_grazers = ASSIMILATION * (graze_small + graze_large) - EXCRETION * grazers - ZOOPLANKTON_DEATH * grazers
    tend_small_det = PHYTO_DEATH * small_phyto + (1.0 - ASSIMILATION) * graze_small - REMINERAL_SMALL * small_detritus
    tend_large_det = (PHYTO_DEATH * large_phyto + ZOOPLANKTON_DEATH * grazers
                      + (1.0 - ASSIMILATION) * graze_large - REMINERAL_LARGE * large_detritus)
    tend_oxygen = OXYGEN_YIELD * growth - OXYGEN_DEMAND * (remin + 2.0 * nitrify)
    return jnp.stack([tend_nitrate, tend_ammonium, tend_small, tend_large, tend_grazers,
                      tend_small_det, tend_large_det, tend_oxygen], axis=0)


def dynamics_update(dynamics_full, entire_ocean_indicator, heating, row_start, total_rows):
    wet_centre = interior(entire_ocean_indicator)
    density = ocean_water_mass_per_volume(dynamics_full[2], dynamics_full[3], entire_ocean_indicator)
    pressure = GRAVITY_STEP * jnp.cumsum(density, axis=0)
    force_east, force_north = pressure_force(pressure, entire_ocean_indicator)
    row_count = dynamics_full.shape[3] - 2
    row_index = (jnp.arange(row_count, dtype=jnp.int32) + row_start + 1).astype(jnp.float32)
    coriolis = CORIOLIS_BASE + CORIOLIS_SLOPE * row_index / total_rows
    earlier = dynamics_full[4:8]
    diffused = laplacian(earlier, entire_ocean_indicator)
    carried = advection(dynamics_full[0], dynamics_full[1], dynamics_full[2:4], entire_ocean_indicator)
    now_centre = interior(dynamics_full[0:4])
    tend_east = coriolis * now_centre[1] - force_east + VISCOSITY * diffused[0]
    tend_north = -coriolis * now_centre[0] - force_north + VISCOSITY * diffused[1]
    tend_temp = -carried[0] + DIFFUSION * diffused[2] + HEATING_GAIN * heating
    tend_salt = -carried[1] + DIFFUSION * diffused[3]
    tendency = jnp.stack([tend_east, tend_north, tend_temp, tend_salt], axis=0)
    earlier_centre = interior(earlier)
    after = earlier_centre + 2.0 * TIME_STEP * tendency * wet_centre
    filtered = now_centre + ASSELIN_GAIN * (earlier_centre - 2.0 * now_centre + after) * wet_centre
    return jnp.concatenate([after, filtered], axis=0)


def tracer_update(tracers_full, flow_full, entire_ocean_indicator, middle):
    wet_centre = interior(entire_ocean_indicator)
    centre = interior(tracers_full)
    carried = advection(flow_full[0], flow_full[1], tracers_full, entire_ocean_indicator)
    spread = laplacian(tracers_full, entire_ocean_indicator)
    mixing = interior(flow_full[3])
    below = jnp.concatenate([centre[:, 1:], jnp.zeros_like(centre[:, :1])], axis=1)
    flux_down = mixing * (below - centre)
    flux_above = jnp.concatenate([jnp.zeros_like(flux_down[:, :1]), flux_down[:, :-1]], axis=1)
    vertical = flux_down - flux_above
    react = biotic_source_terms(centre, interior(flow_full[2]), middle)
    return centre + TIME_STEP * (DIFFUSION * spread - carried + vertical + react) * wet_centre


def pad_global(field_in):
    wrapped = jnp.concatenate([field_in[..., -1:, :], field_in, field_in[..., :1, :]], axis=-2)
    zero_row = jnp.zeros_like(wrapped[..., :1])
    return jnp.concatenate([zero_row, wrapped, zero_row], axis=-1)


def reference(ocean_state, irradiance, land_mask, bottom_level):
    depth_index = jnp.arange(LEV, dtype=jnp.int32)[:, None, None]
    wet_cells = ((land_mask[None] == 1) & (depth_index < bottom_level[None])).astype(jnp.float32)
    lit_wet = irradiance[None] * wet_cells
    lit_padded = pad_global(lit_wet)
    dynamics = ocean_state[:TRACERS]
    tracers = ocean_state[TRACERS:]
    offsets = jnp.arange(NX // CX, dtype=jnp.int32) * CX
    for step_index in range(STEPS):
        dyn_padded = pad_global(dynamics)
        trc_padded = pad_global(tracers)

        def tile_step(offset):
            dyn_tile = lax.dynamic_slice_in_dim(dyn_padded, offset, CX + 2, axis=2)
            trc_tile = lax.dynamic_slice_in_dim(trc_padded, offset, CX + 2, axis=2)
            lit_tile = lax.dynamic_slice_in_dim(lit_padded, offset, CX + 2, axis=1)
            wet_tile = (lit_tile > 0).astype(jnp.float32)
            partner_flow = make_flow(dyn_tile, wet_tile)
            heating, middle = absorption(interior(trc_tile), interior(lit_tile))
            new_dyn = dynamics_update(dyn_tile, wet_tile, heating, -1, NY)
            new_trc = tracer_update(trc_tile, partner_flow, wet_tile, middle)
            return new_dyn, new_trc

        new_dyn, new_trc = lax.map(tile_step, offsets)
        dynamics = jnp.transpose(new_dyn, (1, 2, 0, 3, 4)).reshape(TRACERS, LEV, NX, NY)
        tracers = jnp.transpose(new_trc, (1, 2, 0, 3, 4)).reshape(TRACERS, LEV, NX, NY)
    return jnp.concatenate([dynamics, tracers], axis=0)
```

```python
import functools

import jax
import jax.numpy as jnp
from jax import lax
from jax.experimental import pallas as pl
from jax.experimental.pallas import tpu as pltpu
from jax.sharding import PartitionSpec as P

MESH = pl.DeviceIdType.MESH

SOUTH, NORTH, SW, SE, NW, NE = range(6)
OWN = 2
LEV, LANES = 8, 128


def roll(value, shift, axis):
    return pltpu.roll(value, shift % value.shape[axis], axis)


def lanes(value, shift):
    return roll(value, shift, value.ndim - 1)


def levels(value, shift):
    return roll(value, shift, value.ndim - 2)


def iota(dim):
    return lax.broadcasted_iota(jnp.int32, (LEV, LANES), dim)


def level_sum(value):
    k = iota(0)
    for shift in (1, 2, 4):
        value = value + jnp.where(k >= shift, levels(value, shift), 0.0)
    return value


def density(temp, salt, wet):
    return (0.8 * salt - 0.2 * temp) * wet


def pressure_of(temp, salt, wet):
    return 0.1 * level_sum(density(temp, salt, wet))


def mixing_of(temp, salt, wet):
    rho = density(temp, salt, wet)
    strat = jnp.maximum(levels(rho, -1) - rho, 0.0)
    wet_below = jnp.where(iota(0) == LEV - 1, 0.0, levels(wet, -1))
    return (0.05 + 1.0 / (1.0 + 4.0 * strat)) * wet * wet_below


def absorbed(small, large):
    absorb = 0.08 + 0.05 * (jnp.abs(small) + jnp.abs(large))
    return absorb, level_sum(absorb)


def surface_of(lit):
    return jnp.broadcast_to(lit[0:1, :], (LEV, LANES))


def heating_of(small, large, lit, wet):
    absorb, column = absorbed(small, large)
    return surface_of(lit) * (jnp.exp(absorb - column) - jnp.exp(-column)) * wet


def light_of(small, large, lit):
    absorb, column = absorbed(small, large)
    return surface_of(lit) * jnp.exp(0.5 * absorb - column)


def gradients(p, wet):
    pc, pe, pw, pn, ps = p
    _, we, ww, wn, ws = wet
    return 0.5 * (we * (pe - pc) + ww * (pc - pw)), 0.5 * (wn * (pn - pc) + ws * (pc - ps))


def spread_of(field, wet):
    c, e, w, n, s = field
    _, we, ww, wn, ws = wet
    return we * (e - c) + ww * (w - c) + wn * (n - c) + ws * (s - c)


def faces(u, v, wet):
    (uc, ue, uw), (vc, vn, vs) = u, v
    _, we, ww, wn, ws = wet
    return 0.25 * (uc + ue) * we, 0.25 * (uc + uw) * ww, 0.25 * (vc + vn) * wn, 0.25 * (vc + vs) * ws


def carried_of(field, face):
    c, e, w, n, s = field
    fe, fw, fn, fs = face
    return fe * (c + e) - fw * (c + w) + fn * (c + n) - fs * (c + s)


def pick(five, index):
    return tuple(part[index] for part in five)


def step_speeds(now, before, p, wet, coriolis):
    force_east, force_north = gradients(p, wet)
    u, v = now[0][0], now[0][1]
    du = coriolis * v - force_east + 0.2 * spread_of(pick(before, 0), wet)
    dv = -coriolis * u - force_north + 0.2 * spread_of(pick(before, 1), wet)
    return before[0][0] + 0.2 * du * wet[0], before[0][1] + 0.2 * dv * wet[0]


def step_heat_salt(now, before, wet, heating):
    u = (now[0][0], now[1][0], now[2][0])
    v = (now[0][1], now[3][1], now[4][1])
    face = faces(u, v, wet)
    dt = -carried_of(pick(now, 2), face) + 0.2 * spread_of(pick(before, 2), wet) + 3.0 * heating
    ds = -carried_of(pick(now, 3), face) + 0.2 * spread_of(pick(before, 3), wet)
    return before[0][2] + 0.2 * dt * wet[0], before[0][3] + 0.2 * ds * wet[0]


def filtered(now, before, after, wet):
    return now + 0.1 * (before - 2.0 * now + after) * wet


def transported(field, u, v, wet):
    c, e, w, n, s = field
    _, we, ww, wn, ws = wet
    fe, fw, fn, fs = faces(u, v, wet)
    le, lw, ln, ls = 0.2 * we, 0.2 * ww, 0.2 * wn, 0.2 * ws
    own = (le + fe) + (lw - fw) + (ln + fn) + (ls - fs)
    return (le - fe) * e + (lw + fw) * w + (ln - fn) * n + (ls + fs) * s - own * c


def mixed(c, kappa):
    down = kappa * (levels(c, -1) - c)
    return down - levels(down, 1)


def growth_of(nitrate, ammonium, small, large, temp, light):
    rate = jnp.exp(0.06 * temp) * (light / (light + 0.5))
    both = jnp.abs(nitrate) + jnp.abs(ammonium)
    return 0.6 * rate * small / (0.2 + both), 0.9 * rate * large / (0.8 + both)


def reactions(c, temp, light):
    nn, na = jnp.abs(c[0]), jnp.abs(c[1])
    small, large = growth_of(c[0], c[1], c[2], c[3], temp, light)
    sn, sa, ln, la = small * nn, small * na, large * nn, large * na
    graze = 0.8 * c[4] / (1.0 + jnp.abs(c[2]) + jnp.abs(c[3]))
    gs, gl = graze * c[2], graze * c[3]
    remin = 0.3 * c[5] + 0.1 * c[6]
    nitrify = 0.2 * c[1]
    return jnp.stack(
        [
            nitrify - sn - ln,
            remin + 0.1 * c[4] - nitrify - sa - la,
            sn + sa - gs - 0.1 * c[2],
            ln + la - gl - 0.1 * c[3],
            0.7 * (gs + gl) - 0.1 * c[4] - 0.15 * c[4],
            0.1 * c[2] + 0.3 * gs - 0.3 * c[5],
            0.1 * c[3] + 0.15 * c[4] + 0.3 * gl - 0.1 * c[6],
            1.3 * (sn + sa + ln + la) - (remin + 2.0 * nitrify),
        ]
    )


def plant_reactions(c, temp, light):
    both = jnp.abs(c[0]) + jnp.abs(c[1])
    small, large = growth_of(c[0], c[1], c[2], c[3], temp, light)
    graze = 0.8 * c[4] / (1.0 + jnp.abs(c[2]) + jnp.abs(c[3]))
    return jnp.stack([small * both - graze * c[2] - 0.1 * c[2], large * both - graze * c[3] - 0.1 * c[3]])


def row_edges(strip):
    slot = iota(1) % 4
    return jnp.where(slot == 2, lanes(strip, 64), strip)


def around(columns, edges, col):
    lane = iota(1)
    c = columns(col)
    edge = lanes(edges, -(4 * (col - 1) + 2))
    north = lanes(jnp.where(lane == 0, edge, c), -1)
    south = lanes(jnp.where(lane == LANES - 1, edge, c), 1)
    return c, columns(col + 1), columns(col - 1), north, south


def around_strip(strip):
    return strip, lanes(strip, -4), lanes(strip, 4), lanes(strip, -1), lanes(strip, 1)


def wet_faces(wet):
    c, e, w, n, s = wet
    return c, c * e, c * w, c * n, c * s


def kernel(
    gy_size, gx_size, state, irr, land, bottom, out,
    raw, irr_v, land_v, bottom_v, mine, other, packs, strips_in, strip, edges, strip_o, edges_o,
    wet, press, next_d, next_t, nstrip, nedges,
    load_sem, send_sem, recv_sem,
):
    comp, gy, gx = (lax.axis_index(a) for a in ("comp", "gy", "gx"))
    east, west = lax.rem(gx + 1, gx_size), lax.rem(gx + gx_size - 1, gx_size)
    up, down = lax.rem(gy + 1, gy_size), lax.rem(gy + gy_size - 1, gy_size)
    twin = 1 - comp
    places = [(up, east), (up, west), (down, east), (down, west), (up, gx), (down, gx), (gy, east), (gy, west)]

    barrier = pltpu.get_barrier_semaphore()
    for y, x in places:
        for c in (comp, twin):
            pl.semaphore_signal(barrier, inc=1, device_id=(c, y, x), device_id_type=MESH)
    pl.semaphore_signal(barrier, inc=1, device_id=(twin, gy, gx), device_id_type=MESH)

    loads = [
        pltpu.make_async_copy(src, dst, load_sem.at[i])
        for i, (src, dst) in enumerate([(irr, irr_v), (land, land_v), (bottom, bottom_v), (state, raw)])
    ]
    for load in loads:
        load.start()
    for load in loads:
        load.wait()

    lane, k = iota(1), iota(0)
    slot, quad = lane % 4, lane // 4

    for x in range(4):
        is_wet = (land_v[x : x + 1, :] == 1) & (k < bottom_v[x : x + 1, :])
        mine[8, OWN + x] = jnp.where(is_wet, jnp.broadcast_to(irr_v[x : x + 1, :], (LEV, LANES)), 0.0)
        for f in range(8):
            mine[f, OWN + x] = raw[pl.ds(f * 32 + x, 8, stride=4), :]
    rows = jnp.zeros((LEV, LANES), jnp.float32)
    lit_rows = jnp.zeros((LEV, LANES), jnp.float32)
    for x in range(4):
        for f in range(8):
            rows = jnp.where(quad == 4 * f + x, lanes(mine[f, OWN + x], 16 * f + 4 * x + 2), rows)
        lit_rows = jnp.where(quad == x, lanes(mine[8, OWN + x], 4 * x + 2), lit_rows)
    packs[0] = jnp.where(slot < 2, rows, lanes(lit_rows, 2))
    packs[1] = jnp.where(slot < 2, lanes(lit_rows, -2), rows)

    pl.semaphore_wait(barrier, 2 * len(places) + 1)

    def remote(index, src, dst, target):
        return pltpu.make_async_remote_copy(
            src_ref=src, dst_ref=dst, send_sem=send_sem.at[index], recv_sem=recv_sem.at[index],
            device_id=target, device_id_type=MESH,
        )

    ways = [(SW, 0, up, east), (SE, 0, up, west), (NW, 1, down, east), (NE, 1, down, west), (SOUTH, 0, up, gx), (NORTH, 1, down, gx)]
    same_rows = [remote(s, packs.at[p], strips_in.at[0, s], (comp, y, x)) for s, p, y, x in ways]
    twin_rows = [remote(6 + s, packs.at[p], strips_in.at[1, s], (twin, y, x)) for s, p, y, x in ways]
    same_cols = [
        remote(12, mine.at[:, 4:6], mine.at[:, 0:2], (comp, gy, east)),
        remote(13, mine.at[:, 2:4], mine.at[:, 6:8], (comp, gy, west)),
    ]
    flow_cols = [
        remote(14, mine.at[0:8, 4:6], other.at[0:8, 0:2], (twin, gy, east)),
        remote(15, mine.at[0:8, 2:4], other.at[0:8, 6:8], (twin, gy, west)),
    ]
    plant_cols = [
        remote(14, mine.at[2:4, 5:6], other.at[2:4, 1:2], (twin, gy, east)),
        remote(15, mine.at[2:4, 2:3], other.at[2:4, 6:7], (twin, gy, west)),
    ]
    flow_own = remote(16, mine.at[0:8, 2:6], other.at[0:8, 2:6], (twin, gy, gx))
    plant_own = remote(16, mine.at[0:5, 2:6], other.at[0:5, 2:6], (twin, gy, gx))

    dyn_sends = same_rows[:4] + twin_rows[:4] + same_rows[4:] + twin_rows[4:] + same_cols + flow_cols + [flow_own]
    trc_sends = same_rows + twin_rows[4:] + same_cols + plant_cols + [plant_own]

    @pl.when(comp == 0)
    def _():
        for copy in dyn_sends:
            copy.start()

    @pl.when(comp == 1)
    def _():
        for copy in trc_sends:
            copy.start()

    no_south, no_north = gy == 0, gy == gy_size - 1
    col3 = quad % 4 == 3
    low = lane < 64
    middle = (lane >= 32) & (lane < 96)
    inner = (lane % 64 >= 4) & (lane % 64 < 20)

    def build(own_rows, arrived, fields, store):
        south = jnp.where(slot < 2, arrived[SOUTH], own_rows)
        north = lanes(jnp.where(slot < 2, own_rows, arrived[NORTH]), 64)
        se, nw, ne = lanes(arrived[SE], 32), lanes(arrived[NW], 64), lanes(arrived[NE], 96)
        halves = (jnp.where(low, south, north), jnp.where(low, north, south))
        corners = (
            jnp.where(col3, jnp.where(low, arrived[SW], nw), jnp.where(middle, se, ne)),
            jnp.where(col3, jnp.where(low, nw, arrived[SW]), jnp.where(middle, ne, se)),
        )
        for f in fields:
            store(f, jnp.where(inner, lanes(halves[f // 4], 4 - 16 * f), lanes(corners[f // 4], -12 - 16 * f)))

    def strips(lit_sides, own_strip, own_edges, my_fields, other_rows, other_fields):
        def keep(ref, edge_ref):
            def store(f, value):
                ref[f] = value
                edge_ref[f] = row_edges(value)

            return store

        build(own_strip, [strips_in[0, s] for s in range(6)], my_fields, keep(strip, edges))
        lit_in = []
        for s in range(6):
            southern = s in (SOUTH, SW, SE)
            dry = no_south if southern else no_north
            lit_in.append(jnp.where(dry, 0.0, lanes(strips_in[0, s], -2 if southern else 2)))
        build(lit_sides, lit_in, [0], lambda f, value: keep(strip, edges)(8, value))
        build(other_rows, [strips_in[1, s] for s in range(6)], other_fields, keep(strip_o, edges_o))

    def other_own_rows(fields):
        result = jnp.zeros((LEV, LANES), jnp.float32)
        for f in fields:
            for x in range(4):
                result = jnp.where(quad == 4 * f + x, lanes(other[f, OWN + x], 16 * f + 4 * x + 2), result)
        return result

    def wet_everywhere():
        for col in range(8):
            wet[0, col] = (mine[8, col] > 0).astype(jnp.float32)
        wet_strip = (strip[8] > 0).astype(jnp.float32)
        wet_edges = row_edges(wet_strip)
        at = {col: wet_faces(around(lambda c: wet[0, c], wet_edges, col)) for col in range(1, 7)}
        return at, wet_faces(around_strip(wet_strip)), wet_strip

    first_row = gy * LANES
    coriolis_main = 0.3 + 0.4 * (first_row + lane).astype(jnp.float32) / float(gy_size * LANES)
    strip_row = first_row + slot + jnp.where(low, -2, LANES - 2)
    coriolis_strip = 0.3 + 0.4 * strip_row.astype(jnp.float32) / float(gy_size * LANES)

    def store_out(f, x, value):
        out[pl.ds(f * 32 + x, 8, stride=4), :] = value

    @pl.when(comp == 0)
    def _():
        for copy in [flow_own] + plant_cols + same_cols + twin_rows[4:] + same_rows:
            if copy is flow_own:
                plant_own.wait_recv()
            else:
                copy.wait_recv()
        strips(lit_rows, rows, None, range(8), other_own_rows((2, 3)), (2, 3))
        wet_at, wet_h, wet_strip = wet_everywhere()
        for col in range(8):
            press[0, col] = pressure_of(mine[2, col], mine[3, col], wet[0, col])
        press_h = pressure_of(strip[2], strip[3], wet_strip)
        press_e = row_edges(press_h)

        def full_step(now, before, p, wets, coriolis, heating):
            u, v = step_speeds(now, before, p, wets, coriolis)
            t, s = step_heat_salt(now, before, wets, heating)
            after = jnp.stack([u, v, t, s])
            return after, filtered(now[0], before[0], after, wets[0])

        h_now, h_before = around_strip(strip[0:4]), around_strip(strip[4:8])
        h_heat = heating_of(strip_o[2], strip_o[3], strip[8], wet_strip)
        after, filt = full_step(h_now, h_before, around_strip(press_h), wet_h, coriolis_strip, h_heat)
        nstrip[0:4], nstrip[4:8] = after, filt
        nedges[0:4], nedges[4:8] = row_edges(after), row_edges(filt)
        for col in range(1, 7):
            now = around(lambda c: mine[0:4, c], edges[0:4], col)
            before = around(lambda c: mine[4:8, c], edges[4:8], col)
            p = around(lambda c: press[0, c], press_e, col)
            heat = heating_of(other[2, col], other[3, col], mine[8, col], wet[0, col])
            after, filt = full_step(now, before, p, wet_at[col], coriolis_main, heat)
            next_d[0:4, col], next_d[4:8, col] = after, filt
        for col in range(2, 6):
            c = other[0:5, col]
            u = around(lambda c: mine[0, c], edges[0], col)
            v = around(lambda c: mine[1, c], edges[1], col)
            plants = around(lambda c: other[2:4, c], edges_o[2:4], col)
            kappa = mixing_of(mine[2, col], mine[3, col], wet[0, col])
            light = light_of(c[2], c[3], mine[8, col])
            change = transported(plants, u[:3], (v[0], v[3], v[4]), wet_at[col]) + mixed(plants[0], kappa)
            change = change + plant_reactions(c, mine[2, col], light)
            next_t[2:4, col] = plants[0] + 0.1 * change * wet[0, col]
        for col in range(1, 7):
            press[1, col] = pressure_of(next_d[2, col], next_d[3, col], wet[0, col])
        press_e = row_edges(pressure_of(nstrip[2], nstrip[3], wet_strip))
        for col in range(2, 6):
            now = around(lambda c: next_d[0:4, c], nedges[0:4], col)
            before = around(lambda c: next_d[4:8, c], nedges[4:8], col)
            p = around(lambda c: press[1, c], press_e, col)
            heat = heating_of(next_t[2, col], next_t[3, col], mine[8, col], wet[0, col])
            after, filt = full_step(now, before, p, wet_at[col], coriolis_main, heat)
            for f in range(4):
                store_out(f, col - 2, after[f])
                store_out(4 + f, col - 2, filt[f])

    @pl.when(comp == 1)
    def _():
        for copy in [flow_own] + flow_cols + same_cols + twin_rows[4:] + same_rows[4:] + twin_rows[:4] + same_rows[:4]:
            copy.wait_recv()
        strips(lit_rows, rows, None, range(8), other_own_rows(range(8)), range(8))
        wet_at, wet_h, wet_strip = wet_everywhere()
        for col in range(8):
            press[0, col] = pressure_of(other[2, col], other[3, col], wet[0, col])
        press_h = pressure_of(strip_o[2], strip_o[3], wet_strip)
        press_e = row_edges(press_h)

        def tracer_step(c, u, v, wets, temp, salt, lit):
            kappa = mixing_of(temp, salt, wets[0])
            light = light_of(c[0][2], c[0][3], lit)
            change = transported(c, u, v, wets) + mixed(c[0], kappa) + reactions(c[0], temp, light)
            return c[0] + 0.1 * change * wets[0]

        now, before = around_strip(strip_o[0:4]), around_strip(strip_o[4:6])
        u, v = step_speeds(now, before, around_strip(press_h), wet_h, coriolis_strip)
        nedges[8], nedges[9] = row_edges(u), row_edges(v)
        u = (now[0][0], now[1][0], now[2][0])
        v = (now[0][1], now[3][1], now[4][1])
        new = tracer_step(around_strip(strip[0:8]), u, v, wet_h, strip_o[2], strip_o[3], strip[8])
        nedges[0:8] = row_edges(new)
        for col in range(1, 7):
            now = around(lambda c: other[0:4, c], edges_o[0:4], col)
            before = around(lambda c: other[4:8, c], edges_o[4:8], col)
            p = around(lambda c: press[0, c], press_e, col)
            next_d[0, col], next_d[1, col] = step_speeds(now, before, p, wet_at[col], coriolis_main)
            c = around(lambda c: mine[0:8, c], edges[0:8], col)
            if 2 <= col < 6:
                heat = heating_of(c[0][2], c[0][3], mine[8, col], wet[0, col])
                next_d[2, col], next_d[3, col] = step_heat_salt(now, before, wet_at[col], heat)
            u = (now[0][0], now[1][0], now[2][0])
            v = (now[0][1], now[3][1], now[4][1])
            next_t[0:8, col] = tracer_step(c, u, v, wet_at[col], other[2, col], other[3, col], mine[8, col])
        for col in range(2, 6):
            c = around(lambda c: next_t[0:8, c], nedges[0:8], col)
            u = around(lambda c: next_d[0, c], nedges[8], col)
            v = around(lambda c: next_d[1, c], nedges[9], col)
            new = tracer_step(
                c, u[:3], (v[0], v[3], v[4]), wet_at[col], next_d[2, col], next_d[3, col], mine[8, col]
            )
            for f in range(8):
                store_out(f, col - 2, new[f])

    @pl.when(comp == 0)
    def _():
        for copy in dyn_sends:
            copy.wait_send()

    @pl.when(comp == 1)
    def _():
        for copy in trc_sends:
            copy.wait_send()


def solution(mesh):
    gy_size, gx_size = mesh.shape["gy"], mesh.shape["gx"]

    def local(ocean_state, irradiance, land_mask, bottom_level):
        rows = ocean_state.size // LANES
        anywhere = pl.BlockSpec(memory_space=pl.ANY)
        f32 = jnp.float32
        result = pl.pallas_call(
            functools.partial(kernel, gy_size, gx_size),
            out_shape=jax.ShapeDtypeStruct((rows, LANES), f32),
            in_specs=[anywhere] * 4,
            out_specs=pl.BlockSpec(memory_space=pltpu.VMEM),
            scratch_shapes=[
                pltpu.VMEM((rows, LANES), f32),
                pltpu.VMEM((4, LANES), f32),
                pltpu.VMEM((4, LANES), jnp.int32),
                pltpu.VMEM((4, LANES), jnp.int32),
                pltpu.VMEM((9, 8, LEV, LANES), f32),
                pltpu.VMEM((8, 8, LEV, LANES), f32),
                pltpu.VMEM((2, LEV, LANES), f32),
                pltpu.VMEM((2, 6, LEV, LANES), f32),
                pltpu.VMEM((9, LEV, LANES), f32),
                pltpu.VMEM((9, LEV, LANES), f32),
                pltpu.VMEM((8, LEV, LANES), f32),
                pltpu.VMEM((8, LEV, LANES), f32),
                pltpu.VMEM((1, 8, LEV, LANES), f32),
                pltpu.VMEM((2, 8, LEV, LANES), f32),
                pltpu.VMEM((8, 8, LEV, LANES), f32),
                pltpu.VMEM((8, 8, LEV, LANES), f32),
                pltpu.VMEM((8, LEV, LANES), f32),
                pltpu.VMEM((10, LEV, LANES), f32),
                pltpu.SemaphoreType.DMA((4,)),
                pltpu.SemaphoreType.DMA((17,)),
                pltpu.SemaphoreType.DMA((17,)),
            ],
            compiler_params=pltpu.CompilerParams(
                collective_id=0, has_side_effects=True, vmem_limit_bytes=8 * 1024 * 1024
            ),
            name="coupled_steps",
        )(ocean_state.reshape(rows, LANES), irradiance, land_mask, bottom_level)
        return result.reshape(ocean_state.shape)

    return jax.shard_map(
        local,
        mesh=mesh,
        in_specs=(P("comp", None, "gx", "gy"), P("gx", "gy"), P("gx", "gy"), P("gx", "gy")),
        out_specs=P("comp", None, "gx", "gy"),
        check_vma=False,
    )
```

```python
import functools

import jax
import jax.numpy as jnp
from jax import lax
from jax.experimental import pallas as pl
from jax.experimental.pallas import tpu as pltpu
from jax.sharding import PartitionSpec as P

MESH = pl.DeviceIdType.MESH

SOUTH, NORTH, SW, SE, NW, NE = range(6)
OWN = 2
LEV, LANES = 8, 128


def roll(value, shift, axis):
    return pltpu.roll(value, shift % value.shape[axis], axis)


def lanes(value, shift):
    return roll(value, shift, value.ndim - 1)


def levels(value, shift):
    return roll(value, shift, value.ndim - 2)


def iota(dim):
    return lax.broadcasted_iota(jnp.int32, (LEV, LANES), dim)


def level_sum(value):
    k = iota(0)
    for shift in (1, 2, 4):
        value = value + jnp.where(k >= shift, levels(value, shift), 0.0)
    return value


def density(temp, salt, wet):
    return (0.8 * salt - 0.2 * temp) * wet


def pressure_of(temp, salt, wet):
    return 0.1 * level_sum(density(temp, salt, wet))


def mixing_of(temp, salt, wet):
    rho = density(temp, salt, wet)
    strat = jnp.maximum(levels(rho, -1) - rho, 0.0)
    wet_below = jnp.where(iota(0) == LEV - 1, 0.0, levels(wet, -1))
    return (0.05 + 1.0 / (1.0 + 4.0 * strat)) * wet * wet_below


def absorbed(small, large):
    absorb = 0.08 + 0.05 * (jnp.abs(small) + jnp.abs(large))
    return absorb, level_sum(absorb)


def surface_of(lit):
    return jnp.broadcast_to(lit[0:1, :], (LEV, LANES))


def heating_of(small, large, lit, wet):
    absorb, column = absorbed(small, large)
    return surface_of(lit) * (jnp.exp(absorb - column) - jnp.exp(-column)) * wet


def light_of(small, large, lit):
    absorb, column = absorbed(small, large)
    return surface_of(lit) * jnp.exp(0.5 * absorb - column)


def gradients(p, wet):
    pc, pe, pw, pn, ps = p
    _, we, ww, wn, ws = wet
    return 0.5 * (we * (pe - pc) + ww * (pc - pw)), 0.5 * (wn * (pn - pc) + ws * (pc - ps))


def spread_of(field, wet):
    c, e, w, n, s = field
    _, we, ww, wn, ws = wet
    return we * (e - c) + ww * (w - c) + wn * (n - c) + ws * (s - c)


def faces(u, v, wet):
    (uc, ue, uw), (vc, vn, vs) = u, v
    _, we, ww, wn, ws = wet
    return 0.25 * (uc + ue) * we, 0.25 * (uc + uw) * ww, 0.25 * (vc + vn) * wn, 0.25 * (vc + vs) * ws


def carried_of(field, face):
    c, e, w, n, s = field
    fe, fw, fn, fs = face
    return fe * (c + e) - fw * (c + w) + fn * (c + n) - fs * (c + s)


def pick(five, index):
    return tuple(part[index] for part in five)


def step_speeds(now, before, p, wet, coriolis):
    force_east, force_north = gradients(p, wet)
    u, v = now[0][0], now[0][1]
    du = coriolis * v - force_east + 0.2 * spread_of(pick(before, 0), wet)
    dv = -coriolis * u - force_north + 0.2 * spread_of(pick(before, 1), wet)
    return before[0][0] + 0.2 * du * wet[0], before[0][1] + 0.2 * dv * wet[0]


def step_heat_salt(now, before, wet, heating):
    u = (now[0][0], now[1][0], now[2][0])
    v = (now[0][1], now[3][1], now[4][1])
    face = faces(u, v, wet)
    dt = -carried_of(pick(now, 2), face) + 0.2 * spread_of(pick(before, 2), wet) + 3.0 * heating
    ds = -carried_of(pick(now, 3), face) + 0.2 * spread_of(pick(before, 3), wet)
    return before[0][2] + 0.2 * dt * wet[0], before[0][3] + 0.2 * ds * wet[0]


def filtered(now, before, after, wet):
    return now + 0.1 * (before - 2.0 * now + after) * wet


def transported(field, u, v, wet):
    c, e, w, n, s = field
    _, we, ww, wn, ws = wet
    fe, fw, fn, fs = faces(u, v, wet)
    le, lw, ln, ls = 0.2 * we, 0.2 * ww, 0.2 * wn, 0.2 * ws
    own = (le + fe) + (lw - fw) + (ln + fn) + (ls - fs)
    return (le - fe) * e + (lw + fw) * w + (ln - fn) * n + (ls + fs) * s - own * c


def mixed(c, kappa):
    down = kappa * (levels(c, -1) - c)
    return down - levels(down, 1)


def growth_of(nitrate, ammonium, small, large, temp, light):
    rate = jnp.exp(0.06 * temp) * (light / (light + 0.5))
    both = jnp.abs(nitrate) + jnp.abs(ammonium)
    return 0.6 * rate * small / (0.2 + both), 0.9 * rate * large / (0.8 + both)


def reactions(c, temp, light):
    nn, na = jnp.abs(c[0]), jnp.abs(c[1])
    small, large = growth_of(c[0], c[1], c[2], c[3], temp, light)
    sn, sa, ln, la = small * nn, small * na, large * nn, large * na
    graze = 0.8 * c[4] / (1.0 + jnp.abs(c[2]) + jnp.abs(c[3]))
    gs, gl = graze * c[2], graze * c[3]
    remin = 0.3 * c[5] + 0.1 * c[6]
    nitrify = 0.2 * c[1]
    return jnp.stack(
        [
            nitrify - sn - ln,
            remin + 0.1 * c[4] - nitrify - sa - la,
            sn + sa - gs - 0.1 * c[2],
            ln + la - gl - 0.1 * c[3],
            0.7 * (gs + gl) - 0.1 * c[4] - 0.15 * c[4],
            0.1 * c[2] + 0.3 * gs - 0.3 * c[5],
            0.1 * c[3] + 0.15 * c[4] + 0.3 * gl - 0.1 * c[6],
            1.3 * (sn + sa + ln + la) - (remin + 2.0 * nitrify),
        ]
    )


def plant_reactions(c, temp, light):
    both = jnp.abs(c[0]) + jnp.abs(c[1])
    small, large = growth_of(c[0], c[1], c[2], c[3], temp, light)
    graze = 0.8 * c[4] / (1.0 + jnp.abs(c[2]) + jnp.abs(c[3]))
    return jnp.stack([small * both - graze * c[2] - 0.1 * c[2], large * both - graze * c[3] - 0.1 * c[3]])


def row_edges(strip):
    slot = iota(1) % 4
    return jnp.where(slot == 2, lanes(strip, 64), strip)


def around(columns, edges, col):
    lane = iota(1)
    c = columns(col)
    edge = lanes(edges, -(4 * (col - 1) + 2))
    north = lanes(jnp.where(lane == 0, edge, c), -1)
    south = lanes(jnp.where(lane == LANES - 1, edge, c), 1)
    return c, columns(col + 1), columns(col - 1), north, south


def around_strip(strip):
    return strip, lanes(strip, -4), lanes(strip, 4), lanes(strip, -1), lanes(strip, 1)


def wet_faces(wet):
    c, e, w, n, s = wet
    return c, c * e, c * w, c * n, c * s


def kernel(
    gy_size, gx_size, state, irr, land, bottom, out,
    raw, irr_v, land_v, bottom_v, mine, other, packs, strips_in, strip, edges, strip_o, edges_o,
    wet, press, next_d, next_t, nedges,
    load_sem, send_sem, recv_sem, hello_west, hello_north,
):
    comp, gy, gx = (lax.axis_index(a) for a in ("comp", "gy", "gx"))
    east, west = lax.rem(gx + 1, gx_size), lax.rem(gx + gx_size - 1, gx_size)
    up, down = lax.rem(gy + 1, gy_size), lax.rem(gy + gy_size - 1, gy_size)
    twin = 1 - comp
    eastern = [(c, y, east) for y in (up, gy, down) for c in (comp, twin)]
    western = [(c, y, west) for y in (up, gy, down) for c in (comp, twin)]

    barrier = pltpu.get_barrier_semaphore()
    for target in western + [(comp, up, gx), (twin, up, gx), (twin, gy, gx)]:
        pl.semaphore_signal(barrier, inc=1, device_id=target, device_id_type=MESH)

    loads = [
        pltpu.make_async_copy(src, dst, load_sem.at[i])
        for i, (src, dst) in enumerate([(irr, irr_v), (land, land_v), (bottom, bottom_v), (state, raw)])
    ]
    for load in loads:
        load.start()
    for load in loads:
        load.wait()

    lane, k = iota(1), iota(0)
    slot, quad = lane % 4, lane // 4

    for x in range(4):
        is_wet = (land_v[x : x + 1, :] == 1) & (k < bottom_v[x : x + 1, :])
        mine[8, OWN + x] = jnp.where(is_wet, jnp.broadcast_to(irr_v[x : x + 1, :], (LEV, LANES)), 0.0)
        for f in range(8):
            mine[f, OWN + x] = raw[pl.ds(f * 32 + x, 8, stride=4), :]
    rows = jnp.zeros((LEV, LANES), jnp.float32)
    lit_rows = jnp.zeros((LEV, LANES), jnp.float32)
    for x in range(4):
        for f in range(8):
            rows = jnp.where(quad == 4 * f + x, lanes(mine[f, OWN + x], 16 * f + 4 * x + 2), rows)
        lit_rows = jnp.where(quad == x, lanes(mine[8, OWN + x], 4 * x + 2), lit_rows)
    packs[0] = jnp.where(slot < 2, rows, lanes(lit_rows, 2))
    packs[1] = jnp.where(slot < 2, lanes(lit_rows, -2), rows)

    pl.semaphore_wait(barrier, 9)
    for target in eastern:
        pl.semaphore_signal(hello_west, inc=1, device_id=target, device_id_type=MESH)
    for target in [(comp, down, gx), (twin, down, gx)]:
        pl.semaphore_signal(hello_north, inc=1, device_id=target, device_id_type=MESH)

    def remote(index, src, dst, target):
        return pltpu.make_async_remote_copy(
            src_ref=src, dst_ref=dst, send_sem=send_sem.at[index], recv_sem=recv_sem.at[index],
            device_id=target, device_id_type=MESH,
        )

    ways = [(SW, 0, up, east), (SE, 0, up, west), (NW, 1, down, east), (NE, 1, down, west), (SOUTH, 0, up, gx), (NORTH, 1, down, gx)]
    same_rows = [remote(s, packs.at[p], strips_in.at[0, s], (comp, y, x)) for s, p, y, x in ways]
    twin_rows = [remote(6 + s, packs.at[p], strips_in.at[1, s], (twin, y, x)) for s, p, y, x in ways]
    same_cols = [
        remote(12, mine.at[:, 4:6], mine.at[:, 0:2], (comp, gy, east)),
        remote(13, mine.at[:, 2:4], mine.at[:, 6:8], (comp, gy, west)),
    ]
    flow_cols = [
        remote(14, mine.at[0:8, 4:6], other.at[0:8, 0:2], (twin, gy, east)),
        remote(15, mine.at[0:8, 2:4], other.at[0:8, 6:8], (twin, gy, west)),
    ]
    plant_cols = [
        remote(14, mine.at[2:4, 5:6], other.at[2:4, 1:2], (twin, gy, east)),
        remote(15, mine.at[2:4, 2:3], other.at[2:4, 6:7], (twin, gy, west)),
    ]
    flow_own = remote(16, mine.at[0:8, 2:6], other.at[0:8, 2:6], (twin, gy, gx))
    plant_own = remote(16, mine.at[0:5, 2:6], other.at[0:5, 2:6], (twin, gy, gx))

    dyn_west = [same_rows[0], same_rows[2], twin_rows[0], twin_rows[2], same_cols[0], flow_cols[0]]
    dyn_east = [same_rows[1], same_rows[3], twin_rows[1], twin_rows[3], same_cols[1], flow_cols[1]]
    trc_west = [same_rows[0], same_rows[2], same_cols[0], plant_cols[0]]
    trc_east = [same_rows[1], same_rows[3], same_cols[1], plant_cols[1]]
    to_north = [same_rows[4], twin_rows[4]]
    to_south = [same_rows[5], twin_rows[5]]

    def start(copies):
        for copy in copies:
            copy.start()

    def arrived(copies):
        for copy in copies:
            copy.wait_recv()

    no_south, no_north = gy == 0, gy == gy_size - 1
    low = lane < 64
    middle = (lane >= 32) & (lane < 96)
    inner = (lane % 64 >= 4) & (lane % 64 < 20)

    def strip_rows(own_rows, south, north, fields, store):
        south = jnp.where(slot < 2, south, own_rows)
        north = lanes(jnp.where(slot < 2, own_rows, north), 64)
        halves = (jnp.where(low, south, north), jnp.where(low, north, south))
        for f in fields:
            store(f, jnp.where(inner, lanes(halves[f // 4], 4 - 16 * f), 0.0))

    def strip_corners(south, north, is_east, fields, load, store):
        south, north = (lanes(south, 32), lanes(north, 96)) if is_east else (south, lanes(north, 64))
        first = middle if is_east else low
        halves = (jnp.where(first, south, north), jnp.where(first, north, south))
        there = lane % 64 // 4 == (5 if is_east else 0)
        for f in fields:
            store(f, jnp.where(there, lanes(halves[f // 4], -12 - 16 * f), load(f)))

    def lit_side(s):
        southern = s in (SOUTH, SW, SE)
        return jnp.where(no_south if southern else no_north, 0.0, lanes(strips_in[0, s], -2 if southern else 2))

    def keeper(ref, edge_ref, shift=0):
        def store(f, value):
            ref[f + shift] = value
            edge_ref[f + shift] = row_edges(value)

        return store

    def start_strips(other_fields):
        strip_rows(rows, strips_in[0, SOUTH], strips_in[0, NORTH], range(8), keeper(strip, edges))
        strip_rows(lit_rows, lit_side(SOUTH), lit_side(NORTH), [0], keeper(strip, edges, 8))
        strip_rows(
            other_own_rows(other_fields), strips_in[1, SOUTH], strips_in[1, NORTH], other_fields, keeper(strip_o, edges_o)
        )

    def add_corners(south, north, is_east, other_fields):
        args = (strips_in[0, south], strips_in[0, north], is_east)
        strip_corners(*args, range(8), lambda f: strip[f], keeper(strip, edges))
        strip_corners(lit_side(south), lit_side(north), is_east, [0], lambda f: strip[8], keeper(strip, edges, 8))
        if other_fields:
            args = (strips_in[1, south], strips_in[1, north], is_east)
            strip_corners(*args, other_fields, lambda f: strip_o[f], keeper(strip_o, edges_o))

    def other_own_rows(fields):
        result = jnp.zeros((LEV, LANES), jnp.float32)
        for f in fields:
            for x in range(4):
                result = jnp.where(quad == 4 * f + x, lanes(other[f, OWN + x], 16 * f + 4 * x + 2), result)
        return result

    def wet_columns(cols):
        for col in cols:
            wet[0, col] = (mine[8, col] > 0).astype(jnp.float32)

    def wet_strip():
        return (strip[8] > 0).astype(jnp.float32)

    def wet_at(col):
        return wet_faces(around(lambda c: wet[0, c], row_edges(wet_strip()), col))

    first_row = gy * LANES
    coriolis_main = 0.3 + 0.4 * (first_row + lane).astype(jnp.float32) / float(gy_size * LANES)
    strip_row = first_row + slot + jnp.where(low, -2, LANES - 2)
    coriolis_strip = 0.3 + 0.4 * strip_row.astype(jnp.float32) / float(gy_size * LANES)

    def store_out(f, x, value):
        out[pl.ds(f * 32 + x, 8, stride=4), :] = value

    def full_step(now, before, p, wets, coriolis, heating):
        u, v = step_speeds(now, before, p, wets, coriolis)
        t, s = step_heat_salt(now, before, wets, heating)
        after = jnp.stack([u, v, t, s])
        return after, filtered(now[0], before[0], after, wets[0])

    def tracer_step(c, u, v, wets, temp, salt, lit):
        kappa = mixing_of(temp, salt, wets[0])
        light = light_of(c[0][2], c[0][3], lit)
        change = transported(c, u, v, wets) + mixed(c[0], kappa) + reactions(c[0], temp, light)
        return c[0] + 0.1 * change * wets[0]

    def dyn_pressure(cols):
        for col in cols:
            press[0, col] = pressure_of(mine[2, col], mine[3, col], wet[0, col])

    def dyn_strip():
        dry = wet_strip()
        p = around_strip(pressure_of(strip[2], strip[3], dry))
        heat = heating_of(strip_o[2], strip_o[3], strip[8], dry)
        now, before = around_strip(strip[0:4]), around_strip(strip[4:8])
        after, filt = full_step(now, before, p, wet_faces(around_strip(dry)), coriolis_strip, heat)
        nedges[0:4], nedges[4:8] = row_edges(after), row_edges(filt)
        nedges[8] = row_edges(pressure_of(after[2], after[3], dry))

    def dyn_first(cols):
        press_e = row_edges(pressure_of(strip[2], strip[3], wet_strip()))
        for col in cols:
            wets = wet_at(col)
            now = around(lambda c: mine[0:4, c], edges[0:4], col)
            before = around(lambda c: mine[4:8, c], edges[4:8], col)
            p = around(lambda c: press[0, c], press_e, col)
            heat = heating_of(other[2, col], other[3, col], mine[8, col], wets[0])
            after, filt = full_step(now, before, p, wets, coriolis_main, heat)
            next_d[0:4, col], next_d[4:8, col] = after, filt
            press[1, col] = pressure_of(after[2], after[3], wets[0])
            if 2 <= col < 6:
                c = other[0:5, col]
                plants = around(lambda c: other[2:4, c], edges_o[2:4], col)
                u = (now[0][0], now[1][0], now[2][0])
                v = (now[0][1], now[3][1], now[4][1])
                kappa = mixing_of(now[0][2], now[0][3], wets[0])
                light = light_of(c[2], c[3], mine[8, col])
                change = transported(plants, u, v, wets) + mixed(plants[0], kappa)
                change = change + plant_reactions(c, now[0][2], light)
                next_t[2:4, col] = plants[0] + 0.1 * change * wets[0]

    def dyn_second(cols):
        for col in cols:
            wets = wet_at(col)
            now = around(lambda c: next_d[0:4, c], nedges[0:4], col)
            before = around(lambda c: next_d[4:8, c], nedges[4:8], col)
            p = around(lambda c: press[1, c], nedges[8], col)
            heat = heating_of(next_t[2, col], next_t[3, col], mine[8, col], wets[0])
            after, filt = full_step(now, before, p, wets, coriolis_main, heat)
            for f in range(4):
                store_out(f, col - 2, after[f])
                store_out(4 + f, col - 2, filt[f])

    def trc_pressure(cols):
        for col in cols:
            press[0, col] = pressure_of(other[2, col], other[3, col], wet[0, col])

    def trc_strip():
        dry = wet_strip()
        wets = wet_faces(around_strip(dry))
        p = around_strip(pressure_of(strip_o[2], strip_o[3], dry))
        now, before = around_strip(strip_o[0:4]), around_strip(strip_o[4:6])
        u, v = step_speeds(now, before, p, wets, coriolis_strip)
        nedges[8], nedges[9] = row_edges(u), row_edges(v)
        u = (now[0][0], now[1][0], now[2][0])
        v = (now[0][1], now[3][1], now[4][1])
        nedges[0:8] = row_edges(tracer_step(around_strip(strip[0:8]), u, v, wets, strip_o[2], strip_o[3], strip[8]))

    def trc_first(cols):
        press_e = row_edges(pressure_of(strip_o[2], strip_o[3], wet_strip()))
        for col in cols:
            wets = wet_at(col)
            now = around(lambda c: other[0:4, c], edges_o[0:4], col)
            before = around(lambda c: other[4:8, c], edges_o[4:8], col)
            p = around(lambda c: press[0, c], press_e, col)
            next_d[0, col], next_d[1, col] = step_speeds(now, before, p, wets, coriolis_main)
            c = around(lambda c: mine[0:8, c], edges[0:8], col)
            if 2 <= col < 6:
                heat = heating_of(c[0][2], c[0][3], mine[8, col], wets[0])
                next_d[2, col], next_d[3, col] = step_heat_salt(now, before, wets, heat)
            u = (now[0][0], now[1][0], now[2][0])
            v = (now[0][1], now[3][1], now[4][1])
            next_t[0:8, col] = tracer_step(c, u, v, wets, now[0][2], now[0][3], mine[8, col])

    def trc_second(cols):
        for col in cols:
            c = around(lambda c: next_t[0:8, c], nedges[0:8], col)
            u = around(lambda c: next_d[0, c], nedges[8], col)
            v = around(lambda c: next_d[1, c], nedges[9], col)
            new = tracer_step(
                c, u[:3], (v[0], v[3], v[4]), wet_at(col), next_d[2, col], next_d[3, col], mine[8, col]
            )
            for f in range(8):
                store_out(f, col - 2, new[f])

    def run(own, own_in, west_out, east_out, west_in, east_in, rows_of, pressure, at_strip, first, second, corner_fields):
        start(west_out + to_south + [own])
        pl.semaphore_wait(hello_north, 2)
        start(to_north)
        arrived([own_in] + to_north + to_south)
        start_strips(rows_of)
        wet_columns(range(2, 6))
        pressure(range(2, 6))
        first((3, 4))
        pl.semaphore_wait(hello_west, 6)
        start(east_out)
        arrived(east_in)
        add_corners(SE, NE, True, corner_fields)
        wet_columns((6, 7))
        pressure((6, 7))
        first((5, 6))
        at_strip()
        second((4, 5))
        arrived(west_in)
        add_corners(SW, NW, False, corner_fields)
        wet_columns((0, 1))
        pressure((0, 1))
        first((1, 2))
        at_strip()
        second((2, 3))
        for copy in [own] + west_out + east_out + to_north + to_south:
            copy.wait_send()

    @pl.when(comp == 0)
    def _():
        run(
            flow_own, plant_own, dyn_west, dyn_east,
            [same_rows[0], same_rows[2], same_cols[0], plant_cols[0]],
            [same_rows[1], same_rows[3], same_cols[1], plant_cols[1]],
            (2, 3), dyn_pressure, dyn_strip, dyn_first, dyn_second, (),
        )

    @pl.when(comp == 1)
    def _():
        run(
            plant_own, flow_own, trc_west, trc_east,
            [same_rows[0], same_rows[2], twin_rows[0], twin_rows[2], same_cols[0], flow_cols[0]],
            [same_rows[1], same_rows[3], twin_rows[1], twin_rows[3], same_cols[1], flow_cols[1]],
            range(8), trc_pressure, trc_strip, trc_first, trc_second, range(8),
        )


def solution(mesh):
    gy_size, gx_size = mesh.shape["gy"], mesh.shape["gx"]

    def local(ocean_state, irradiance, land_mask, bottom_level):
        rows = ocean_state.size // LANES
        anywhere = pl.BlockSpec(memory_space=pl.ANY)
        f32 = jnp.float32
        operands = (ocean_state.reshape(rows, LANES), irradiance, land_mask, bottom_level)
        result = pl.pallas_call(
            functools.partial(kernel, gy_size, gx_size),
            out_shape=jax.ShapeDtypeStruct((rows, LANES), f32),
            in_specs=[anywhere] * 4,
            out_specs=pl.BlockSpec(memory_space=pltpu.VMEM),
            scratch_shapes=[
                pltpu.VMEM((rows, LANES), f32),
                pltpu.VMEM((4, LANES), f32),
                pltpu.VMEM((4, LANES), jnp.int32),
                pltpu.VMEM((4, LANES), jnp.int32),
                pltpu.VMEM((9, 8, LEV, LANES), f32),
                pltpu.VMEM((8, 8, LEV, LANES), f32),
                pltpu.VMEM((2, LEV, LANES), f32),
                pltpu.VMEM((2, 6, LEV, LANES), f32),
                pltpu.VMEM((9, LEV, LANES), f32),
                pltpu.VMEM((9, LEV, LANES), f32),
                pltpu.VMEM((8, LEV, LANES), f32),
                pltpu.VMEM((8, LEV, LANES), f32),
                pltpu.VMEM((1, 8, LEV, LANES), f32),
                pltpu.VMEM((2, 8, LEV, LANES), f32),
                pltpu.VMEM((8, 8, LEV, LANES), f32),
                pltpu.VMEM((8, 8, LEV, LANES), f32),
                pltpu.VMEM((10, LEV, LANES), f32),
                pltpu.SemaphoreType.DMA((4,)),
                pltpu.SemaphoreType.DMA((17,)),
                pltpu.SemaphoreType.DMA((17,)),
                pltpu.SemaphoreType.REGULAR,
                pltpu.SemaphoreType.REGULAR,
            ],
            compiler_params=pltpu.CompilerParams(
                collective_id=0, has_side_effects=True, vmem_limit_bytes=8 * 1024 * 1024
            ),
            name="coupled_steps",
        )(*[pltpu.with_memory_space_constraint(a, pltpu.HBM) for a in operands])
        return result.reshape(ocean_state.shape)

    return jax.shard_map(
        local,
        mesh=mesh,
        in_specs=(P("comp", None, "gx", "gy"), P("gx", "gy"), P("gx", "gy"), P("gx", "gy")),
        out_specs=P("comp", None, "gx", "gy"),
        check_vma=False,
    )
```

```python
import functools

import jax
import jax.numpy as jnp
from jax import lax
from jax.experimental import pallas as pl
from jax.experimental.pallas import tpu as pltpu
from jax.sharding import PartitionSpec as P

MESH = pl.DeviceIdType.MESH

SW, SE, NW, NE = range(4)
OWN = 2
LEV, LANES = 8, 128


def roll(value, shift, axis):
    return pltpu.roll(value, shift % value.shape[axis] if isinstance(shift, int) else shift, axis)


def lanes(value, shift):
    return roll(value, shift, value.ndim - 1)


def levels(value, shift):
    return roll(value, shift, value.ndim - 2)


def iota(dim):
    return lax.broadcasted_iota(jnp.int32, (LEV, LANES), dim)


def level_sum(value):
    k = iota(0)
    for shift in (1, 2, 4):
        value = value + jnp.where(k >= shift, levels(value, shift), 0.0)
    return value


def density(temp, salt, wet):
    return (0.8 * salt - 0.2 * temp) * wet


def pressure_of(temp, salt, wet):
    return 0.1 * level_sum(density(temp, salt, wet))


def mixing_of(temp, salt, wet):
    rho = density(temp, salt, wet)
    strat = jnp.maximum(levels(rho, -1) - rho, 0.0)
    wet_below = jnp.where(iota(0) == LEV - 1, 0.0, levels(wet, -1))
    return (0.05 + 1.0 / (1.0 + 4.0 * strat)) * wet * wet_below


def absorbed(small, large):
    absorb = 0.08 + 0.05 * (jnp.abs(small) + jnp.abs(large))
    return absorb, level_sum(absorb)


def surface_of(lit):
    return jnp.broadcast_to(lit[0:1, :], (LEV, LANES))


def heating_of(small, large, lit, wet):
    absorb, column = absorbed(small, large)
    return surface_of(lit) * (jnp.exp(absorb - column) - jnp.exp(-column)) * wet


def light_of(small, large, lit):
    absorb, column = absorbed(small, large)
    return surface_of(lit) * jnp.exp(0.5 * absorb - column)


def gradients(p, wet):
    pc, pe, pw, pn, ps = p
    _, we, ww, wn, ws = wet
    return 0.5 * (we * (pe - pc) + ww * (pc - pw)), 0.5 * (wn * (pn - pc) + ws * (pc - ps))


def spread_of(field, wet):
    c, e, w, n, s = field
    _, we, ww, wn, ws = wet
    return we * (e - c) + ww * (w - c) + wn * (n - c) + ws * (s - c)


def faces(u, v, wet):
    (uc, ue, uw), (vc, vn, vs) = u, v
    _, we, ww, wn, ws = wet
    return 0.25 * (uc + ue) * we, 0.25 * (uc + uw) * ww, 0.25 * (vc + vn) * wn, 0.25 * (vc + vs) * ws


def carried_of(field, face):
    c, e, w, n, s = field
    fe, fw, fn, fs = face
    return fe * (c + e) - fw * (c + w) + fn * (c + n) - fs * (c + s)


def pick(five, index):
    return tuple(part[index] for part in five)


def step_speeds(now, before, p, wet, coriolis):
    force_east, force_north = gradients(p, wet)
    u, v = now[0][0], now[0][1]
    du = coriolis * v - force_east + 0.2 * spread_of(pick(before, 0), wet)
    dv = -coriolis * u - force_north + 0.2 * spread_of(pick(before, 1), wet)
    return before[0][0] + 0.2 * du * wet[0], before[0][1] + 0.2 * dv * wet[0]


def step_heat_salt(now, before, wet, heating):
    u = (now[0][0], now[1][0], now[2][0])
    v = (now[0][1], now[3][1], now[4][1])
    face = faces(u, v, wet)
    dt = -carried_of(pick(now, 2), face) + 0.2 * spread_of(pick(before, 2), wet) + 3.0 * heating
    ds = -carried_of(pick(now, 3), face) + 0.2 * spread_of(pick(before, 3), wet)
    return before[0][2] + 0.2 * dt * wet[0], before[0][3] + 0.2 * ds * wet[0]


def filtered(now, before, after, wet):
    return now + 0.1 * (before - 2.0 * now + after) * wet


def transported(field, u, v, wet):
    c, e, w, n, s = field
    _, we, ww, wn, ws = wet
    fe, fw, fn, fs = faces(u, v, wet)
    le, lw, ln, ls = 0.2 * we, 0.2 * ww, 0.2 * wn, 0.2 * ws
    own = (le + fe) + (lw - fw) + (ln + fn) + (ls - fs)
    return (le - fe) * e + (lw + fw) * w + (ln - fn) * n + (ls + fs) * s - own * c


def mixed(c, kappa):
    down = kappa * (levels(c, -1) - c)
    return down - levels(down, 1)


def growth_of(nitrate, ammonium, small, large, temp, light):
    rate = jnp.exp(0.06 * temp) * (light / (light + 0.5))
    both = jnp.abs(nitrate) + jnp.abs(ammonium)
    return 0.6 * rate * small / (0.2 + both), 0.9 * rate * large / (0.8 + both)


def reactions(c, temp, light):
    nn, na = jnp.abs(c[0]), jnp.abs(c[1])
    small, large = growth_of(c[0], c[1], c[2], c[3], temp, light)
    sn, sa, ln, la = small * nn, small * na, large * nn, large * na
    graze = 0.8 * c[4] / (1.0 + jnp.abs(c[2]) + jnp.abs(c[3]))
    gs, gl = graze * c[2], graze * c[3]
    remin = 0.3 * c[5] + 0.1 * c[6]
    nitrify = 0.2 * c[1]
    return jnp.stack(
        [
            nitrify - sn - ln,
            remin + 0.1 * c[4] - nitrify - sa - la,
            sn + sa - gs - 0.1 * c[2],
            ln + la - gl - 0.1 * c[3],
            0.7 * (gs + gl) - 0.1 * c[4] - 0.15 * c[4],
            0.1 * c[2] + 0.3 * gs - 0.3 * c[5],
            0.1 * c[3] + 0.15 * c[4] + 0.3 * gl - 0.1 * c[6],
            1.3 * (sn + sa + ln + la) - (remin + 2.0 * nitrify),
        ]
    )


def plant_reactions(c, temp, light):
    both = jnp.abs(c[0]) + jnp.abs(c[1])
    small, large = growth_of(c[0], c[1], c[2], c[3], temp, light)
    graze = 0.8 * c[4] / (1.0 + jnp.abs(c[2]) + jnp.abs(c[3]))
    return jnp.stack([small * both - graze * c[2] - 0.1 * c[2], large * both - graze * c[3] - 0.1 * c[3]])


def row_edges(strip):
    slot = iota(1) % 4
    return jnp.where(slot == 2, lanes(strip, 64), strip)


def around(columns, edges, col):
    lane = iota(1)
    c = columns(col)
    edge = lanes(edges, LANES - 2 - 4 * (col - 1))
    north = lanes(jnp.where(lane == 0, edge, c), -1)
    south = lanes(jnp.where(lane == LANES - 1, edge, c), 1)
    return c, columns(col + 1), columns(col - 1), north, south


def around_strip(strip):
    return strip, lanes(strip, -4), lanes(strip, 4), lanes(strip, -1), lanes(strip, 1)


def wet_faces(wet):
    c, e, w, n, s = wet
    return c, c * e, c * w, c * n, c * s


def speeds_of(now):
    return (now[0][0], now[1][0], now[2][0]), (now[0][1], now[3][1], now[4][1])


def kernel(
    gy_size, gx_size, state, irr, land, bottom, out,
    raw, irr_v, land_v, bottom_v, mine, other, packs, pairs, corners_in, rows_in, strip, edges, strip_o, edges_o,
    wet, press, next_d, next_t, nedges,
    load_sem, send_sem, recv_sem, hello, intro,
):
    comp, gy, gx = (lax.axis_index(a) for a in ("comp", "gy", "gx"))
    east, west = lax.rem(gx + 1, gx_size), lax.rem(gx + gx_size - 1, gx_size)
    up, down = lax.rem(gy + 1, gy_size), lax.rem(gy + gy_size - 1, gy_size)
    twin = 1 - comp
    eastern = [(c, y, east) for y in (up, down, gy) for c in (comp, twin)]
    western = [(c, y, west) for y in (up, down, gy) for c in (comp, twin)]

    barrier = pltpu.get_barrier_semaphore()
    for target in western + [(twin, gy, gx)]:
        pl.semaphore_signal(barrier, inc=1, device_id=target, device_id_type=MESH)

    loads = [
        pltpu.make_async_copy(src, dst, load_sem.at[i])
        for i, (src, dst) in enumerate([(irr, irr_v), (land, land_v), (bottom, bottom_v), (state, raw)])
    ]
    for load in loads:
        load.start()

    pl.semaphore_wait(barrier, 7)
    for target in eastern:
        pl.semaphore_signal(hello, inc=1, device_id=target, device_id_type=MESH)
    for load in loads:
        load.wait()

    lane, k = iota(1), iota(0)
    slot, quad = lane % 4, lane // 4
    blank = jnp.zeros((LEV, LANES), jnp.float32)

    def take(x, carry):
        rows, lit_rows = carry
        is_wet = (land_v[pl.ds(x, 1), :] == 1) & (k < bottom_v[pl.ds(x, 1), :])
        lit = jnp.where(is_wet, jnp.broadcast_to(irr_v[pl.ds(x, 1), :], (LEV, LANES)), 0.0)
        mine[8, OWN + x] = lit
        lit_rows = jnp.where(quad == x, lanes(lit, 4 * x + 2), lit_rows)
        for f in range(8):
            value = raw[pl.ds(f * 32 + x, 8, stride=4), :]
            mine[f, OWN + x] = value
            rows = jnp.where(quad == 4 * f + x, lanes(value, lax.rem(16 * f + 4 * x + 2, LANES)), rows)
        return rows, lit_rows

    rows, lit_rows = lax.fori_loop(0, 4, take, (blank, blank))
    packs[0] = jnp.where(slot < 2, rows, lanes(lit_rows, 2))
    packs[1] = jnp.where(slot < 2, lanes(lit_rows, -2), rows)

    def remote(index, src, dst, target):
        return pltpu.make_async_remote_copy(
            src_ref=src, dst_ref=dst, send_sem=send_sem.at[index], recv_sem=recv_sem.at[index],
            device_id=target, device_id_type=MESH,
        )

    ways = [(SW, 0, up, east), (SE, 0, up, west), (NW, 1, down, east), (NE, 1, down, west)]
    same_corners = [remote(s, packs.at[p], corners_in.at[0, s], (comp, y, x)) for s, p, y, x in ways]
    twin_corners = [remote(4 + s, packs.at[p], corners_in.at[1, s], (twin, y, x)) for s, p, y, x in ways]
    row_sends = [
        remote(8 + 2 * p + c, pairs.at[p], rows_in.at[p], (c, y, gx)) for p, y in ((0, up), (1, down)) for c in (0, 1)
    ]
    same_cols = [
        remote(12, mine.at[:, 4:6], mine.at[:, 0:2], (comp, gy, east)),
        remote(13, mine.at[:, 2:4], mine.at[:, 6:8], (comp, gy, west)),
    ]
    flow_cols = [
        remote(14, mine.at[0:8, 4:6], other.at[0:8, 0:2], (twin, gy, east)),
        remote(15, mine.at[0:8, 2:4], other.at[0:8, 6:8], (twin, gy, west)),
    ]
    plant_cols = [
        remote(14, mine.at[2:4, 5:6], other.at[2:4, 1:2], (twin, gy, east)),
        remote(15, mine.at[2:4, 2:3], other.at[2:4, 6:7], (twin, gy, west)),
    ]
    flow_own = remote(16, mine.at[0:8, 2:6], other.at[0:8, 2:6], (twin, gy, gx))
    plant_own = remote(16, mine.at[0:5, 2:6], other.at[0:5, 2:6], (twin, gy, gx))
    pack_own = remote(17, packs, pairs.at[:, 1], (twin, gy, gx))

    dyn_east = [same_corners[SW], twin_corners[SW], same_corners[NW], twin_corners[NW], same_cols[0], flow_cols[0]]
    dyn_west = [same_corners[SE], twin_corners[SE], same_corners[NE], twin_corners[NE], same_cols[1], flow_cols[1]]
    trc_east = [same_corners[SW], same_corners[NW], same_cols[0], plant_cols[0]]
    trc_west = [same_corners[SE], same_corners[NE], same_cols[1], plant_cols[1]]

    def start(copies):
        for copy in copies:
            copy.start()

    def arrived(copies):
        for copy in copies:
            copy.wait_recv()

    def sent(copies):
        for copy in copies:
            copy.wait_send()

    no_south, no_north = gy == 0, gy == gy_size - 1
    low = lane < 64
    inner = (lane % 64 >= 4) & (lane % 64 < 20)

    def keep(ref, edge_ref, f, value):
        ref[f] = value
        edge_ref[f] = row_edges(value)

    def lit_part(value, southern):
        return jnp.where(no_south if southern else no_north, 0.0, lanes(value, -2 if southern else 2))

    def other_rows_of(fields):
        def add(x, result):
            for f in fields:
                value = lanes(other[f, OWN + x], lax.rem(16 * f + 4 * x + 2, LANES))
                result = jnp.where(quad == 4 * f + x, value, result)
            return result

        return lax.fori_loop(0, 4, add, blank)

    def start_strips(me, plants_only):
        def halves_of(own_rows, south, north):
            south = jnp.where(slot < 2, south, own_rows)
            north = lanes(jnp.where(slot < 2, own_rows, north), 64)
            return jnp.where(low, south, north), jnp.where(low, north, south)

        def put(ref, edge_ref, f, half, by=None):
            keep(ref, edge_ref, f, jnp.where(inner, lanes(half, 4 - 16 * f if by is None else by), 0.0))

        south, north = rows_in[0, me], rows_in[1, me]
        south_o, north_o = rows_in[0, 1 - me], rows_in[1, 1 - me]
        first, last = halves_of(rows, south, north)
        lit_first, _ = halves_of(lit_rows, lit_part(south, True), lit_part(north, False))
        put(strip, edges, 8, lit_first, 4)
        first_o, last_o = halves_of(other_rows_of((2, 3) if plants_only else range(8)), south_o, north_o)

        def field(f, carry):
            by, by_last = lax.rem(LANES + 4 - 16 * f, LANES), 68 - 16 * f
            put(strip, edges, f, first, by)
            put(strip, edges, f + 4, last, by_last)
            if not plants_only:
                put(strip_o, edges_o, f, first_o, by)
                put(strip_o, edges_o, f + 4, last_o, by_last)
            return carry

        lax.fori_loop(0, 4, field, 0)
        if plants_only:
            for f in (2, 3):
                put(strip_o, edges_o, f, first_o)

    def add_corners(is_east, plants_only):
        left = 32 * is_east
        there = lane % 64 // 4 == 5 * is_east
        first = (lane >= left) & (lane < 64 + left)

        def halves_of(south, north):
            south, north = lanes(south, left), lanes(north, 64 + left)
            return jnp.where(first, south, north), jnp.where(first, north, south)

        def put(ref, edge_ref, f, half, by):
            keep(ref, edge_ref, f, jnp.where(there, lanes(half, by), ref[f]))

        south, north = corners_in[0, is_east], corners_in[0, 2 + is_east]
        lit_half, _ = halves_of(lit_part(south, True), lit_part(north, False))
        put(strip, edges, 8, lit_half, LANES - 12)
        first_half, last_half = halves_of(south, north)
        if not plants_only:
            first_o, last_o = halves_of(corners_in[1, is_east], corners_in[1, 2 + is_east])

        def field(f, carry):
            by, by_last = LANES - 12 - 16 * f, lax.rem(2 * LANES - 76 - 16 * f, LANES)
            put(strip, edges, f, first_half, by)
            put(strip, edges, f + 4, last_half, by_last)
            if not plants_only:
                put(strip_o, edges_o, f, first_o, by)
                put(strip_o, edges_o, f + 4, last_o, by_last)
            return carry

        lax.fori_loop(0, 4, field, 0)

    def wet_strip():
        return (strip[8] > 0).astype(jnp.float32)

    def wet_at(col, wet_edges):
        return wet_faces(around(lambda c: wet[0, c], wet_edges, col))

    first_row = gy * LANES
    coriolis_main = 0.3 + 0.4 * (first_row + lane).astype(jnp.float32) / float(gy_size * LANES)
    strip_row = first_row + slot + jnp.where(low, -2, LANES - 2)
    coriolis_strip = 0.3 + 0.4 * strip_row.astype(jnp.float32) / float(gy_size * LANES)

    def store_out(f, col, value):
        out[pl.ds(f * 32 + col - OWN, 8, stride=4), :] = value

    def full_step(now, before, p, wets, coriolis, heating):
        u, v = step_speeds(now, before, p, wets, coriolis)
        t, s = step_heat_salt(now, before, wets, heating)
        after = jnp.stack([u, v, t, s])
        return after, filtered(now[0], before[0], after, wets[0])

    def tracer_step(c, u, v, wets, temp, salt, lit):
        kappa = mixing_of(temp, salt, wets[0])
        light = light_of(c[0][2], c[0][3], lit)
        change = transported(c, u, v, wets) + mixed(c[0], kappa) + reactions(c[0], temp, light)
        return c[0] + 0.1 * change * wets[0]

    def dyn_strip():
        dry = wet_strip()
        p = around_strip(pressure_of(strip[2], strip[3], dry))
        heat = heating_of(strip_o[2], strip_o[3], strip[8], dry)
        now, before = around_strip(strip[0:4]), around_strip(strip[4:8])
        after, filt = full_step(now, before, p, wet_faces(around_strip(dry)), coriolis_strip, heat)
        nedges[0:4], nedges[4:8] = row_edges(after), row_edges(filt)
        nedges[8] = row_edges(pressure_of(after[2], after[3], dry))

    def dyn_first(col, wet_edges, press_edges):
        wets = wet_at(col, wet_edges)
        now = around(lambda c: mine[0:4, c], edges[0:4], col)
        before = around(lambda c: mine[4:8, c], edges[4:8], col)
        p = around(lambda c: press[0, c], press_edges, col)
        heat = heating_of(other[2, col], other[3, col], mine[8, col], wets[0])
        after, filt = full_step(now, before, p, wets, coriolis_main, heat)
        next_d[0:4, col], next_d[4:8, col] = after, filt
        press[1, col] = pressure_of(after[2], after[3], wets[0])

        @pl.when((col >= OWN) & (col < OWN + 4))
        def _():
            c = other[0:5, col]
            plants = around(lambda c: other[2:4, c], edges_o[2:4], col)
            kappa = mixing_of(now[0][2], now[0][3], wets[0])
            light = light_of(c[2], c[3], mine[8, col])
            change = transported(plants, *speeds_of(now), wets) + mixed(plants[0], kappa)
            change = change + plant_reactions(c, now[0][2], light)
            next_t[2:4, col] = plants[0] + 0.1 * change * wets[0]

    def dyn_second(col, wet_edges):
        wets = wet_at(col, wet_edges)
        now = around(lambda c: next_d[0:4, c], nedges[0:4], col)
        before = around(lambda c: next_d[4:8, c], nedges[4:8], col)
        p = around(lambda c: press[1, c], nedges[8], col)
        heat = heating_of(next_t[2, col], next_t[3, col], mine[8, col], wets[0])
        after, filt = full_step(now, before, p, wets, coriolis_main, heat)
        for f in range(4):
            store_out(f, col, after[f])
            store_out(4 + f, col, filt[f])

    def trc_strip():
        dry = wet_strip()
        wets = wet_faces(around_strip(dry))
        p = around_strip(pressure_of(strip_o[2], strip_o[3], dry))
        now, before = around_strip(strip_o[0:4]), around_strip(strip_o[4:6])
        u, v = step_speeds(now, before, p, wets, coriolis_strip)
        nedges[8], nedges[9] = row_edges(u), row_edges(v)
        c = around_strip(strip[0:8])
        nedges[0:8] = row_edges(tracer_step(c, *speeds_of(now), wets, strip_o[2], strip_o[3], strip[8]))

    def trc_first(col, wet_edges, press_edges):
        wets = wet_at(col, wet_edges)
        now = around(lambda c: other[0:4, c], edges_o[0:4], col)
        before = around(lambda c: other[4:8, c], edges_o[4:8], col)
        p = around(lambda c: press[0, c], press_edges, col)
        next_d[0, col], next_d[1, col] = step_speeds(now, before, p, wets, coriolis_main)
        c = around(lambda c: mine[0:8, c], edges[0:8], col)
        heat = heating_of(c[0][2], c[0][3], mine[8, col], wets[0])
        next_d[2, col], next_d[3, col] = step_heat_salt(now, before, wets, heat)
        next_t[0:8, col] = tracer_step(c, *speeds_of(now), wets, now[0][2], now[0][3], mine[8, col])

    def trc_second(col, wet_edges):
        c = around(lambda c: next_t[0:8, c], nedges[0:8], col)
        u = around(lambda c: next_d[0, c], nedges[8], col)
        v = around(lambda c: next_d[1, c], nedges[9], col)
        new = tracer_step(
            c, u[:3], (v[0], v[3], v[4]), wet_at(col, wet_edges), next_d[2, col], next_d[3, col], mine[8, col]
        )
        for f in range(8):
            store_out(f, col, new[f])

    def phases(me, own_in, at_east, east_in, west_in, flow, flow_strip, first, at_strip, second):
        def phase(it, carry):
            @pl.when(it == 0)
            def _():
                arrived([own_in, row_sends[me], row_sends[2 + me]])
                start_strips(me, me == 0)

            @pl.when(it == 1)
            def _():
                at_east()
                arrived(east_in)

            @pl.when(it == 2)
            def _():
                arrived(west_in)

            @pl.when(it > 0)
            def _():
                add_corners(2 - it, me == 0)

            dry = wet_strip()
            wet_edges = row_edges(dry)
            press_edges = row_edges(pressure_of(flow_strip[2], flow_strip[3], dry))

            def ready(col, carry):
                is_wet = (mine[8, col] > 0).astype(jnp.float32)
                wet[0, col] = is_wet
                press[0, col] = pressure_of(flow[2, col], flow[3, col], is_wet)
                return carry

            def one(col, carry):
                first(col, wet_edges, press_edges)
                return carry

            def two(col, carry):
                second(col, wet_edges)
                return carry

            begin = jnp.where(it == 0, 2, jnp.where(it == 1, 6, 0))
            lax.fori_loop(begin, begin + jnp.where(it == 0, 4, 2), ready, 0)
            begin = jnp.where(it == 0, 3, jnp.where(it == 1, 5, 1))
            lax.fori_loop(begin, begin + 2, one, 0)

            @pl.when(it > 0)
            def _():
                at_strip()
                lax.fori_loop(6 - 2 * it, 8 - 2 * it, two, 0)

            return carry

        lax.fori_loop(0, 3, phase, 0)

    @pl.when(comp == 0)
    def _():
        start(dyn_east + [flow_own])
        pairs[0, 0] = packs[0]
        pairs[1, 0] = packs[1]
        arrived([pack_own])
        pl.semaphore_wait(intro, 1)
        start(row_sends)

        def at_east():
            pl.semaphore_wait(hello, 6)
            start(dyn_west)

        east_in = [same_corners[SE], same_corners[NE], same_cols[1], plant_cols[1]]
        west_in = [same_corners[SW], same_corners[NW], same_cols[0], plant_cols[0]]
        phases(0, plant_own, at_east, east_in, west_in, mine, strip, dyn_first, dyn_strip, dyn_second)
        sent(dyn_east + [flow_own] + row_sends + dyn_west)

    @pl.when(comp == 1)
    def _():
        start([pack_own] + trc_east + [plant_own])
        pl.semaphore_wait(hello, 6)
        pl.semaphore_signal(intro, inc=1, device_id=(twin, gy, west), device_id_type=MESH)
        start(trc_west)
        east_in = [same_corners[SE], same_corners[NE], twin_corners[SE], twin_corners[NE], same_cols[1], flow_cols[1]]
        west_in = [same_corners[SW], same_corners[NW], twin_corners[SW], twin_corners[NW], same_cols[0], flow_cols[0]]
        phases(1, flow_own, lambda: None, east_in, west_in, other, strip_o, trc_first, trc_strip, trc_second)
        sent([pack_own] + trc_east + [plant_own] + trc_west)


def solution(mesh):
    gy_size, gx_size = mesh.shape["gy"], mesh.shape["gx"]

    def local(ocean_state, irradiance, land_mask, bottom_level):
        rows = ocean_state.size // LANES
        anywhere = pl.BlockSpec(memory_space=pl.ANY)
        f32 = jnp.float32
        operands = (ocean_state.reshape(rows, LANES), irradiance, land_mask, bottom_level)
        result = pl.pallas_call(
            functools.partial(kernel, gy_size, gx_size),
            out_shape=jax.ShapeDtypeStruct((rows, LANES), f32),
            in_specs=[anywhere] * 4,
            out_specs=pl.BlockSpec(memory_space=pltpu.VMEM),
            scratch_shapes=[
                pltpu.VMEM((rows, LANES), f32),
                pltpu.VMEM((4, LANES), f32),
                pltpu.VMEM((4, LANES), jnp.int32),
                pltpu.VMEM((4, LANES), jnp.int32),
                pltpu.VMEM((9, 8, LEV, LANES), f32),
                pltpu.VMEM((8, 8, LEV, LANES), f32),
                pltpu.VMEM((2, LEV, LANES), f32),
                pltpu.VMEM((2, 2, LEV, LANES), f32),
                pltpu.VMEM((2, 4, LEV, LANES), f32),
                pltpu.VMEM((2, 2, LEV, LANES), f32),
                pltpu.VMEM((9, LEV, LANES), f32),
                pltpu.VMEM((9, LEV, LANES), f32),
                pltpu.VMEM((8, LEV, LANES), f32),
                pltpu.VMEM((8, LEV, LANES), f32),
                pltpu.VMEM((1, 8, LEV, LANES), f32),
                pltpu.VMEM((2, 8, LEV, LANES), f32),
                pltpu.VMEM((8, 8, LEV, LANES), f32),
                pltpu.VMEM((8, 8, LEV, LANES), f32),
                pltpu.VMEM((10, LEV, LANES), f32),
                pltpu.SemaphoreType.DMA((4,)),
                pltpu.SemaphoreType.DMA((18,)),
                pltpu.SemaphoreType.DMA((18,)),
                pltpu.SemaphoreType.REGULAR,
                pltpu.SemaphoreType.REGULAR,
            ],
            compiler_params=pltpu.CompilerParams(
                collective_id=0, has_side_effects=True, vmem_limit_bytes=8 * 1024 * 1024
            ),
            name="coupled_steps",
        )(*[pltpu.with_memory_space_constraint(a, pltpu.HBM) for a in operands])
        return result.reshape(ocean_state.shape)

    return jax.shard_map(
        local,
        mesh=mesh,
        in_specs=(P("comp", None, "gx", "gy"), P("gx", "gy"), P("gx", "gy"), P("gx", "gy")),
        out_specs=P("comp", None, "gx", "gy"),
        check_vma=False,
    )
```

```python
import functools

import jax
import jax.numpy as jnp
from jax import lax
from jax.experimental import pallas as pl
from jax.experimental.pallas import tpu as pltpu
from jax.sharding import PartitionSpec as P

MESH = pl.DeviceIdType.MESH

SW, SE, NW, NE = range(4)
OWN = 2
LEV, LANES = 8, 128


def roll(value, shift, axis):
    return pltpu.roll(value, shift % value.shape[axis] if isinstance(shift, int) else shift, axis)


def lanes(value, shift):
    return roll(value, shift, value.ndim - 1)


def levels(value, shift):
    return roll(value, shift, value.ndim - 2)


def iota(dim):
    return lax.broadcasted_iota(jnp.int32, (LEV, LANES), dim)


def level_sum(value):
    k = iota(0)
    for shift in (1, 2, 4):
        value = value + jnp.where(k >= shift, levels(value, shift), 0.0)
    return value


def density(temp, salt, wet):
    return (0.8 * salt - 0.2 * temp) * wet


def pressure_of(temp, salt, wet):
    return 0.1 * level_sum(density(temp, salt, wet))


def mixing_of(temp, salt, wet):
    rho = density(temp, salt, wet)
    strat = jnp.maximum(levels(rho, -1) - rho, 0.0)
    wet_below = jnp.where(iota(0) == LEV - 1, 0.0, levels(wet, -1))
    return (0.05 + 1.0 / (1.0 + 4.0 * strat)) * wet * wet_below


def absorbed(small, large):
    absorb = 0.08 + 0.05 * (jnp.abs(small) + jnp.abs(large))
    return absorb, level_sum(absorb)


def surface_of(lit):
    return jnp.broadcast_to(lit[0:1, :], (LEV, LANES))


def heating_of(small, large, lit, wet):
    absorb, column = absorbed(small, large)
    return surface_of(lit) * (jnp.exp(absorb - column) - jnp.exp(-column)) * wet


def light_of(small, large, lit):
    absorb, column = absorbed(small, large)
    return surface_of(lit) * jnp.exp(0.5 * absorb - column)


def gradients(p, wet):
    pc, pe, pw, pn, ps = p
    _, we, ww, wn, ws = wet
    return 0.5 * (we * (pe - pc) + ww * (pc - pw)), 0.5 * (wn * (pn - pc) + ws * (pc - ps))


def spread_of(field, wet):
    c, e, w, n, s = field
    _, we, ww, wn, ws = wet
    return we * (e - c) + ww * (w - c) + wn * (n - c) + ws * (s - c)


def faces(u, v, wet):
    (uc, ue, uw), (vc, vn, vs) = u, v
    _, we, ww, wn, ws = wet
    return 0.25 * (uc + ue) * we, 0.25 * (uc + uw) * ww, 0.25 * (vc + vn) * wn, 0.25 * (vc + vs) * ws


def carried_of(field, face):
    c, e, w, n, s = field
    fe, fw, fn, fs = face
    return fe * (c + e) - fw * (c + w) + fn * (c + n) - fs * (c + s)


def pick(five, index):
    return tuple(part[index] for part in five)


def step_speeds(now, before, p, wet, coriolis):
    force_east, force_north = gradients(p, wet)
    u, v = now[0][0], now[0][1]
    du = coriolis * v - force_east + 0.2 * spread_of(pick(before, 0), wet)
    dv = -coriolis * u - force_north + 0.2 * spread_of(pick(before, 1), wet)
    return before[0][0] + 0.2 * du * wet[0], before[0][1] + 0.2 * dv * wet[0]


def step_heat_salt(now, before, wet, heating):
    u = (now[0][0], now[1][0], now[2][0])
    v = (now[0][1], now[3][1], now[4][1])
    face = faces(u, v, wet)
    dt = -carried_of(pick(now, 2), face) + 0.2 * spread_of(pick(before, 2), wet) + 3.0 * heating
    ds = -carried_of(pick(now, 3), face) + 0.2 * spread_of(pick(before, 3), wet)
    return before[0][2] + 0.2 * dt * wet[0], before[0][3] + 0.2 * ds * wet[0]


def filtered(now, before, after, wet):
    return now + 0.1 * (before - 2.0 * now + after) * wet


def transported(field, u, v, wet):
    c, e, w, n, s = field
    _, we, ww, wn, ws = wet
    fe, fw, fn, fs = faces(u, v, wet)
    le, lw, ln, ls = 0.2 * we, 0.2 * ww, 0.2 * wn, 0.2 * ws
    own = (le + fe) + (lw - fw) + (ln + fn) + (ls - fs)
    return (le - fe) * e + (lw + fw) * w + (ln - fn) * n + (ls + fs) * s - own * c


def mixed(c, kappa):
    down = kappa * (levels(c, -1) - c)
    return down - levels(down, 1)


def growth_of(nitrate, ammonium, small, large, temp, light):
    rate = jnp.exp(0.06 * temp) * (light / (light + 0.5))
    both = jnp.abs(nitrate) + jnp.abs(ammonium)
    return 0.6 * rate * small / (0.2 + both), 0.9 * rate * large / (0.8 + both)


def reactions(c, temp, light):
    nn, na = jnp.abs(c[0]), jnp.abs(c[1])
    small, large = growth_of(c[0], c[1], c[2], c[3], temp, light)
    sn, sa, ln, la = small * nn, small * na, large * nn, large * na
    graze = 0.8 * c[4] / (1.0 + jnp.abs(c[2]) + jnp.abs(c[3]))
    gs, gl = graze * c[2], graze * c[3]
    remin = 0.3 * c[5] + 0.1 * c[6]
    nitrify = 0.2 * c[1]
    return jnp.stack(
        [
            nitrify - sn - ln,
            remin + 0.1 * c[4] - nitrify - sa - la,
            sn + sa - gs - 0.1 * c[2],
            ln + la - gl - 0.1 * c[3],
            0.7 * (gs + gl) - 0.1 * c[4] - 0.15 * c[4],
            0.1 * c[2] + 0.3 * gs - 0.3 * c[5],
            0.1 * c[3] + 0.15 * c[4] + 0.3 * gl - 0.1 * c[6],
            1.3 * (sn + sa + ln + la) - (remin + 2.0 * nitrify),
        ]
    )


def plant_reactions(c, temp, light):
    both = jnp.abs(c[0]) + jnp.abs(c[1])
    small, large = growth_of(c[0], c[1], c[2], c[3], temp, light)
    graze = 0.8 * c[4] / (1.0 + jnp.abs(c[2]) + jnp.abs(c[3]))
    return jnp.stack([small * both - graze * c[2] - 0.1 * c[2], large * both - graze * c[3] - 0.1 * c[3]])


def row_edges(strip):
    slot = iota(1) % 4
    return jnp.where(slot == 2, lanes(strip, 64), strip)


def around(columns, edges, col):
    lane = iota(1)
    c = columns(col)
    edge = lanes(edges, LANES - 2 - 4 * (col - 1))
    north = lanes(jnp.where(lane == 0, edge, c), -1)
    south = lanes(jnp.where(lane == LANES - 1, edge, c), 1)
    return c, columns(col + 1), columns(col - 1), north, south


def around_strip(strip):
    return strip, lanes(strip, -4), lanes(strip, 4), lanes(strip, -1), lanes(strip, 1)


def wet_faces(wet):
    c, e, w, n, s = wet
    return c, c * e, c * w, c * n, c * s


def speeds_of(now):
    return (now[0][0], now[1][0], now[2][0]), (now[0][1], now[3][1], now[4][1])


def kernel(
    gy_size, gx_size, state, irr, land, bottom, out,
    raw, irr_v, land_v, bottom_v, mine, other, packs, pairs, corners_in, rows_in, strip, edges, strip_o, edges_o,
    wet, press, next_d, next_t, nedges,
    load_sem, send_sem, recv_sem, hello, intro,
):
    comp, gy, gx = (lax.axis_index(a) for a in ("comp", "gy", "gx"))
    east, west = lax.rem(gx + 1, gx_size), lax.rem(gx + gx_size - 1, gx_size)
    up, down = lax.rem(gy + 1, gy_size), lax.rem(gy + gy_size - 1, gy_size)
    twin = 1 - comp
    eastern = [(c, y, east) for y in (up, down, gy) for c in (comp, twin)]
    western = [(c, y, west) for y in (up, down, gy) for c in (comp, twin)]

    barrier = pltpu.get_barrier_semaphore()
    for target in western + [(twin, gy, gx)]:
        pl.semaphore_signal(barrier, inc=1, device_id=target, device_id_type=MESH)

    loads = [
        pltpu.make_async_copy(src, dst, load_sem.at[i])
        for i, (src, dst) in enumerate([(irr, irr_v), (land, land_v), (bottom, bottom_v), (state, raw)])
    ]
    for load in loads:
        load.start()

    pl.semaphore_wait(barrier, 7)
    for target in eastern:
        pl.semaphore_signal(hello, inc=1, device_id=target, device_id_type=MESH)
    for load in loads:
        load.wait()

    lane, k = iota(1), iota(0)
    slot, quad = lane % 4, lane // 4
    blank = jnp.zeros((LEV, LANES), jnp.float32)

    for x in (2, 3, 0, 1):
        is_wet = (land_v[x : x + 1, :] == 1) & (k < bottom_v[x : x + 1, :])
        mine[8, OWN + x] = jnp.where(is_wet, jnp.broadcast_to(irr_v[x : x + 1, :], (LEV, LANES)), 0.0)
        for f in range(8):
            mine[f, OWN + x] = raw[pl.ds(f * 32 + x, 8, stride=4), :]

    def remote(index, src, dst, target):
        return pltpu.make_async_remote_copy(
            src_ref=src, dst_ref=dst, send_sem=send_sem.at[index], recv_sem=recv_sem.at[index],
            device_id=target, device_id_type=MESH,
        )

    ways = [(SW, 0, up, east), (SE, 0, up, west), (NW, 1, down, east), (NE, 1, down, west)]
    same_corners = [remote(s, packs.at[p], corners_in.at[0, s], (comp, y, x)) for s, p, y, x in ways]
    twin_corners = [remote(4 + s, packs.at[p], corners_in.at[1, s], (twin, y, x)) for s, p, y, x in ways]
    row_sends = [
        remote(8 + 2 * p + c, pairs.at[p], rows_in.at[p], (c, y, gx)) for p, y in ((0, up), (1, down)) for c in (0, 1)
    ]
    same_cols = [
        remote(12, mine.at[:, 4:6], mine.at[:, 0:2], (comp, gy, east)),
        remote(13, mine.at[:, 2:4], mine.at[:, 6:8], (comp, gy, west)),
    ]
    flow_cols = [
        remote(14, mine.at[0:8, 4:6], other.at[0:8, 0:2], (twin, gy, east)),
        remote(15, mine.at[0:8, 2:4], other.at[0:8, 6:8], (twin, gy, west)),
    ]
    plant_cols = [
        remote(14, mine.at[2:4, 5:6], other.at[2:4, 1:2], (twin, gy, east)),
        remote(15, mine.at[2:4, 2:3], other.at[2:4, 6:7], (twin, gy, west)),
    ]
    flow_own = remote(16, mine.at[0:8, 2:6], other.at[0:8, 2:6], (twin, gy, gx))
    plant_own = remote(16, mine.at[0:5, 2:6], other.at[0:5, 2:6], (twin, gy, gx))
    pack_own = remote(17, packs, pairs.at[:, 1], (twin, gy, gx))

    dyn_east = [same_corners[SW], twin_corners[SW], same_corners[NW], twin_corners[NW], same_cols[0], flow_cols[0]]
    dyn_west = [same_corners[SE], twin_corners[SE], same_corners[NE], twin_corners[NE], same_cols[1], flow_cols[1]]
    trc_east = [same_corners[SW], same_corners[NW], same_cols[0], plant_cols[0]]
    trc_west = [same_corners[SE], same_corners[NE], same_cols[1], plant_cols[1]]

    def start(copies):
        for copy in copies:
            copy.start()

    def arrived(copies):
        for copy in copies:
            copy.wait_recv()

    def sent(copies):
        for copy in copies:
            copy.wait_send()

    @pl.when(comp == 0)
    def _():
        start([same_cols[0], flow_cols[0]])

    @pl.when(comp == 1)
    def _():
        start([same_cols[0], plant_cols[0]])

    rows, lit_rows = blank, blank
    for x in range(4):
        for f in range(8):
            rows = jnp.where(quad == 4 * f + x, lanes(mine[f, OWN + x], 16 * f + 4 * x + 2), rows)
        lit_rows = jnp.where(quad == x, lanes(mine[8, OWN + x], 4 * x + 2), lit_rows)
    packs[0] = jnp.where(slot < 2, rows, lanes(lit_rows, 2))
    packs[1] = jnp.where(slot < 2, lanes(lit_rows, -2), rows)

    no_south, no_north = gy == 0, gy == gy_size - 1
    low = lane < 64
    inner = (lane % 64 >= 4) & (lane % 64 < 20)

    def keep(ref, edge_ref, f, value):
        ref[f] = value
        edge_ref[f] = row_edges(value)

    def lit_part(value, southern):
        return jnp.where(no_south if southern else no_north, 0.0, lanes(value, -2 if southern else 2))

    def other_rows_of(fields):
        result = blank
        for x in range(4):
            for f in fields:
                result = jnp.where(quad == 4 * f + x, lanes(other[f, OWN + x], 16 * f + 4 * x + 2), result)
        return result

    def start_strips(me, plants_only):
        def halves_of(own_rows, south, north):
            south = jnp.where(slot < 2, south, own_rows)
            north = lanes(jnp.where(slot < 2, own_rows, north), 64)
            return jnp.where(low, south, north), jnp.where(low, north, south)

        def put(ref, edge_ref, f, half, by):
            keep(ref, edge_ref, f, jnp.where(inner, lanes(half, by), 0.0))

        south, north = rows_in[0, me], rows_in[1, me]
        south_o, north_o = rows_in[0, 1 - me], rows_in[1, 1 - me]
        first, last = halves_of(rows, south, north)
        lit_first, _ = halves_of(lit_rows, lit_part(south, True), lit_part(north, False))
        put(strip, edges, 8, lit_first, 4)
        fields = (2, 3) if plants_only else range(8)
        halves = (first, last)
        halves_o = halves_of(other_rows_of(fields), south_o, north_o)
        for f in range(8):
            put(strip, edges, f, halves[f // 4], 4 - 16 * f)
        for f in fields:
            put(strip_o, edges_o, f, halves_o[f // 4], 4 - 16 * f)

    def add_corners(is_east, plants_only):
        left = 32 * is_east
        there = lane % 64 // 4 == 5 * is_east
        first = (lane >= left) & (lane < 64 + left)

        def halves_of(south, north):
            south, north = lanes(south, left), lanes(north, 64 + left)
            return jnp.where(first, south, north), jnp.where(first, north, south)

        def put(ref, edge_ref, f, half, by):
            keep(ref, edge_ref, f, jnp.where(there, lanes(half, by), ref[f]))

        south, north = corners_in[0, is_east], corners_in[0, 2 + is_east]
        lit_half, _ = halves_of(lit_part(south, True), lit_part(north, False))
        put(strip, edges, 8, lit_half, -12)
        halves = halves_of(south, north)
        for f in range(8):
            put(strip, edges, f, halves[f // 4], -12 - 16 * f)
        if not plants_only:
            halves_o = halves_of(corners_in[1, is_east], corners_in[1, 2 + is_east])
            for f in range(8):
                put(strip_o, edges_o, f, halves_o[f // 4], -12 - 16 * f)

    def wet_strip():
        return (strip[8] > 0).astype(jnp.float32)

    def wet_at(col, wet_edges):
        return wet_faces(around(lambda c: wet[0, c], wet_edges, col))

    first_row = gy * LANES
    coriolis_main = 0.3 + 0.4 * (first_row + lane).astype(jnp.float32) / float(gy_size * LANES)
    strip_row = first_row + slot + jnp.where(low, -2, LANES - 2)
    coriolis_strip = 0.3 + 0.4 * strip_row.astype(jnp.float32) / float(gy_size * LANES)

    def store_out(f, col, value):
        out[pl.ds(f * 32 + col - OWN, 8, stride=4), :] = value

    def full_step(now, before, p, wets, coriolis, heating):
        u, v = step_speeds(now, before, p, wets, coriolis)
        t, s = step_heat_salt(now, before, wets, heating)
        after = jnp.stack([u, v, t, s])
        return after, filtered(now[0], before[0], after, wets[0])

    def tracer_step(c, u, v, wets, temp, salt, lit):
        kappa = mixing_of(temp, salt, wets[0])
        light = light_of(c[0][2], c[0][3], lit)
        change = transported(c, u, v, wets) + mixed(c[0], kappa) + reactions(c[0], temp, light)
        return c[0] + 0.1 * change * wets[0]

    def dyn_strip():
        dry = wet_strip()
        p = around_strip(pressure_of(strip[2], strip[3], dry))
        heat = heating_of(strip_o[2], strip_o[3], strip[8], dry)
        now, before = around_strip(strip[0:4]), around_strip(strip[4:8])
        after, filt = full_step(now, before, p, wet_faces(around_strip(dry)), coriolis_strip, heat)
        nedges[0:4], nedges[4:8] = row_edges(after), row_edges(filt)
        nedges[8] = row_edges(pressure_of(after[2], after[3], dry))

    def dyn_first(col, wet_edges, press_edges):
        wets = wet_at(col, wet_edges)
        now = around(lambda c: mine[0:4, c], edges[0:4], col)
        before = around(lambda c: mine[4:8, c], edges[4:8], col)
        p = around(lambda c: press[0, c], press_edges, col)
        heat = heating_of(other[2, col], other[3, col], mine[8, col], wets[0])
        after, filt = full_step(now, before, p, wets, coriolis_main, heat)
        next_d[0:4, col], next_d[4:8, col] = after, filt
        press[1, col] = pressure_of(after[2], after[3], wets[0])

        if OWN <= col < OWN + 4:
            c = other[0:5, col]
            plants = around(lambda c: other[2:4, c], edges_o[2:4], col)
            kappa = mixing_of(now[0][2], now[0][3], wets[0])
            light = light_of(c[2], c[3], mine[8, col])
            change = transported(plants, *speeds_of(now), wets) + mixed(plants[0], kappa)
            change = change + plant_reactions(c, now[0][2], light)
            next_t[2:4, col] = plants[0] + 0.1 * change * wets[0]

    def dyn_second(col, wet_edges):
        wets = wet_at(col, wet_edges)
        now = around(lambda c: next_d[0:4, c], nedges[0:4], col)
        before = around(lambda c: next_d[4:8, c], nedges[4:8], col)
        p = around(lambda c: press[1, c], nedges[8], col)
        heat = heating_of(next_t[2, col], next_t[3, col], mine[8, col], wets[0])
        after, filt = full_step(now, before, p, wets, coriolis_main, heat)
        for f in range(4):
            store_out(f, col, after[f])
            store_out(4 + f, col, filt[f])

    def trc_strip():
        dry = wet_strip()
        wets = wet_faces(around_strip(dry))
        p = around_strip(pressure_of(strip_o[2], strip_o[3], dry))
        now, before = around_strip(strip_o[0:4]), around_strip(strip_o[4:6])
        u, v = step_speeds(now, before, p, wets, coriolis_strip)
        nedges[8], nedges[9] = row_edges(u), row_edges(v)
        c = around_strip(strip[0:8])
        nedges[0:8] = row_edges(tracer_step(c, *speeds_of(now), wets, strip_o[2], strip_o[3], strip[8]))

    def trc_first(col, wet_edges, press_edges):
        wets = wet_at(col, wet_edges)
        now = around(lambda c: other[0:4, c], edges_o[0:4], col)
        before = around(lambda c: other[4:8, c], edges_o[4:8], col)
        p = around(lambda c: press[0, c], press_edges, col)
        next_d[0, col], next_d[1, col] = step_speeds(now, before, p, wets, coriolis_main)
        c = around(lambda c: mine[0:8, c], edges[0:8], col)
        if OWN <= col < OWN + 4:
            heat = heating_of(c[0][2], c[0][3], mine[8, col], wets[0])
            next_d[2, col], next_d[3, col] = step_heat_salt(now, before, wets, heat)
        next_t[0:8, col] = tracer_step(c, *speeds_of(now), wets, now[0][2], now[0][3], mine[8, col])

    def trc_second(col, wet_edges):
        c = around(lambda c: next_t[0:8, c], nedges[0:8], col)
        u = around(lambda c: next_d[0, c], nedges[8], col)
        v = around(lambda c: next_d[1, c], nedges[9], col)
        new = tracer_step(
            c, u[:3], (v[0], v[3], v[4]), wet_at(col, wet_edges), next_d[2, col], next_d[3, col], mine[8, col]
        )
        for f in range(8):
            store_out(f, col, new[f])

    def phases(me, own_in, east_in, west_in, flow, flow_strip, first, at_strip, second):
        inputs = [own_in, row_sends[me], row_sends[2 + me]], east_in, west_in
        for it, (new, todo) in enumerate([(range(2, 6), (3, 4)), ((6, 7), (5, 6)), ((0, 1), (2, 1))]):
            arrived(inputs[it])
            if it == 0:
                start_strips(me, me == 0)
            else:
                add_corners(2 - it, me == 0)
            dry = wet_strip()
            wet_edges = row_edges(dry)
            press_edges = row_edges(pressure_of(flow_strip[2], flow_strip[3], dry))
            for col in new:
                is_wet = (mine[8, col] > 0).astype(jnp.float32)
                wet[0, col] = is_wet
                press[0, col] = pressure_of(flow[2, col], flow[3, col], is_wet)
            for col in todo:
                first(col, wet_edges, press_edges)
            if it > 0:
                at_strip()
                for col in (6 - 2 * it, 7 - 2 * it):
                    second(col, wet_edges)

    @pl.when(comp == 0)
    def _():
        start(dyn_east[:4] + [flow_own])
        pairs[0, 0] = packs[0]
        pairs[1, 0] = packs[1]
        arrived([pack_own])
        pl.semaphore_wait(intro, 1)
        start(row_sends)
        pl.semaphore_wait(hello, 6)
        start(dyn_west)
        east_in = [same_corners[SE], same_corners[NE], same_cols[1], plant_cols[1]]
        west_in = [same_corners[SW], same_corners[NW], same_cols[0], plant_cols[0]]
        phases(0, plant_own, east_in, west_in, mine, strip, dyn_first, dyn_strip, dyn_second)
        sent(dyn_east + [flow_own] + row_sends + dyn_west)

    @pl.when(comp == 1)
    def _():
        start(trc_east[:2] + [pack_own, plant_own])
        pl.semaphore_wait(hello, 6)
        pl.semaphore_signal(intro, inc=1, device_id=(twin, gy, west), device_id_type=MESH)
        start(trc_west)
        east_in = [same_corners[SE], same_corners[NE], twin_corners[SE], twin_corners[NE], same_cols[1], flow_cols[1]]
        west_in = [same_corners[SW], same_corners[NW], twin_corners[SW], twin_corners[NW], same_cols[0], flow_cols[0]]
        phases(1, flow_own, east_in, west_in, other, strip_o, trc_first, trc_strip, trc_second)
        sent([pack_own] + trc_east + [plant_own] + trc_west)


def solution(mesh):
    gy_size, gx_size = mesh.shape["gy"], mesh.shape["gx"]

    def local(ocean_state, irradiance, land_mask, bottom_level):
        rows = ocean_state.size // LANES
        anywhere = pl.BlockSpec(memory_space=pl.ANY)
        f32 = jnp.float32
        operands = (ocean_state.reshape(rows, LANES), irradiance, land_mask, bottom_level)
        result = pl.pallas_call(
            functools.partial(kernel, gy_size, gx_size),
            out_shape=jax.ShapeDtypeStruct((rows, LANES), f32),
            in_specs=[anywhere] * 4,
            out_specs=pl.BlockSpec(memory_space=pltpu.VMEM),
            scratch_shapes=[
                pltpu.VMEM((rows, LANES), f32),
                pltpu.VMEM((4, LANES), f32),
                pltpu.VMEM((4, LANES), jnp.int32),
                pltpu.VMEM((4, LANES), jnp.int32),
                pltpu.VMEM((9, 8, LEV, LANES), f32),
                pltpu.VMEM((8, 8, LEV, LANES), f32),
                pltpu.VMEM((2, LEV, LANES), f32),
                pltpu.VMEM((2, 2, LEV, LANES), f32),
                pltpu.VMEM((2, 4, LEV, LANES), f32),
                pltpu.VMEM((2, 2, LEV, LANES), f32),
                pltpu.VMEM((9, LEV, LANES), f32),
                pltpu.VMEM((9, LEV, LANES), f32),
                pltpu.VMEM((8, LEV, LANES), f32),
                pltpu.VMEM((8, LEV, LANES), f32),
                pltpu.VMEM((1, 8, LEV, LANES), f32),
                pltpu.VMEM((2, 8, LEV, LANES), f32),
                pltpu.VMEM((8, 8, LEV, LANES), f32),
                pltpu.VMEM((8, 8, LEV, LANES), f32),
                pltpu.VMEM((10, LEV, LANES), f32),
                pltpu.SemaphoreType.DMA((4,)),
                pltpu.SemaphoreType.DMA((18,)),
                pltpu.SemaphoreType.DMA((18,)),
                pltpu.SemaphoreType.REGULAR,
                pltpu.SemaphoreType.REGULAR,
            ],
            compiler_params=pltpu.CompilerParams(
                collective_id=0, has_side_effects=True, vmem_limit_bytes=8 * 1024 * 1024
            ),
            name="coupled_steps",
        )(*[pltpu.with_memory_space_constraint(a, pltpu.HBM) for a in operands])
        return result.reshape(ocean_state.shape)

    return jax.shard_map(
        local,
        mesh=mesh,
        in_specs=(P("comp", None, "gx", "gy"), P("gx", "gy"), P("gx", "gy"), P("gx", "gy")),
        out_specs=P("comp", None, "gx", "gy"),
        check_vma=False,
    )
```

```python
import functools

import jax
import jax.numpy as jnp
from jax import lax
from jax.experimental import pallas as pl
from jax.experimental.pallas import tpu as pltpu
from jax.sharding import PartitionSpec as P

MESH = pl.DeviceIdType.MESH

SW, SE, NW, NE = range(4)
OWN = 2
LEV, LANES = 8, 128


def roll(value, shift, axis):
    return pltpu.roll(value, shift % value.shape[axis] if isinstance(shift, int) else shift, axis)


def lanes(value, shift):
    return roll(value, shift, value.ndim - 1)


def levels(value, shift):
    return roll(value, shift, value.ndim - 2)


def iota(dim):
    return lax.broadcasted_iota(jnp.int32, (LEV, LANES), dim)


def level_sum(value):
    k = iota(0)
    for shift in (1, 2, 4):
        value = value + jnp.where(k >= shift, levels(value, shift), 0.0)
    return value


def density(temp, salt, wet):
    return (0.8 * salt - 0.2 * temp) * wet


def pressure_of(temp, salt, wet):
    return 0.1 * level_sum(density(temp, salt, wet))


def mixing_of(temp, salt, wet):
    rho = density(temp, salt, wet)
    strat = jnp.maximum(levels(rho, -1) - rho, 0.0)
    wet_below = jnp.where(iota(0) == LEV - 1, 0.0, levels(wet, -1))
    return (0.05 + 1.0 / (1.0 + 4.0 * strat)) * wet * wet_below


def absorbed(small, large):
    absorb = 0.08 + 0.05 * (jnp.abs(small) + jnp.abs(large))
    return absorb, level_sum(absorb)


def surface_of(lit):
    return jnp.broadcast_to(lit[0:1, :], (LEV, LANES))


def heating_of(small, large, lit, wet):
    absorb, column = absorbed(small, large)
    return surface_of(lit) * (jnp.exp(absorb - column) - jnp.exp(-column)) * wet


def light_of(small, large, lit):
    absorb, column = absorbed(small, large)
    return surface_of(lit) * jnp.exp(0.5 * absorb - column)


def gradients(p, wet):
    pc, pe, pw, pn, ps = p
    _, we, ww, wn, ws = wet
    return 0.5 * (we * (pe - pc) + ww * (pc - pw)), 0.5 * (wn * (pn - pc) + ws * (pc - ps))


def spread_of(field, wet):
    c, e, w, n, s = field
    _, we, ww, wn, ws = wet
    return we * (e - c) + ww * (w - c) + wn * (n - c) + ws * (s - c)


def faces(u, v, wet):
    (uc, ue, uw), (vc, vn, vs) = u, v
    _, we, ww, wn, ws = wet
    return 0.25 * (uc + ue) * we, 0.25 * (uc + uw) * ww, 0.25 * (vc + vn) * wn, 0.25 * (vc + vs) * ws


def carried_of(field, face):
    c, e, w, n, s = field
    fe, fw, fn, fs = face
    return fe * (c + e) - fw * (c + w) + fn * (c + n) - fs * (c + s)


def pick(five, index):
    return tuple(part[index] for part in five)


def step_speeds(now, before, p, wet, coriolis):
    force_east, force_north = gradients(p, wet)
    u, v = now[0][0], now[0][1]
    du = coriolis * v - force_east + 0.2 * spread_of(pick(before, 0), wet)
    dv = -coriolis * u - force_north + 0.2 * spread_of(pick(before, 1), wet)
    return before[0][0] + 0.2 * du * wet[0], before[0][1] + 0.2 * dv * wet[0]


def step_heat_salt(now, before, wet, heating):
    u = (now[0][0], now[1][0], now[2][0])
    v = (now[0][1], now[3][1], now[4][1])
    face = faces(u, v, wet)
    dt = -carried_of(pick(now, 2), face) + 0.2 * spread_of(pick(before, 2), wet) + 3.0 * heating
    ds = -carried_of(pick(now, 3), face) + 0.2 * spread_of(pick(before, 3), wet)
    return before[0][2] + 0.2 * dt * wet[0], before[0][3] + 0.2 * ds * wet[0]


def filtered(now, before, after, wet):
    return now + 0.1 * (before - 2.0 * now + after) * wet


def transported(field, u, v, wet):
    c, e, w, n, s = field
    _, we, ww, wn, ws = wet
    fe, fw, fn, fs = faces(u, v, wet)
    le, lw, ln, ls = 0.2 * we, 0.2 * ww, 0.2 * wn, 0.2 * ws
    own = (le + fe) + (lw - fw) + (ln + fn) + (ls - fs)
    return (le - fe) * e + (lw + fw) * w + (ln - fn) * n + (ls + fs) * s - own * c


def mixed(c, kappa):
    down = kappa * (levels(c, -1) - c)
    return down - levels(down, 1)


def growth_of(nitrate, ammonium, small, large, temp, light):
    rate = jnp.exp(0.06 * temp) * (light / (light + 0.5))
    both = jnp.abs(nitrate) + jnp.abs(ammonium)
    return 0.6 * rate * small / (0.2 + both), 0.9 * rate * large / (0.8 + both)


def reactions(c, temp, light):
    nn, na = jnp.abs(c[0]), jnp.abs(c[1])
    small, large = growth_of(c[0], c[1], c[2], c[3], temp, light)
    sn, sa, ln, la = small * nn, small * na, large * nn, large * na
    graze = 0.8 * c[4] / (1.0 + jnp.abs(c[2]) + jnp.abs(c[3]))
    gs, gl = graze * c[2], graze * c[3]
    remin = 0.3 * c[5] + 0.1 * c[6]
    nitrify = 0.2 * c[1]
    return jnp.stack(
        [
            nitrify - sn - ln,
            remin + 0.1 * c[4] - nitrify - sa - la,
            sn + sa - gs - 0.1 * c[2],
            ln + la - gl - 0.1 * c[3],
            0.7 * (gs + gl) - 0.1 * c[4] - 0.15 * c[4],
            0.1 * c[2] + 0.3 * gs - 0.3 * c[5],
            0.1 * c[3] + 0.15 * c[4] + 0.3 * gl - 0.1 * c[6],
            1.3 * (sn + sa + ln + la) - (remin + 2.0 * nitrify),
        ]
    )


def plant_reactions(c, temp, light):
    both = jnp.abs(c[0]) + jnp.abs(c[1])
    small, large = growth_of(c[0], c[1], c[2], c[3], temp, light)
    graze = 0.8 * c[4] / (1.0 + jnp.abs(c[2]) + jnp.abs(c[3]))
    return jnp.stack([small * both - graze * c[2] - 0.1 * c[2], large * both - graze * c[3] - 0.1 * c[3]])


def row_edges(strip):
    slot = iota(1) % 4
    return jnp.where(slot == 2, lanes(strip, 64), strip)


def around(columns, edges, col):
    lane = iota(1)
    c = columns(col)
    edge = lanes(edges, LANES - 2 - 4 * (col - 1))
    north = lanes(jnp.where(lane == 0, edge, c), -1)
    south = lanes(jnp.where(lane == LANES - 1, edge, c), 1)
    return c, columns(col + 1), columns(col - 1), north, south


def around_strip(strip):
    return strip, lanes(strip, -4), lanes(strip, 4), lanes(strip, -1), lanes(strip, 1)


def wet_faces(wet):
    c, e, w, n, s = wet
    return c, c * e, c * w, c * n, c * s


def speeds_of(now):
    return (now[0][0], now[1][0], now[2][0]), (now[0][1], now[3][1], now[4][1])


def kernel(
    gy_size, gx_size, state, irr, land, bottom, out,
    raw, irr_v, land_v, bottom_v, mine, other, packs, pairs, corners_in, rows_in, strip, edges, strip_o, edges_o,
    wet, press, next_d, next_t, nedges,
    load_sem, send_sem, recv_sem, hello, intro,
):
    comp, gy, gx = (lax.axis_index(a) for a in ("comp", "gy", "gx"))
    east, west = lax.rem(gx + 1, gx_size), lax.rem(gx + gx_size - 1, gx_size)
    up, down = lax.rem(gy + 1, gy_size), lax.rem(gy + gy_size - 1, gy_size)
    twin = 1 - comp
    eastern = [(c, y, east) for y in (up, down, gy) for c in (comp, twin)]
    western = [(c, y, west) for y in (up, down, gy) for c in (comp, twin)]

    run = gx_size // 2
    last, foremost = lax.rem(gx, run) == run - 1, lax.rem(gx, run) == 0

    barrier = pltpu.get_barrier_semaphore()
    for target in western + [(twin, gy, gx)]:
        pl.semaphore_signal(barrier, inc=1, device_id=target, device_id_type=MESH)

    @pl.when(jnp.logical_not(last))
    def _():
        pl.semaphore_signal(barrier, inc=1, device_id=(0, up, gx), device_id_type=MESH)

    loads = [
        pltpu.make_async_copy(src, dst, load_sem.at[i])
        for i, (src, dst) in enumerate([(irr, irr_v), (land, land_v), (bottom, bottom_v), (state, raw)])
    ]
    for load in loads:
        load.start()

    by_barrier = jnp.logical_and(comp == 0, jnp.logical_not(last))
    pl.semaphore_wait(barrier, jnp.where(by_barrier, 9, 7))

    @pl.when(by_barrier)
    def _():
        pl.semaphore_signal(intro, inc=1, device_id=(0, down, gx), device_id_type=MESH)

    for target in eastern:
        pl.semaphore_signal(hello, inc=1, device_id=target, device_id_type=MESH)
    for load in loads:
        load.wait()

    lane, k = iota(1), iota(0)
    slot, quad = lane % 4, lane // 4
    blank = jnp.zeros((LEV, LANES), jnp.float32)

    for x in (2, 3, 0, 1):
        is_wet = (land_v[x : x + 1, :] == 1) & (k < bottom_v[x : x + 1, :])
        mine[8, OWN + x] = jnp.where(is_wet, jnp.broadcast_to(irr_v[x : x + 1, :], (LEV, LANES)), 0.0)
        for f in range(8):
            mine[f, OWN + x] = raw[pl.ds(f * 32 + x, 8, stride=4), :]

    def remote(index, src, dst, target):
        return pltpu.make_async_remote_copy(
            src_ref=src, dst_ref=dst, send_sem=send_sem.at[index], recv_sem=recv_sem.at[index],
            device_id=target, device_id_type=MESH,
        )

    ways = [(SW, 0, up, east), (SE, 0, up, west), (NW, 1, down, east), (NE, 1, down, west)]
    same_corners = [remote(s, packs.at[p], corners_in.at[0, s], (comp, y, x)) for s, p, y, x in ways]
    twin_corners = [remote(4 + s, packs.at[p], corners_in.at[1, s], (twin, y, x)) for s, p, y, x in ways]
    row_sends = [
        remote(8 + 2 * p + c, pairs.at[p], rows_in.at[p], (c, y, gx)) for p, y in ((0, up), (1, down)) for c in (0, 1)
    ]
    same_cols = [
        remote(12, mine.at[:, 4:6], mine.at[:, 0:2], (comp, gy, east)),
        remote(13, mine.at[:, 2:4], mine.at[:, 6:8], (comp, gy, west)),
    ]
    flow_cols = [
        remote(14, mine.at[0:8, 4:6], other.at[0:8, 0:2], (twin, gy, east)),
        remote(15, mine.at[0:8, 2:4], other.at[0:8, 6:8], (twin, gy, west)),
    ]
    plant_cols = [
        remote(14, mine.at[2:4, 5:6], other.at[2:4, 1:2], (twin, gy, east)),
        remote(15, mine.at[2:4, 2:3], other.at[2:4, 6:7], (twin, gy, west)),
    ]
    flow_own = remote(16, mine.at[0:8, 2:6], other.at[0:8, 2:6], (twin, gy, gx))
    plant_own = remote(16, mine.at[0:5, 2:6], other.at[0:5, 2:6], (twin, gy, gx))
    pack_own = remote(17, packs, pairs.at[:, 1], (twin, gy, gx))

    dyn_east = [same_corners[SW], twin_corners[SW], same_corners[NW], twin_corners[NW], same_cols[0], flow_cols[0]]
    dyn_west = [same_corners[SE], twin_corners[SE], same_corners[NE], twin_corners[NE], same_cols[1], flow_cols[1]]
    trc_east = [same_corners[SW], same_corners[NW], same_cols[0], plant_cols[0]]
    trc_west = [same_corners[SE], same_corners[NE], same_cols[1], plant_cols[1]]

    def start(copies):
        for copy in copies:
            copy.start()

    def arrived(copies):
        for copy in copies:
            copy.wait_recv()

    def sent(copies):
        for copy in copies:
            copy.wait_send()

    @pl.when(comp == 0)
    def _():
        start([same_cols[0], flow_cols[0]])

    @pl.when(comp == 1)
    def _():
        start([same_cols[0], plant_cols[0]])

    rows, lit_rows = blank, blank
    for x in range(4):
        for f in range(8):
            rows = jnp.where(quad == 4 * f + x, lanes(mine[f, OWN + x], 16 * f + 4 * x + 2), rows)
        lit_rows = jnp.where(quad == x, lanes(mine[8, OWN + x], 4 * x + 2), lit_rows)
    packs[0] = jnp.where(slot < 2, rows, lanes(lit_rows, 2))
    packs[1] = jnp.where(slot < 2, lanes(lit_rows, -2), rows)

    no_south, no_north = gy == 0, gy == gy_size - 1
    low = lane < 64
    inner = (lane % 64 >= 4) & (lane % 64 < 20)

    def keep(ref, edge_ref, f, value):
        ref[f] = value
        edge_ref[f] = row_edges(value)

    def lit_part(value, southern):
        return jnp.where(no_south if southern else no_north, 0.0, lanes(value, -2 if southern else 2))

    def other_rows_of(fields):
        result = blank
        for x in range(4):
            for f in fields:
                result = jnp.where(quad == 4 * f + x, lanes(other[f, OWN + x], 16 * f + 4 * x + 2), result)
        return result

    def start_strips(me, plants_only):
        def halves_of(own_rows, south, north):
            south = jnp.where(slot < 2, south, own_rows)
            north = lanes(jnp.where(slot < 2, own_rows, north), 64)
            return jnp.where(low, south, north), jnp.where(low, north, south)

        def put(ref, edge_ref, f, half, by):
            keep(ref, edge_ref, f, jnp.where(inner, lanes(half, by), 0.0))

        south, north = rows_in[0, me], rows_in[1, me]
        south_o, north_o = rows_in[0, 1 - me], rows_in[1, 1 - me]
        first, last = halves_of(rows, south, north)
        lit_first, _ = halves_of(lit_rows, lit_part(south, True), lit_part(north, False))
        put(strip, edges, 8, lit_first, 4)
        fields = (2, 3) if plants_only else range(8)
        halves = (first, last)
        halves_o = halves_of(other_rows_of(fields), south_o, north_o)
        for f in range(8):
            put(strip, edges, f, halves[f // 4], 4 - 16 * f)
        for f in fields:
            put(strip_o, edges_o, f, halves_o[f // 4], 4 - 16 * f)

    def add_corners(is_east, plants_only):
        left = 32 * is_east
        there = lane % 64 // 4 == 5 * is_east
        first = (lane >= left) & (lane < 64 + left)

        def halves_of(south, north):
            south, north = lanes(south, left), lanes(north, 64 + left)
            return jnp.where(first, south, north), jnp.where(first, north, south)

        def put(ref, edge_ref, f, half, by):
            keep(ref, edge_ref, f, jnp.where(there, lanes(half, by), ref[f]))

        south, north = corners_in[0, is_east], corners_in[0, 2 + is_east]
        lit_half, _ = halves_of(lit_part(south, True), lit_part(north, False))
        put(strip, edges, 8, lit_half, -12)
        halves = halves_of(south, north)
        for f in range(8):
            put(strip, edges, f, halves[f // 4], -12 - 16 * f)
        if not plants_only:
            halves_o = halves_of(corners_in[1, is_east], corners_in[1, 2 + is_east])
            for f in range(8):
                put(strip_o, edges_o, f, halves_o[f // 4], -12 - 16 * f)

    def wet_strip():
        return (strip[8] > 0).astype(jnp.float32)

    def wet_at(col, wet_edges):
        return wet_faces(around(lambda c: wet[0, c], wet_edges, col))

    first_row = gy * LANES
    coriolis_main = 0.3 + 0.4 * (first_row + lane).astype(jnp.float32) / float(gy_size * LANES)
    strip_row = first_row + slot + jnp.where(low, -2, LANES - 2)
    coriolis_strip = 0.3 + 0.4 * strip_row.astype(jnp.float32) / float(gy_size * LANES)

    def store_out(f, col, value):
        out[pl.ds(f * 32 + col - OWN, 8, stride=4), :] = value

    def full_step(now, before, p, wets, coriolis, heating):
        u, v = step_speeds(now, before, p, wets, coriolis)
        t, s = step_heat_salt(now, before, wets, heating)
        after = jnp.stack([u, v, t, s])
        return after, filtered(now[0], before[0], after, wets[0])

    def tracer_step(c, u, v, wets, temp, salt, lit):
        kappa = mixing_of(temp, salt, wets[0])
        light = light_of(c[0][2], c[0][3], lit)
        change = transported(c, u, v, wets) + mixed(c[0], kappa) + reactions(c[0], temp, light)
        return c[0] + 0.1 * change * wets[0]

    def dyn_strip():
        dry = wet_strip()
        p = around_strip(pressure_of(strip[2], strip[3], dry))
        heat = heating_of(strip_o[2], strip_o[3], strip[8], dry)
        now, before = around_strip(strip[0:4]), around_strip(strip[4:8])
        after, filt = full_step(now, before, p, wet_faces(around_strip(dry)), coriolis_strip, heat)
        nedges[0:4], nedges[4:8] = row_edges(after), row_edges(filt)
        nedges[8] = row_edges(pressure_of(after[2], after[3], dry))

    def dyn_first(col, wet_edges, press_edges):
        wets = wet_at(col, wet_edges)
        now = around(lambda c: mine[0:4, c], edges[0:4], col)
        before = around(lambda c: mine[4:8, c], edges[4:8], col)
        p = around(lambda c: press[0, c], press_edges, col)
        heat = heating_of(other[2, col], other[3, col], mine[8, col], wets[0])
        after, filt = full_step(now, before, p, wets, coriolis_main, heat)
        next_d[0:4, col], next_d[4:8, col] = after, filt
        press[1, col] = pressure_of(after[2], after[3], wets[0])

        if OWN <= col < OWN + 4:
            c = other[0:5, col]
            plants = around(lambda c: other[2:4, c], edges_o[2:4], col)
            kappa = mixing_of(now[0][2], now[0][3], wets[0])
            light = light_of(c[2], c[3], mine[8, col])
            change = transported(plants, *speeds_of(now), wets) + mixed(plants[0], kappa)
            change = change + plant_reactions(c, now[0][2], light)
            next_t[2:4, col] = plants[0] + 0.1 * change * wets[0]

    def dyn_second(col, wet_edges):
        wets = wet_at(col, wet_edges)
        now = around(lambda c: next_d[0:4, c], nedges[0:4], col)
        before = around(lambda c: next_d[4:8, c], nedges[4:8], col)
        p = around(lambda c: press[1, c], nedges[8], col)
        heat = heating_of(next_t[2, col], next_t[3, col], mine[8, col], wets[0])
        after, filt = full_step(now, before, p, wets, coriolis_main, heat)
        for f in range(4):
            store_out(f, col, after[f])
            store_out(4 + f, col, filt[f])

    def trc_strip():
        dry = wet_strip()
        wets = wet_faces(around_strip(dry))
        p = around_strip(pressure_of(strip_o[2], strip_o[3], dry))
        now, before = around_strip(strip_o[0:4]), around_strip(strip_o[4:6])
        u, v = step_speeds(now, before, p, wets, coriolis_strip)
        nedges[8], nedges[9] = row_edges(u), row_edges(v)
        c = around_strip(strip[0:8])
        nedges[0:8] = row_edges(tracer_step(c, *speeds_of(now), wets, strip_o[2], strip_o[3], strip[8]))

    def trc_first(col, wet_edges, press_edges):
        wets = wet_at(col, wet_edges)
        now = around(lambda c: other[0:4, c], edges_o[0:4], col)
        before = around(lambda c: other[4:8, c], edges_o[4:8], col)
        p = around(lambda c: press[0, c], press_edges, col)
        next_d[0, col], next_d[1, col] = step_speeds(now, before, p, wets, coriolis_main)
        c = around(lambda c: mine[0:8, c], edges[0:8], col)
        if OWN <= col < OWN + 4:
            heat = heating_of(c[0][2], c[0][3], mine[8, col], wets[0])
            next_d[2, col], next_d[3, col] = step_heat_salt(now, before, wets, heat)
        next_t[0:8, col] = tracer_step(c, *speeds_of(now), wets, now[0][2], now[0][3], mine[8, col])

    def trc_second(col, wet_edges):
        c = around(lambda c: next_t[0:8, c], nedges[0:8], col)
        u = around(lambda c: next_d[0, c], nedges[8], col)
        v = around(lambda c: next_d[1, c], nedges[9], col)
        new = tracer_step(
            c, u[:3], (v[0], v[3], v[4]), wet_at(col, wet_edges), next_d[2, col], next_d[3, col], mine[8, col]
        )
        for f in range(8):
            store_out(f, col, new[f])

    def phases(me, own_in, east_in, west_in, flow, flow_strip, first, at_strip, second):
        inputs = [own_in, row_sends[me], row_sends[2 + me]], east_in, west_in
        for it, (new, todo) in enumerate([(range(2, 6), (3, 4)), ((6, 7), (5, 6)), ((0, 1), (2, 1))]):
            arrived(inputs[it])
            if it == 0:
                start_strips(me, me == 0)
            else:
                add_corners(2 - it, me == 0)
            dry = wet_strip()
            wet_edges = row_edges(dry)
            press_edges = row_edges(pressure_of(flow_strip[2], flow_strip[3], dry))
            for col in new:
                is_wet = (mine[8, col] > 0).astype(jnp.float32)
                wet[0, col] = is_wet
                press[0, col] = pressure_of(flow[2, col], flow[3, col], is_wet)
            for col in todo:
                first(col, wet_edges, press_edges)
            if it > 0:
                at_strip()
                for col in (6 - 2 * it, 7 - 2 * it):
                    second(col, wet_edges)

    @pl.when(comp == 0)
    def _():
        start(dyn_east[:4] + [flow_own])
        pairs[0, 0] = packs[0]
        pairs[1, 0] = packs[1]
        arrived([pack_own])
        pl.semaphore_wait(intro, 1)
        start(row_sends)
        pl.semaphore_wait(hello, 6)
        start(dyn_west)
        east_in = [same_corners[SE], same_corners[NE], same_cols[1], plant_cols[1]]
        west_in = [same_corners[SW], same_corners[NW], same_cols[0], plant_cols[0]]
        phases(0, plant_own, east_in, west_in, mine, strip, dyn_first, dyn_strip, dyn_second)
        sent(dyn_east + [flow_own] + row_sends + dyn_west)

    @pl.when(comp == 1)
    def _():
        start(trc_east[:2] + [pack_own, plant_own])
        pl.semaphore_wait(hello, 6)

        @pl.when(foremost)
        def _():
            pl.semaphore_signal(intro, inc=1, device_id=(0, gy, west), device_id_type=MESH)

        start(trc_west)
        east_in = [same_corners[SE], same_corners[NE], twin_corners[SE], twin_corners[NE], same_cols[1], flow_cols[1]]
        west_in = [same_corners[SW], same_corners[NW], twin_corners[SW], twin_corners[NW], same_cols[0], flow_cols[0]]
        phases(1, flow_own, east_in, west_in, other, strip_o, trc_first, trc_strip, trc_second)
        sent([pack_own] + trc_east + [plant_own] + trc_west)


def solution(mesh):
    gy_size, gx_size = mesh.shape["gy"], mesh.shape["gx"]

    def local(ocean_state, irradiance, land_mask, bottom_level):
        rows = ocean_state.size // LANES
        anywhere = pl.BlockSpec(memory_space=pl.ANY)
        f32 = jnp.float32
        operands = (ocean_state.reshape(rows, LANES), irradiance, land_mask, bottom_level)
        result = pl.pallas_call(
            functools.partial(kernel, gy_size, gx_size),
            out_shape=jax.ShapeDtypeStruct((rows, LANES), f32),
            in_specs=[anywhere] * 4,
            out_specs=pl.BlockSpec(memory_space=pltpu.VMEM),
            scratch_shapes=[
                pltpu.VMEM((rows, LANES), f32),
                pltpu.VMEM((4, LANES), f32),
                pltpu.VMEM((4, LANES), jnp.int32),
                pltpu.VMEM((4, LANES), jnp.int32),
                pltpu.VMEM((9, 8, LEV, LANES), f32),
                pltpu.VMEM((8, 8, LEV, LANES), f32),
                pltpu.VMEM((2, LEV, LANES), f32),
                pltpu.VMEM((2, 2, LEV, LANES), f32),
                pltpu.VMEM((2, 4, LEV, LANES), f32),
                pltpu.VMEM((2, 2, LEV, LANES), f32),
                pltpu.VMEM((9, LEV, LANES), f32),
                pltpu.VMEM((9, LEV, LANES), f32),
                pltpu.VMEM((8, LEV, LANES), f32),
                pltpu.VMEM((8, LEV, LANES), f32),
                pltpu.VMEM((1, 8, LEV, LANES), f32),
                pltpu.VMEM((2, 8, LEV, LANES), f32),
                pltpu.VMEM((8, 8, LEV, LANES), f32),
                pltpu.VMEM((8, 8, LEV, LANES), f32),
                pltpu.VMEM((10, LEV, LANES), f32),
                pltpu.SemaphoreType.DMA((4,)),
                pltpu.SemaphoreType.DMA((18,)),
                pltpu.SemaphoreType.DMA((18,)),
                pltpu.SemaphoreType.REGULAR,
                pltpu.SemaphoreType.REGULAR,
            ],
            compiler_params=pltpu.CompilerParams(
                collective_id=0, has_side_effects=True, vmem_limit_bytes=8 * 1024 * 1024
            ),
            name="coupled_steps",
        )(*[pltpu.with_memory_space_constraint(a, pltpu.HBM) for a in operands])
        return result.reshape(ocean_state.shape)

    return jax.shard_map(
        local,
        mesh=mesh,
        in_specs=(P("comp", None, "gx", "gy"), P("gx", "gy"), P("gx", "gy"), P("gx", "gy")),
        out_specs=P("comp", None, "gx", "gy"),
        check_vma=False,
    )
```

```python
import functools

import jax
import jax.numpy as jnp
from jax import lax
from jax.experimental import pallas as pl
from jax.experimental.pallas import tpu as pltpu
from jax.sharding import PartitionSpec as P

MESH = pl.DeviceIdType.MESH

SW, SE, NW, NE = range(4)
OWN = 2
LEV, LANES = 8, 128


def roll(value, shift, axis):
    return pltpu.roll(value, shift % value.shape[axis] if isinstance(shift, int) else shift, axis)


def lanes(value, shift):
    return roll(value, shift, value.ndim - 1)


def levels(value, shift):
    return roll(value, shift, value.ndim - 2)


def iota(dim):
    return lax.broadcasted_iota(jnp.int32, (LEV, LANES), dim)


def level_sum(value):
    k = iota(0)
    for shift in (1, 2, 4):
        value = value + jnp.where(k >= shift, levels(value, shift), 0.0)
    return value


def density(temp, salt, wet):
    return (0.8 * salt - 0.2 * temp) * wet


def pressure_of(temp, salt, wet):
    return 0.1 * level_sum(density(temp, salt, wet))


def mixing_of(temp, salt, wet):
    rho = density(temp, salt, wet)
    strat = jnp.maximum(levels(rho, -1) - rho, 0.0)
    wet_below = jnp.where(iota(0) == LEV - 1, 0.0, levels(wet, -1))
    return (0.05 + 1.0 / (1.0 + 4.0 * strat)) * wet * wet_below


def absorbed(small, large):
    absorb = 0.08 + 0.05 * (jnp.abs(small) + jnp.abs(large))
    return absorb, level_sum(absorb)


def surface_of(lit):
    return jnp.broadcast_to(lit[0:1, :], (LEV, LANES))


def heating_of(small, large, lit, wet):
    absorb, column = absorbed(small, large)
    return surface_of(lit) * (jnp.exp(absorb - column) - jnp.exp(-column)) * wet


def light_of(small, large, lit):
    absorb, column = absorbed(small, large)
    return surface_of(lit) * jnp.exp(0.5 * absorb - column)


def gradients(p, wet):
    pc, pe, pw, pn, ps = p
    _, we, ww, wn, ws = wet
    return 0.5 * (we * (pe - pc) + ww * (pc - pw)), 0.5 * (wn * (pn - pc) + ws * (pc - ps))


def spread_of(field, wet):
    c, e, w, n, s = field
    _, we, ww, wn, ws = wet
    return we * (e - c) + ww * (w - c) + wn * (n - c) + ws * (s - c)


def faces(u, v, wet):
    (uc, ue, uw), (vc, vn, vs) = u, v
    _, we, ww, wn, ws = wet
    return 0.25 * (uc + ue) * we, 0.25 * (uc + uw) * ww, 0.25 * (vc + vn) * wn, 0.25 * (vc + vs) * ws


def carried_of(field, face):
    c, e, w, n, s = field
    fe, fw, fn, fs = face
    return fe * (c + e) - fw * (c + w) + fn * (c + n) - fs * (c + s)


def pick(five, index):
    return tuple(part[index] for part in five)


def step_speeds(now, before, p, wet, coriolis):
    force_east, force_north = gradients(p, wet)
    u, v = now[0][0], now[0][1]
    du = coriolis * v - force_east + 0.2 * spread_of(pick(before, 0), wet)
    dv = -coriolis * u - force_north + 0.2 * spread_of(pick(before, 1), wet)
    return before[0][0] + 0.2 * du * wet[0], before[0][1] + 0.2 * dv * wet[0]


def step_heat_salt(now, before, wet, heating):
    u = (now[0][0], now[1][0], now[2][0])
    v = (now[0][1], now[3][1], now[4][1])
    face = faces(u, v, wet)
    dt = -carried_of(pick(now, 2), face) + 0.2 * spread_of(pick(before, 2), wet) + 3.0 * heating
    ds = -carried_of(pick(now, 3), face) + 0.2 * spread_of(pick(before, 3), wet)
    return before[0][2] + 0.2 * dt * wet[0], before[0][3] + 0.2 * ds * wet[0]


def filtered(now, before, after, wet):
    return now + 0.1 * (before - 2.0 * now + after) * wet


def transported(field, u, v, wet):
    c, e, w, n, s = field
    _, we, ww, wn, ws = wet
    fe, fw, fn, fs = faces(u, v, wet)
    le, lw, ln, ls = 0.2 * we, 0.2 * ww, 0.2 * wn, 0.2 * ws
    own = (le + fe) + (lw - fw) + (ln + fn) + (ls - fs)
    return (le - fe) * e + (lw + fw) * w + (ln - fn) * n + (ls + fs) * s - own * c


def mixed(c, kappa):
    down = kappa * (levels(c, -1) - c)
    return down - levels(down, 1)


def growth_of(nitrate, ammonium, small, large, temp, light):
    rate = jnp.exp(0.06 * temp) * (light / (light + 0.5))
    both = jnp.abs(nitrate) + jnp.abs(ammonium)
    return 0.6 * rate * small / (0.2 + both), 0.9 * rate * large / (0.8 + both)


def reactions(c, temp, light):
    nn, na = jnp.abs(c[0]), jnp.abs(c[1])
    small, large = growth_of(c[0], c[1], c[2], c[3], temp, light)
    sn, sa, ln, la = small * nn, small * na, large * nn, large * na
    graze = 0.8 * c[4] / (1.0 + jnp.abs(c[2]) + jnp.abs(c[3]))
    gs, gl = graze * c[2], graze * c[3]
    remin = 0.3 * c[5] + 0.1 * c[6]
    nitrify = 0.2 * c[1]
    return jnp.stack(
        [
            nitrify - sn - ln,
            remin + 0.1 * c[4] - nitrify - sa - la,
            sn + sa - gs - 0.1 * c[2],
            ln + la - gl - 0.1 * c[3],
            0.7 * (gs + gl) - 0.1 * c[4] - 0.15 * c[4],
            0.1 * c[2] + 0.3 * gs - 0.3 * c[5],
            0.1 * c[3] + 0.15 * c[4] + 0.3 * gl - 0.1 * c[6],
            1.3 * (sn + sa + ln + la) - (remin + 2.0 * nitrify),
        ]
    )


def plant_reactions(c, temp, light):
    both = jnp.abs(c[0]) + jnp.abs(c[1])
    small, large = growth_of(c[0], c[1], c[2], c[3], temp, light)
    graze = 0.8 * c[4] / (1.0 + jnp.abs(c[2]) + jnp.abs(c[3]))
    return jnp.stack([small * both - graze * c[2] - 0.1 * c[2], large * both - graze * c[3] - 0.1 * c[3]])


def row_edges(strip):
    slot = iota(1) % 4
    return jnp.where(slot == 2, lanes(strip, 64), strip)


def around(columns, edges, col):
    lane = iota(1)
    c = columns(col)
    edge = lanes(edges, LANES - 2 - 4 * (col - 1))
    north = lanes(jnp.where(lane == 0, edge, c), -1)
    south = lanes(jnp.where(lane == LANES - 1, edge, c), 1)
    return c, columns(col + 1), columns(col - 1), north, south


def around_strip(strip):
    return strip, lanes(strip, -4), lanes(strip, 4), lanes(strip, -1), lanes(strip, 1)


def wet_faces(wet):
    c, e, w, n, s = wet
    return c, c * e, c * w, c * n, c * s


def speeds_of(now):
    return (now[0][0], now[1][0], now[2][0]), (now[0][1], now[3][1], now[4][1])


class Guarded:
    def __init__(self, copy, sends, receives):
        self.copy, self.sends, self.receives = copy, sends, receives

    def start(self):
        pl.when(self.sends)(self.copy.start)

    def wait_send(self):
        pl.when(self.sends)(self.copy.wait_send)

    def wait_recv(self):
        pl.when(self.receives)(self.copy.wait_recv)


def kernel(
    gy_size, gx_size, state, irr, land, bottom, out,
    raw, irr_v, land_v, bottom_v, mine, other, packs, pairs, corners_in, rows_in, strip, edges, strip_o, edges_o,
    wet, press, next_d, next_t, nedges,
    load_sem, send_sem, recv_sem, hello, intro,
):
    comp, gy, gx = (lax.axis_index(a) for a in ("comp", "gy", "gx"))
    east, west = lax.rem(gx + 1, gx_size), lax.rem(gx + gx_size - 1, gx_size)
    up, down = lax.rem(gy + 1, gy_size), lax.rem(gy + gy_size - 1, gy_size)
    twin = 1 - comp
    eastern = [(c, y, east) for y in (up, down, gy) for c in (comp, twin)]
    western = [(c, y, west) for y in (up, down, gy) for c in (comp, twin)]

    run = gx_size // 2
    last, foremost = lax.rem(gx, run) == run - 1, lax.rem(gx, run) == 0

    barrier = pltpu.get_barrier_semaphore()
    for target in western + [(twin, gy, gx)]:
        pl.semaphore_signal(barrier, inc=1, device_id=target, device_id_type=MESH)

    @pl.when(jnp.logical_not(last))
    def _():
        pl.semaphore_signal(barrier, inc=1, device_id=(0, up, gx), device_id_type=MESH)

    loads = [
        pltpu.make_async_copy(src, dst, load_sem.at[i])
        for i, (src, dst) in enumerate([(irr, irr_v), (land, land_v), (bottom, bottom_v), (state, raw)])
    ]
    for load in loads:
        load.start()

    by_barrier = jnp.logical_and(comp == 0, jnp.logical_not(last))
    pl.semaphore_wait(barrier, jnp.where(by_barrier, 9, 7))

    @pl.when(by_barrier)
    def _():
        pl.semaphore_signal(intro, inc=1, device_id=(0, down, gx), device_id_type=MESH)

    for target in eastern:
        pl.semaphore_signal(hello, inc=1, device_id=target, device_id_type=MESH)
    for load in loads:
        load.wait()

    lane, k = iota(1), iota(0)
    slot, quad = lane % 4, lane // 4
    blank = jnp.zeros((LEV, LANES), jnp.float32)

    for x in (2, 3, 0, 1):
        is_wet = (land_v[x : x + 1, :] == 1) & (k < bottom_v[x : x + 1, :])
        mine[8, OWN + x] = jnp.where(is_wet, jnp.broadcast_to(irr_v[x : x + 1, :], (LEV, LANES)), 0.0)
        for f in range(8):
            mine[f, OWN + x] = raw[pl.ds(f * 32 + x, 8, stride=4), :]

    def remote(index, src, dst, target):
        return pltpu.make_async_remote_copy(
            src_ref=src, dst_ref=dst, send_sem=send_sem.at[index], recv_sem=recv_sem.at[index],
            device_id=target, device_id_type=MESH,
        )

    ways = [(SW, 0, up, east), (SE, 0, up, west), (NW, 1, down, east), (NE, 1, down, west)]
    no_south, no_north = gy == 0, gy == gy_size - 1
    inside = [(gy < gy_size - 1, gy > 0), (gy > 0, gy < gy_size - 1)]
    same_corners = [
        Guarded(remote(s, packs.at[p], corners_in.at[0, s], (comp, y, x)), *inside[p]) for s, p, y, x in ways
    ]
    twin_corners = [
        Guarded(remote(4 + s, packs.at[p], corners_in.at[1, s], (twin, y, x)), *inside[p]) for s, p, y, x in ways
    ]

    @pl.when(no_south)
    def _():
        corners_in[:, SW : SE + 1] = jnp.zeros((2, 2, LEV, LANES), jnp.float32)

    @pl.when(no_north)
    def _():
        corners_in[:, NW : NE + 1] = jnp.zeros((2, 2, LEV, LANES), jnp.float32)

    row_sends = [
        remote(8 + 2 * p + c, pairs.at[p], rows_in.at[p], (c, y, gx)) for p, y in ((0, up), (1, down)) for c in (0, 1)
    ]
    same_cols = [
        remote(12, mine.at[:, 4:6], mine.at[:, 0:2], (comp, gy, east)),
        remote(13, mine.at[:, 2:4], mine.at[:, 6:8], (comp, gy, west)),
    ]
    flow_cols = [
        remote(14, mine.at[0:8, 4:6], other.at[0:8, 0:2], (twin, gy, east)),
        remote(15, mine.at[0:8, 2:4], other.at[0:8, 6:8], (twin, gy, west)),
    ]
    plant_cols = [
        remote(14, mine.at[2:4, 5:6], other.at[2:4, 1:2], (twin, gy, east)),
        remote(15, mine.at[2:4, 2:3], other.at[2:4, 6:7], (twin, gy, west)),
    ]
    flow_own = remote(16, mine.at[0:8, 2:6], other.at[0:8, 2:6], (twin, gy, gx))
    plant_own = remote(16, mine.at[0:5, 2:6], other.at[0:5, 2:6], (twin, gy, gx))
    pack_own = remote(17, packs, pairs.at[:, 1], (twin, gy, gx))

    dyn_east = [same_corners[SW], twin_corners[SW], same_corners[NW], twin_corners[NW], same_cols[0], flow_cols[0]]
    dyn_west = [same_corners[SE], twin_corners[SE], same_corners[NE], twin_corners[NE], same_cols[1], flow_cols[1]]
    trc_east = [same_corners[SW], same_corners[NW], same_cols[0], plant_cols[0]]
    trc_west = [same_corners[SE], same_corners[NE], same_cols[1], plant_cols[1]]

    def start(copies):
        for copy in copies:
            copy.start()

    def arrived(copies):
        for copy in copies:
            copy.wait_recv()

    def sent(copies):
        for copy in copies:
            copy.wait_send()

    @pl.when(comp == 0)
    def _():
        start([same_cols[0], flow_cols[0]])

    @pl.when(comp == 1)
    def _():
        start([same_cols[0], plant_cols[0]])

    rows, lit_rows = blank, blank
    for x in range(4):
        for f in range(8):
            rows = jnp.where(quad == 4 * f + x, lanes(mine[f, OWN + x], 16 * f + 4 * x + 2), rows)
        lit_rows = jnp.where(quad == x, lanes(mine[8, OWN + x], 4 * x + 2), lit_rows)
    packs[0] = jnp.where(slot < 2, rows, lanes(lit_rows, 2))
    packs[1] = jnp.where(slot < 2, lanes(lit_rows, -2), rows)

    low = lane < 64
    inner = (lane % 64 >= 4) & (lane % 64 < 20)

    def keep(ref, edge_ref, f, value):
        ref[f] = value
        edge_ref[f] = row_edges(value)

    def lit_part(value, southern):
        return jnp.where(no_south if southern else no_north, 0.0, lanes(value, -2 if southern else 2))

    def other_rows_of(fields):
        result = blank
        for x in range(4):
            for f in fields:
                result = jnp.where(quad == 4 * f + x, lanes(other[f, OWN + x], 16 * f + 4 * x + 2), result)
        return result

    def start_strips(me, plants_only):
        def halves_of(own_rows, south, north):
            south = jnp.where(slot < 2, south, own_rows)
            north = lanes(jnp.where(slot < 2, own_rows, north), 64)
            return jnp.where(low, south, north), jnp.where(low, north, south)

        def put(ref, edge_ref, f, half, by):
            keep(ref, edge_ref, f, jnp.where(inner, lanes(half, by), 0.0))

        south, north = rows_in[0, me], rows_in[1, me]
        south_o, north_o = rows_in[0, 1 - me], rows_in[1, 1 - me]
        first, last = halves_of(rows, south, north)
        lit_first, _ = halves_of(lit_rows, lit_part(south, True), lit_part(north, False))
        put(strip, edges, 8, lit_first, 4)
        fields = (2, 3) if plants_only else range(8)
        halves = (first, last)
        halves_o = halves_of(other_rows_of(fields), south_o, north_o)
        for f in range(8):
            put(strip, edges, f, halves[f // 4], 4 - 16 * f)
        for f in fields:
            put(strip_o, edges_o, f, halves_o[f // 4], 4 - 16 * f)

    def add_corners(is_east, plants_only):
        left = 32 * is_east
        there = lane % 64 // 4 == 5 * is_east
        first = (lane >= left) & (lane < 64 + left)

        def halves_of(south, north):
            south, north = lanes(south, left), lanes(north, 64 + left)
            return jnp.where(first, south, north), jnp.where(first, north, south)

        def put(ref, edge_ref, f, half, by):
            keep(ref, edge_ref, f, jnp.where(there, lanes(half, by), ref[f]))

        south, north = corners_in[0, is_east], corners_in[0, 2 + is_east]
        lit_half, _ = halves_of(lit_part(south, True), lit_part(north, False))
        put(strip, edges, 8, lit_half, -12)
        halves = halves_of(south, north)
        for f in range(8):
            put(strip, edges, f, halves[f // 4], -12 - 16 * f)
        if not plants_only:
            halves_o = halves_of(corners_in[1, is_east], corners_in[1, 2 + is_east])
            for f in range(8):
                put(strip_o, edges_o, f, halves_o[f // 4], -12 - 16 * f)

    def wet_strip():
        return (strip[8] > 0).astype(jnp.float32)

    def wet_at(col, wet_edges):
        return wet_faces(around(lambda c: wet[0, c], wet_edges, col))

    first_row = gy * LANES
    coriolis_main = 0.3 + 0.4 * (first_row + lane).astype(jnp.float32) / float(gy_size * LANES)
    strip_row = first_row + slot + jnp.where(low, -2, LANES - 2)
    coriolis_strip = 0.3 + 0.4 * strip_row.astype(jnp.float32) / float(gy_size * LANES)

    def store_out(f, col, value):
        out[pl.ds(f * 32 + col - OWN, 8, stride=4), :] = value

    def full_step(now, before, p, wets, coriolis, heating):
        u, v = step_speeds(now, before, p, wets, coriolis)
        t, s = step_heat_salt(now, before, wets, heating)
        after = jnp.stack([u, v, t, s])
        return after, filtered(now[0], before[0], after, wets[0])

    def tracer_step(c, u, v, wets, temp, salt, lit):
        kappa = mixing_of(temp, salt, wets[0])
        light = light_of(c[0][2], c[0][3], lit)
        change = transported(c, u, v, wets) + mixed(c[0], kappa) + reactions(c[0], temp, light)
        return c[0] + 0.1 * change * wets[0]

    def dyn_strip():
        dry = wet_strip()
        p = around_strip(pressure_of(strip[2], strip[3], dry))
        heat = heating_of(strip_o[2], strip_o[3], strip[8], dry)
        now, before = around_strip(strip[0:4]), around_strip(strip[4:8])
        after, filt = full_step(now, before, p, wet_faces(around_strip(dry)), coriolis_strip, heat)
        nedges[0:4], nedges[4:8] = row_edges(after), row_edges(filt)
        nedges[8] = row_edges(pressure_of(after[2], after[3], dry))

    def dyn_first(col, wet_edges, press_edges):
        wets = wet_at(col, wet_edges)
        now = around(lambda c: mine[0:4, c], edges[0:4], col)
        before = around(lambda c: mine[4:8, c], edges[4:8], col)
        p = around(lambda c: press[0, c], press_edges, col)
        heat = heating_of(other[2, col], other[3, col], mine[8, col], wets[0])
        after, filt = full_step(now, before, p, wets, coriolis_main, heat)
        next_d[0:4, col], next_d[4:8, col] = after, filt
        press[1, col] = pressure_of(after[2], after[3], wets[0])

        if OWN <= col < OWN + 4:
            c = other[0:5, col]
            plants = around(lambda c: other[2:4, c], edges_o[2:4], col)
            kappa = mixing_of(now[0][2], now[0][3], wets[0])
            light = light_of(c[2], c[3], mine[8, col])
            change = transported(plants, *speeds_of(now), wets) + mixed(plants[0], kappa)
            change = change + plant_reactions(c, now[0][2], light)
            next_t[2:4, col] = plants[0] + 0.1 * change * wets[0]

    def dyn_second(col, wet_edges):
        wets = wet_at(col, wet_edges)
        now = around(lambda c: next_d[0:4, c], nedges[0:4], col)
        before = around(lambda c: next_d[4:8, c], nedges[4:8], col)
        p = around(lambda c: press[1, c], nedges[8], col)
        heat = heating_of(next_t[2, col], next_t[3, col], mine[8, col], wets[0])
        after, filt = full_step(now, before, p, wets, coriolis_main, heat)
        for f in range(4):
            store_out(f, col, after[f])
            store_out(4 + f, col, filt[f])

    def trc_strip():
        dry = wet_strip()
        wets = wet_faces(around_strip(dry))
        p = around_strip(pressure_of(strip_o[2], strip_o[3], dry))
        now, before = around_strip(strip_o[0:4]), around_strip(strip_o[4:6])
        u, v = step_speeds(now, before, p, wets, coriolis_strip)
        nedges[8], nedges[9] = row_edges(u), row_edges(v)
        c = around_strip(strip[0:8])
        nedges[0:8] = row_edges(tracer_step(c, *speeds_of(now), wets, strip_o[2], strip_o[3], strip[8]))

    def trc_first(col, wet_edges, press_edges):
        wets = wet_at(col, wet_edges)
        now = around(lambda c: other[0:4, c], edges_o[0:4], col)
        before = around(lambda c: other[4:8, c], edges_o[4:8], col)
        p = around(lambda c: press[0, c], press_edges, col)
        next_d[0, col], next_d[1, col] = step_speeds(now, before, p, wets, coriolis_main)
        c = around(lambda c: mine[0:8, c], edges[0:8], col)
        if OWN <= col < OWN + 4:
            heat = heating_of(c[0][2], c[0][3], mine[8, col], wets[0])
            next_d[2, col], next_d[3, col] = step_heat_salt(now, before, wets, heat)
        next_t[0:8, col] = tracer_step(c, *speeds_of(now), wets, now[0][2], now[0][3], mine[8, col])

    def trc_second(col, wet_edges):
        c = around(lambda c: next_t[0:8, c], nedges[0:8], col)
        u = around(lambda c: next_d[0, c], nedges[8], col)
        v = around(lambda c: next_d[1, c], nedges[9], col)
        new = tracer_step(
            c, u[:3], (v[0], v[3], v[4]), wet_at(col, wet_edges), next_d[2, col], next_d[3, col], mine[8, col]
        )
        for f in range(8):
            store_out(f, col, new[f])

    def phases(me, own_in, east_in, west_in, flow, flow_strip, first, at_strip, second):
        inputs = [own_in, row_sends[me], row_sends[2 + me]], east_in, west_in
        for it, (new, todo) in enumerate([(range(2, 6), (3, 4)), ((6, 7), (5, 6)), ((0, 1), (2, 1))]):
            arrived(inputs[it])
            if it == 0:
                start_strips(me, me == 0)
            else:
                add_corners(2 - it, me == 0)
            dry = wet_strip()
            wet_edges = row_edges(dry)
            press_edges = row_edges(pressure_of(flow_strip[2], flow_strip[3], dry))
            for col in new:
                is_wet = (mine[8, col] > 0).astype(jnp.float32)
                wet[0, col] = is_wet
                press[0, col] = pressure_of(flow[2, col], flow[3, col], is_wet)
            for col in todo:
                first(col, wet_edges, press_edges)
            if it > 0:
                at_strip()
                for col in (6 - 2 * it, 7 - 2 * it):
                    second(col, wet_edges)

    @pl.when(comp == 0)
    def _():
        start(dyn_east[:4] + [flow_own])
        pairs[0, 0] = packs[0]
        pairs[1, 0] = packs[1]
        arrived([pack_own])
        pl.semaphore_wait(intro, 1)
        start(row_sends)
        pl.semaphore_wait(hello, 6)
        start(dyn_west)
        east_in = [same_corners[SE], same_corners[NE], same_cols[1], plant_cols[1]]
        west_in = [same_corners[SW], same_corners[NW], same_cols[0], plant_cols[0]]
        phases(0, plant_own, east_in, west_in, mine, strip, dyn_first, dyn_strip, dyn_second)
        sent(dyn_east + [flow_own] + row_sends + dyn_west)

    @pl.when(comp == 1)
    def _():
        start(trc_east[:2] + [pack_own, plant_own])
        pl.semaphore_wait(hello, 6)

        @pl.when(foremost)
        def _():
            pl.semaphore_signal(intro, inc=1, device_id=(0, gy, west), device_id_type=MESH)

        start(trc_west)
        east_in = [same_corners[SE], same_corners[NE], twin_corners[SE], twin_corners[NE], same_cols[1], flow_cols[1]]
        west_in = [same_corners[SW], same_corners[NW], twin_corners[SW], twin_corners[NW], same_cols[0], flow_cols[0]]
        phases(1, flow_own, east_in, west_in, other, strip_o, trc_first, trc_strip, trc_second)
        sent([pack_own] + trc_east + [plant_own] + trc_west)


def solution(mesh):
    gy_size, gx_size = mesh.shape["gy"], mesh.shape["gx"]

    def local(ocean_state, irradiance, land_mask, bottom_level):
        rows = ocean_state.size // LANES
        anywhere = pl.BlockSpec(memory_space=pl.ANY)
        f32 = jnp.float32
        operands = (ocean_state.reshape(rows, LANES), irradiance, land_mask, bottom_level)
        result = pl.pallas_call(
            functools.partial(kernel, gy_size, gx_size),
            out_shape=jax.ShapeDtypeStruct((rows, LANES), f32),
            in_specs=[anywhere] * 4,
            out_specs=pl.BlockSpec(memory_space=pltpu.VMEM),
            scratch_shapes=[
                pltpu.VMEM((rows, LANES), f32),
                pltpu.VMEM((4, LANES), f32),
                pltpu.VMEM((4, LANES), jnp.int32),
                pltpu.VMEM((4, LANES), jnp.int32),
                pltpu.VMEM((9, 8, LEV, LANES), f32),
                pltpu.VMEM((8, 8, LEV, LANES), f32),
                pltpu.VMEM((2, LEV, LANES), f32),
                pltpu.VMEM((2, 2, LEV, LANES), f32),
                pltpu.VMEM((2, 4, LEV, LANES), f32),
                pltpu.VMEM((2, 2, LEV, LANES), f32),
                pltpu.VMEM((9, LEV, LANES), f32),
                pltpu.VMEM((9, LEV, LANES), f32),
                pltpu.VMEM((8, LEV, LANES), f32),
                pltpu.VMEM((8, LEV, LANES), f32),
                pltpu.VMEM((1, 8, LEV, LANES), f32),
                pltpu.VMEM((2, 8, LEV, LANES), f32),
                pltpu.VMEM((8, 8, LEV, LANES), f32),
                pltpu.VMEM((8, 8, LEV, LANES), f32),
                pltpu.VMEM((10, LEV, LANES), f32),
                pltpu.SemaphoreType.DMA((4,)),
                pltpu.SemaphoreType.DMA((18,)),
                pltpu.SemaphoreType.DMA((18,)),
                pltpu.SemaphoreType.REGULAR,
                pltpu.SemaphoreType.REGULAR,
            ],
            compiler_params=pltpu.CompilerParams(
                collective_id=0, has_side_effects=True, vmem_limit_bytes=8 * 1024 * 1024
            ),
            name="coupled_steps",
        )(*[pltpu.with_memory_space_constraint(a, pltpu.HBM) for a in operands])
        return result.reshape(ocean_state.shape)

    return jax.shard_map(
        local,
        mesh=mesh,
        in_specs=(P("comp", None, "gx", "gy"), P("gx", "gy"), P("gx", "gy"), P("gx", "gy")),
        out_specs=P("comp", None, "gx", "gy"),
        check_vma=False,
    )
```

```python
import functools

import jax
import jax.numpy as jnp
from jax import lax
from jax.experimental import pallas as pl
from jax.experimental.pallas import tpu as pltpu
from jax.sharding import PartitionSpec as P

MESH = pl.DeviceIdType.MESH

SW, SE, NW, NE = range(4)
OWN = 2
LEV, LANES = 8, 128


def roll(value, shift, axis):
    return pltpu.roll(value, shift % value.shape[axis] if isinstance(shift, int) else shift, axis)


def lanes(value, shift):
    return roll(value, shift, value.ndim - 1)


def levels(value, shift):
    return roll(value, shift, value.ndim - 2)


def iota(dim):
    return lax.broadcasted_iota(jnp.int32, (LEV, LANES), dim)


def level_sum(value):
    k = iota(0)
    for shift in (1, 2, 4):
        value = value + jnp.where(k >= shift, levels(value, shift), 0.0)
    return value


def density(temp, salt, wet):
    return (0.8 * salt - 0.2 * temp) * wet


def pressure_of(temp, salt, wet):
    return 0.1 * level_sum(density(temp, salt, wet))


def mixing_of(temp, salt, wet):
    rho = density(temp, salt, wet)
    strat = jnp.maximum(levels(rho, -1) - rho, 0.0)
    wet_below = jnp.where(iota(0) == LEV - 1, 0.0, levels(wet, -1))
    return (0.05 + 1.0 / (1.0 + 4.0 * strat)) * wet * wet_below


def absorbed(small, large):
    absorb = 0.08 + 0.05 * (jnp.abs(small) + jnp.abs(large))
    return absorb, level_sum(absorb)


def surface_of(lit):
    return jnp.broadcast_to(lit[0:1, :], (LEV, LANES))


def heating_of(small, large, lit, wet):
    absorb, column = absorbed(small, large)
    return surface_of(lit) * (jnp.exp(absorb - column) - jnp.exp(-column)) * wet


def light_of(small, large, lit):
    absorb, column = absorbed(small, large)
    return surface_of(lit) * jnp.exp(0.5 * absorb - column)


def gradients(p, wet):
    pc, pe, pw, pn, ps = p
    _, we, ww, wn, ws = wet
    return 0.5 * (we * (pe - pc) + ww * (pc - pw)), 0.5 * (wn * (pn - pc) + ws * (pc - ps))


def spread_of(field, wet):
    c, e, w, n, s = field
    _, we, ww, wn, ws = wet
    return we * (e - c) + ww * (w - c) + wn * (n - c) + ws * (s - c)


def faces(u, v, wet):
    (uc, ue, uw), (vc, vn, vs) = u, v
    _, we, ww, wn, ws = wet
    return 0.25 * (uc + ue) * we, 0.25 * (uc + uw) * ww, 0.25 * (vc + vn) * wn, 0.25 * (vc + vs) * ws


def carried_of(field, face):
    c, e, w, n, s = field
    fe, fw, fn, fs = face
    return fe * (c + e) - fw * (c + w) + fn * (c + n) - fs * (c + s)


def pick(five, index):
    return tuple(part[index] for part in five)


def step_speeds(now, before, p, wet, coriolis):
    force_east, force_north = gradients(p, wet)
    u, v = now[0][0], now[0][1]
    du = coriolis * v - force_east + 0.2 * spread_of(pick(before, 0), wet)
    dv = -coriolis * u - force_north + 0.2 * spread_of(pick(before, 1), wet)
    return before[0][0] + 0.2 * du * wet[0], before[0][1] + 0.2 * dv * wet[0]


def step_heat_salt(now, before, wet, heating):
    u = (now[0][0], now[1][0], now[2][0])
    v = (now[0][1], now[3][1], now[4][1])
    face = faces(u, v, wet)
    dt = -carried_of(pick(now, 2), face) + 0.2 * spread_of(pick(before, 2), wet) + 3.0 * heating
    ds = -carried_of(pick(now, 3), face) + 0.2 * spread_of(pick(before, 3), wet)
    return before[0][2] + 0.2 * dt * wet[0], before[0][3] + 0.2 * ds * wet[0]


def filtered(now, before, after, wet):
    return now + 0.1 * (before - 2.0 * now + after) * wet


def transported(field, u, v, wet):
    c, e, w, n, s = field
    _, we, ww, wn, ws = wet
    fe, fw, fn, fs = faces(u, v, wet)
    le, lw, ln, ls = 0.2 * we, 0.2 * ww, 0.2 * wn, 0.2 * ws
    own = (le + fe) + (lw - fw) + (ln + fn) + (ls - fs)
    return (le - fe) * e + (lw + fw) * w + (ln - fn) * n + (ls + fs) * s - own * c


def mixed(c, kappa):
    down = kappa * (levels(c, -1) - c)
    return down - levels(down, 1)


def growth_of(nitrate, ammonium, small, large, temp, light):
    rate = jnp.exp(0.06 * temp) * (light / (light + 0.5))
    both = jnp.abs(nitrate) + jnp.abs(ammonium)
    return 0.6 * rate * small / (0.2 + both), 0.9 * rate * large / (0.8 + both)


def reactions(c, temp, light):
    nn, na = jnp.abs(c[0]), jnp.abs(c[1])
    small, large = growth_of(c[0], c[1], c[2], c[3], temp, light)
    sn, sa, ln, la = small * nn, small * na, large * nn, large * na
    graze = 0.8 * c[4] / (1.0 + jnp.abs(c[2]) + jnp.abs(c[3]))
    gs, gl = graze * c[2], graze * c[3]
    remin = 0.3 * c[5] + 0.1 * c[6]
    nitrify = 0.2 * c[1]
    return jnp.stack(
        [
            nitrify - sn - ln,
            remin + 0.1 * c[4] - nitrify - sa - la,
            sn + sa - gs - 0.1 * c[2],
            ln + la - gl - 0.1 * c[3],
            0.7 * (gs + gl) - 0.1 * c[4] - 0.15 * c[4],
            0.1 * c[2] + 0.3 * gs - 0.3 * c[5],
            0.1 * c[3] + 0.15 * c[4] + 0.3 * gl - 0.1 * c[6],
            1.3 * (sn + sa + ln + la) - (remin + 2.0 * nitrify),
        ]
    )


def plant_reactions(c, temp, light):
    both = jnp.abs(c[0]) + jnp.abs(c[1])
    small, large = growth_of(c[0], c[1], c[2], c[3], temp, light)
    graze = 0.8 * c[4] / (1.0 + jnp.abs(c[2]) + jnp.abs(c[3]))
    return jnp.stack([small * both - graze * c[2] - 0.1 * c[2], large * both - graze * c[3] - 0.1 * c[3]])


def row_edges(strip):
    slot = iota(1) % 4
    return jnp.where(slot == 2, lanes(strip, 64), strip)


def around(columns, edges, col):
    lane = iota(1)
    c = columns(col)
    edge = lanes(edges, LANES - 2 - 4 * (col - 1))
    north = lanes(jnp.where(lane == 0, edge, c), -1)
    south = lanes(jnp.where(lane == LANES - 1, edge, c), 1)
    return c, columns(col + 1), columns(col - 1), north, south


def around_strip(strip):
    return strip, lanes(strip, -4), lanes(strip, 4), lanes(strip, -1), lanes(strip, 1)


def wet_faces(wet):
    c, e, w, n, s = wet
    return c, c * e, c * w, c * n, c * s


def speeds_of(now):
    return (now[0][0], now[1][0], now[2][0]), (now[0][1], now[3][1], now[4][1])


class Guarded:
    def __init__(self, copy, sends, receives):
        self.copy, self.sends, self.receives = copy, sends, receives

    def start(self):
        pl.when(self.sends)(self.copy.start)

    def wait_send(self):
        pl.when(self.sends)(self.copy.wait_send)

    def wait_recv(self):
        pl.when(self.receives)(self.copy.wait_recv)


def kernel(
    gy_size, gx_size, state, irr, land, bottom, out,
    raw, irr_v, land_v, bottom_v, mine, other, packs, pairs, corners_in, rows_in, strip, edges, strip_o, edges_o,
    wet, press, next_d, next_t, nedges,
    load_sem, send_sem, recv_sem, hello, intro,
):
    comp, gy, gx = (lax.axis_index(a) for a in ("comp", "gy", "gx"))
    east, west = lax.rem(gx + 1, gx_size), lax.rem(gx + gx_size - 1, gx_size)
    up, down = lax.rem(gy + 1, gy_size), lax.rem(gy + gy_size - 1, gy_size)
    twin = 1 - comp
    eastern = [(c, y, east) for y in (up, down, gy) for c in (comp, twin)]
    western = [(c, y, west) for y in (up, down, gy) for c in (comp, twin)]

    loads = [
        pltpu.make_async_copy(src, dst, load_sem.at[i])
        for i, (src, dst) in enumerate([(state, raw), (irr, irr_v), (land, land_v), (bottom, bottom_v)])
    ]
    for load in loads:
        load.start()

    run = gx_size // 2
    last, foremost = lax.rem(gx, run) == run - 1, lax.rem(gx, run) == 0

    barrier = pltpu.get_barrier_semaphore()
    for target in western + [(twin, gy, gx)]:
        pl.semaphore_signal(barrier, inc=1, device_id=target, device_id_type=MESH)

    @pl.when(jnp.logical_not(last))
    def _():
        pl.semaphore_signal(barrier, inc=1, device_id=(0, up, gx), device_id_type=MESH)

    by_barrier = jnp.logical_and(comp == 0, jnp.logical_not(last))
    pl.semaphore_wait(barrier, jnp.where(by_barrier, 9, 7))

    @pl.when(by_barrier)
    def _():
        pl.semaphore_signal(intro, inc=1, device_id=(0, down, gx), device_id_type=MESH)

    for place, target in zip((1, 1, 0, 0, 2, 2), eastern):
        pl.semaphore_signal(hello.at[place], inc=1, device_id=target, device_id_type=MESH)
    for load in loads:
        load.wait()

    lane, k = iota(1), iota(0)
    slot, quad = lane % 4, lane // 4
    blank = jnp.zeros((LEV, LANES), jnp.float32)

    for x in (2, 3, 0, 1):
        is_wet = (land_v[x : x + 1, :] == 1) & (k < bottom_v[x : x + 1, :])
        mine[8, OWN + x] = jnp.where(is_wet, jnp.broadcast_to(irr_v[x : x + 1, :], (LEV, LANES)), 0.0)
        for f in range(8):
            mine[f, OWN + x] = raw[pl.ds(f * 32 + x, 8, stride=4), :]

    def remote(index, src, dst, target):
        return pltpu.make_async_remote_copy(
            src_ref=src, dst_ref=dst, send_sem=send_sem.at[index], recv_sem=recv_sem.at[index],
            device_id=target, device_id_type=MESH,
        )

    ways = [(SW, 0, up, east), (SE, 0, up, west), (NW, 1, down, east), (NE, 1, down, west)]
    no_south, no_north = gy == 0, gy == gy_size - 1
    inside = [(gy < gy_size - 1, gy > 0), (gy > 0, gy < gy_size - 1)]
    same_corners = [
        Guarded(remote(s, packs.at[p], corners_in.at[0, s], (comp, y, x)), *inside[p]) for s, p, y, x in ways
    ]
    twin_corners = [
        Guarded(remote(4 + s, packs.at[p], corners_in.at[1, s], (twin, y, x)), *inside[p]) for s, p, y, x in ways
    ]

    @pl.when(no_south)
    def _():
        corners_in[:, SW : SE + 1] = jnp.zeros((2, 2, LEV, LANES), jnp.float32)

    @pl.when(no_north)
    def _():
        corners_in[:, NW : NE + 1] = jnp.zeros((2, 2, LEV, LANES), jnp.float32)

    row_sends = [
        remote(8 + 2 * p + c, pairs.at[p], rows_in.at[p], (c, y, gx)) for p, y in ((0, up), (1, down)) for c in (0, 1)
    ]
    same_cols = [
        remote(12, mine.at[:, 4:6], mine.at[:, 0:2], (comp, gy, east)),
        remote(13, mine.at[:, 2:4], mine.at[:, 6:8], (comp, gy, west)),
    ]
    flow_cols = [
        remote(14, mine.at[0:8, 4:6], other.at[0:8, 0:2], (twin, gy, east)),
        remote(15, mine.at[0:8, 2:4], other.at[0:8, 6:8], (twin, gy, west)),
    ]
    plant_cols = [
        remote(14, mine.at[2:4, 5:6], other.at[2:4, 1:2], (twin, gy, east)),
        remote(15, mine.at[2:4, 2:3], other.at[2:4, 6:7], (twin, gy, west)),
    ]
    flow_own = remote(16, mine.at[0:8, 2:6], other.at[0:8, 2:6], (twin, gy, gx))
    plant_own = remote(16, mine.at[0:5, 2:6], other.at[0:5, 2:6], (twin, gy, gx))
    pack_own = remote(17, packs, pairs.at[:, 1], (twin, gy, gx))

    dyn_east = [same_corners[SW], twin_corners[SW], same_corners[NW], twin_corners[NW], same_cols[0], flow_cols[0]]
    dyn_west = [same_corners[SE], twin_corners[SE], same_corners[NE], twin_corners[NE], same_cols[1], flow_cols[1]]
    trc_east = [same_corners[SW], same_corners[NW], same_cols[0], plant_cols[0]]
    trc_west = [same_corners[SE], same_corners[NE], same_cols[1], plant_cols[1]]

    def start(copies):
        for copy in copies:
            copy.start()

    def arrived(copies):
        for copy in copies:
            copy.wait_recv()

    def sent(copies):
        for copy in copies:
            copy.wait_send()

    @pl.when(comp == 0)
    def _():
        start([flow_cols[0], same_cols[0]])

    @pl.when(comp == 1)
    def _():
        start([same_cols[0], plant_cols[0]])

    rows, lit_rows = blank, blank
    for x in range(4):
        for f in range(8):
            rows = jnp.where(quad == 4 * f + x, lanes(mine[f, OWN + x], 16 * f + 4 * x + 2), rows)
        lit_rows = jnp.where(quad == x, lanes(mine[8, OWN + x], 4 * x + 2), lit_rows)
    packs[0] = jnp.where(slot < 2, rows, lanes(lit_rows, 2))
    packs[1] = jnp.where(slot < 2, lanes(lit_rows, -2), rows)

    low = lane < 64
    inner = (lane % 64 >= 4) & (lane % 64 < 20)

    def keep(ref, edge_ref, f, value):
        ref[f] = value
        edge_ref[f] = row_edges(value)

    def lit_part(value, southern):
        return jnp.where(no_south if southern else no_north, 0.0, lanes(value, -2 if southern else 2))

    def other_rows_of(fields):
        result = blank
        for x in range(4):
            for f in fields:
                result = jnp.where(quad == 4 * f + x, lanes(other[f, OWN + x], 16 * f + 4 * x + 2), result)
        return result

    def start_strips(me, plants_only):
        def halves_of(own_rows, south, north):
            south = jnp.where(slot < 2, south, own_rows)
            north = lanes(jnp.where(slot < 2, own_rows, north), 64)
            return jnp.where(low, south, north), jnp.where(low, north, south)

        def put(ref, edge_ref, f, half, by):
            keep(ref, edge_ref, f, jnp.where(inner, lanes(half, by), 0.0))

        south, north = rows_in[0, me], rows_in[1, me]
        south_o, north_o = rows_in[0, 1 - me], rows_in[1, 1 - me]
        first, last = halves_of(rows, south, north)
        lit_first, _ = halves_of(lit_rows, lit_part(south, True), lit_part(north, False))
        put(strip, edges, 8, lit_first, 4)
        fields = (2, 3) if plants_only else range(8)
        halves = (first, last)
        halves_o = halves_of(other_rows_of(fields), south_o, north_o)
        for f in range(8):
            put(strip, edges, f, halves[f // 4], 4 - 16 * f)
        for f in fields:
            put(strip_o, edges_o, f, halves_o[f // 4], 4 - 16 * f)

    def add_corners(is_east, plants_only):
        left = 32 * is_east
        there = lane % 64 // 4 == 5 * is_east
        first = (lane >= left) & (lane < 64 + left)

        def halves_of(south, north):
            south, north = lanes(south, left), lanes(north, 64 + left)
            return jnp.where(first, south, north), jnp.where(first, north, south)

        def put(ref, edge_ref, f, half, by):
            keep(ref, edge_ref, f, jnp.where(there, lanes(half, by), ref[f]))

        south, north = corners_in[0, is_east], corners_in[0, 2 + is_east]
        lit_half, _ = halves_of(lit_part(south, True), lit_part(north, False))
        put(strip, edges, 8, lit_half, -12)
        halves = halves_of(south, north)
        for f in range(8):
            put(strip, edges, f, halves[f // 4], -12 - 16 * f)
        if not plants_only:
            halves_o = halves_of(corners_in[1, is_east], corners_in[1, 2 + is_east])
            for f in range(8):
                put(strip_o, edges_o, f, halves_o[f // 4], -12 - 16 * f)

    def wet_strip():
        return (strip[8] > 0).astype(jnp.float32)

    def wet_at(col, wet_edges):
        return wet_faces(around(lambda c: wet[0, c], wet_edges, col))

    first_row = gy * LANES
    coriolis_main = 0.3 + 0.4 * (first_row + lane).astype(jnp.float32) / float(gy_size * LANES)
    strip_row = first_row + slot + jnp.where(low, -2, LANES - 2)
    coriolis_strip = 0.3 + 0.4 * strip_row.astype(jnp.float32) / float(gy_size * LANES)

    def store_out(f, col, value):
        out[pl.ds(f * 32 + col - OWN, 8, stride=4), :] = value

    def full_step(now, before, p, wets, coriolis, heating):
        u, v = step_speeds(now, before, p, wets, coriolis)
        t, s = step_heat_salt(now, before, wets, heating)
        after = jnp.stack([u, v, t, s])
        return after, filtered(now[0], before[0], after, wets[0])

    def tracer_step(c, u, v, wets, temp, salt, lit):
        kappa = mixing_of(temp, salt, wets[0])
        light = light_of(c[0][2], c[0][3], lit)
        change = transported(c, u, v, wets) + mixed(c[0], kappa) + reactions(c[0], temp, light)
        return c[0] + 0.1 * change * wets[0]

    def dyn_strip():
        dry = wet_strip()
        p = around_strip(pressure_of(strip[2], strip[3], dry))
        heat = heating_of(strip_o[2], strip_o[3], strip[8], dry)
        now, before = around_strip(strip[0:4]), around_strip(strip[4:8])
        after, filt = full_step(now, before, p, wet_faces(around_strip(dry)), coriolis_strip, heat)
        nedges[0:4], nedges[4:8] = row_edges(after), row_edges(filt)
        nedges[8] = row_edges(pressure_of(after[2], after[3], dry))

    def dyn_first(col, wet_edges, press_edges):
        wets = wet_at(col, wet_edges)
        now = around(lambda c: mine[0:4, c], edges[0:4], col)
        before = around(lambda c: mine[4:8, c], edges[4:8], col)
        p = around(lambda c: press[0, c], press_edges, col)
        heat = heating_of(other[2, col], other[3, col], mine[8, col], wets[0])
        after, filt = full_step(now, before, p, wets, coriolis_main, heat)
        next_d[0:4, col], next_d[4:8, col] = after, filt
        press[1, col] = pressure_of(after[2], after[3], wets[0])

        if OWN <= col < OWN + 4:
            c = other[0:5, col]
            plants = around(lambda c: other[2:4, c], edges_o[2:4], col)
            kappa = mixing_of(now[0][2], now[0][3], wets[0])
            light = light_of(c[2], c[3], mine[8, col])
            change = transported(plants, *speeds_of(now), wets) + mixed(plants[0], kappa)
            change = change + plant_reactions(c, now[0][2], light)
            next_t[2:4, col] = plants[0] + 0.1 * change * wets[0]

    def dyn_second(col, wet_edges):
        wets = wet_at(col, wet_edges)
        now = around(lambda c: next_d[0:4, c], nedges[0:4], col)
        before = around(lambda c: next_d[4:8, c], nedges[4:8], col)
        p = around(lambda c: press[1, c], nedges[8], col)
        heat = heating_of(next_t[2, col], next_t[3, col], mine[8, col], wets[0])
        after, filt = full_step(now, before, p, wets, coriolis_main, heat)
        for f in range(4):
            store_out(f, col, after[f])
            store_out(4 + f, col, filt[f])

    def trc_strip():
        dry = wet_strip()
        wets = wet_faces(around_strip(dry))
        p = around_strip(pressure_of(strip_o[2], strip_o[3], dry))
        now, before = around_strip(strip_o[0:4]), around_strip(strip_o[4:6])
        u, v = step_speeds(now, before, p, wets, coriolis_strip)
        nedges[8], nedges[9] = row_edges(u), row_edges(v)
        c = around_strip(strip[0:8])
        nedges[0:8] = row_edges(tracer_step(c, *speeds_of(now), wets, strip_o[2], strip_o[3], strip[8]))

    def trc_first(col, wet_edges, press_edges):
        wets = wet_at(col, wet_edges)
        now = around(lambda c: other[0:4, c], edges_o[0:4], col)
        before = around(lambda c: other[4:8, c], edges_o[4:8], col)
        p = around(lambda c: press[0, c], press_edges, col)
        next_d[0, col], next_d[1, col] = step_speeds(now, before, p, wets, coriolis_main)
        c = around(lambda c: mine[0:8, c], edges[0:8], col)
        if OWN <= col < OWN + 4:
            heat = heating_of(c[0][2], c[0][3], mine[8, col], wets[0])
            next_d[2, col], next_d[3, col] = step_heat_salt(now, before, wets, heat)
        next_t[0:8, col] = tracer_step(c, *speeds_of(now), wets, now[0][2], now[0][3], mine[8, col])

    def trc_second(col, wet_edges):
        c = around(lambda c: next_t[0:8, c], nedges[0:8], col)
        u = around(lambda c: next_d[0, c], nedges[8], col)
        v = around(lambda c: next_d[1, c], nedges[9], col)
        new = tracer_step(
            c, u[:3], (v[0], v[3], v[4]), wet_at(col, wet_edges), next_d[2, col], next_d[3, col], mine[8, col]
        )
        for f in range(8):
            store_out(f, col, new[f])

    def phases(me, own_in, east_in, west_in, flow, flow_strip, first, at_strip, second):
        inputs = [own_in, row_sends[me], row_sends[2 + me]], east_in, west_in
        for it, (new, todo) in enumerate([(range(2, 6), (3, 4)), ((6, 7), (5, 6)), ((0, 1), (2, 1))]):
            arrived(inputs[it])
            if it == 0:
                start_strips(me, me == 0)
            else:
                add_corners(2 - it, me == 0)
            dry = wet_strip()
            wet_edges = row_edges(dry)
            press_edges = row_edges(pressure_of(flow_strip[2], flow_strip[3], dry))
            for col in new:
                is_wet = (mine[8, col] > 0).astype(jnp.float32)
                wet[0, col] = is_wet
                press[0, col] = pressure_of(flow[2, col], flow[3, col], is_wet)
            for col in todo:
                first(col, wet_edges, press_edges)
            if it > 0:
                at_strip()
                for col in (6 - 2 * it, 7 - 2 * it):
                    second(col, wet_edges)

    @pl.when(comp == 0)
    def _():
        start(dyn_east[:4] + [flow_own])
        pairs[0, 0] = packs[0]
        pairs[1, 0] = packs[1]
        arrived([pack_own])
        pl.semaphore_wait(intro, 1)
        start(row_sends)
        pl.semaphore_wait(hello.at[2], 2)
        start([flow_cols[1], same_cols[1]])
        pl.semaphore_wait(hello.at[0], 2)
        pl.semaphore_wait(hello.at[1], 2)
        start(dyn_west[:4])
        east_in = [same_corners[SE], same_corners[NE], same_cols[1], plant_cols[1]]
        west_in = [same_corners[SW], same_corners[NW], same_cols[0], plant_cols[0]]
        phases(0, plant_own, east_in, west_in, mine, strip, dyn_first, dyn_strip, dyn_second)
        sent(dyn_east + [flow_own] + row_sends + dyn_west)

    @pl.when(comp == 1)
    def _():
        start(trc_east[:2] + [pack_own, plant_own])
        pl.semaphore_wait(hello.at[2], 2)
        start(trc_west[2:])
        pl.semaphore_wait(hello.at[0], 2)
        pl.semaphore_wait(hello.at[1], 2)
        start(trc_west[:2])

        @pl.when(foremost)
        def _():
            pl.semaphore_signal(intro, inc=1, device_id=(0, gy, west), device_id_type=MESH)

        east_in = [same_corners[SE], same_corners[NE], twin_corners[SE], twin_corners[NE], same_cols[1], flow_cols[1]]
        west_in = [same_corners[SW], same_corners[NW], twin_corners[SW], twin_corners[NW], same_cols[0], flow_cols[0]]
        phases(1, flow_own, east_in, west_in, other, strip_o, trc_first, trc_strip, trc_second)
        sent([pack_own] + trc_east + [plant_own] + trc_west)


def solution(mesh):
    gy_size, gx_size = mesh.shape["gy"], mesh.shape["gx"]

    def local(ocean_state, irradiance, land_mask, bottom_level):
        rows = ocean_state.size // LANES
        anywhere = pl.BlockSpec(memory_space=pl.ANY)
        f32 = jnp.float32
        operands = (ocean_state.reshape(rows, LANES), irradiance, land_mask, bottom_level)
        result = pl.pallas_call(
            functools.partial(kernel, gy_size, gx_size),
            out_shape=jax.ShapeDtypeStruct((rows, LANES), f32),
            in_specs=[anywhere] * 4,
            out_specs=pl.BlockSpec(memory_space=pltpu.VMEM),
            scratch_shapes=[
                pltpu.VMEM((rows, LANES), f32),
                pltpu.VMEM((4, LANES), f32),
                pltpu.VMEM((4, LANES), jnp.int32),
                pltpu.VMEM((4, LANES), jnp.int32),
                pltpu.VMEM((9, 8, LEV, LANES), f32),
                pltpu.VMEM((8, 8, LEV, LANES), f32),
                pltpu.VMEM((2, LEV, LANES), f32),
                pltpu.VMEM((2, 2, LEV, LANES), f32),
                pltpu.VMEM((2, 4, LEV, LANES), f32),
                pltpu.VMEM((2, 2, LEV, LANES), f32),
                pltpu.VMEM((9, LEV, LANES), f32),
                pltpu.VMEM((9, LEV, LANES), f32),
                pltpu.VMEM((8, LEV, LANES), f32),
                pltpu.VMEM((8, LEV, LANES), f32),
                pltpu.VMEM((1, 8, LEV, LANES), f32),
                pltpu.VMEM((2, 8, LEV, LANES), f32),
                pltpu.VMEM((8, 8, LEV, LANES), f32),
                pltpu.VMEM((8, 8, LEV, LANES), f32),
                pltpu.VMEM((10, LEV, LANES), f32),
                pltpu.SemaphoreType.DMA((4,)),
                pltpu.SemaphoreType.DMA((18,)),
                pltpu.SemaphoreType.DMA((18,)),
                pltpu.SemaphoreType.REGULAR((3,)),
                pltpu.SemaphoreType.REGULAR,
            ],
            compiler_params=pltpu.CompilerParams(
                collective_id=0, has_side_effects=True, vmem_limit_bytes=8 * 1024 * 1024
            ),
            name="coupled_steps",
        )(*[pltpu.with_memory_space_constraint(a, pltpu.HBM) for a in operands])
        return result.reshape(ocean_state.shape)

    return jax.shard_map(
        local,
        mesh=mesh,
        in_specs=(P("comp", None, "gx", "gy"), P("gx", "gy"), P("gx", "gy"), P("gx", "gy")),
        out_specs=P("comp", None, "gx", "gy"),
        check_vma=False,
    )
```

```python
import functools

import jax
import jax.numpy as jnp
from jax import lax
from jax.experimental import pallas as pl
from jax.experimental.pallas import tpu as pltpu
from jax.sharding import PartitionSpec as P

MESH = pl.DeviceIdType.MESH

SW, SE, NW, NE = range(4)
OWN = 2
LEV, LANES = 8, 128


def roll(value, shift, axis):
    return pltpu.roll(value, shift % value.shape[axis] if isinstance(shift, int) else shift, axis)


def lanes(value, shift):
    return roll(value, shift, value.ndim - 1)


def levels(value, shift):
    return roll(value, shift, value.ndim - 2)


def iota(dim):
    return lax.broadcasted_iota(jnp.int32, (LEV, LANES), dim)


def level_sum(value):
    k = iota(0)
    for shift in (1, 2, 4):
        value = value + jnp.where(k >= shift, levels(value, shift), 0.0)
    return value


def density(temp, salt, wet):
    return (0.8 * salt - 0.2 * temp) * wet


def pressure_of(temp, salt, wet):
    return 0.1 * level_sum(density(temp, salt, wet))


def mixing_of(temp, salt, wet):
    rho = density(temp, salt, wet)
    strat = jnp.maximum(levels(rho, -1) - rho, 0.0)
    wet_below = jnp.where(iota(0) == LEV - 1, 0.0, levels(wet, -1))
    return (0.05 + 1.0 / (1.0 + 4.0 * strat)) * wet * wet_below


def absorbed(small, large):
    absorb = 0.08 + 0.05 * (jnp.abs(small) + jnp.abs(large))
    return absorb, level_sum(absorb)


def surface_of(lit):
    return jnp.broadcast_to(lit[0:1, :], (LEV, LANES))


def heating_of(small, large, lit, wet):
    absorb, column = absorbed(small, large)
    return surface_of(lit) * (jnp.exp(absorb - column) - jnp.exp(-column)) * wet


def light_of(small, large, lit):
    absorb, column = absorbed(small, large)
    return surface_of(lit) * jnp.exp(0.5 * absorb - column)


def gradients(p, wet):
    pc, pe, pw, pn, ps = p
    _, we, ww, wn, ws = wet
    return 0.5 * (we * (pe - pc) + ww * (pc - pw)), 0.5 * (wn * (pn - pc) + ws * (pc - ps))


def spread_of(field, wet):
    c, e, w, n, s = field
    _, we, ww, wn, ws = wet
    return we * (e - c) + ww * (w - c) + wn * (n - c) + ws * (s - c)


def faces(u, v, wet):
    (uc, ue, uw), (vc, vn, vs) = u, v
    _, we, ww, wn, ws = wet
    return 0.25 * (uc + ue) * we, 0.25 * (uc + uw) * ww, 0.25 * (vc + vn) * wn, 0.25 * (vc + vs) * ws


def carried_of(field, face):
    c, e, w, n, s = field
    fe, fw, fn, fs = face
    return fe * (c + e) - fw * (c + w) + fn * (c + n) - fs * (c + s)


def pick(five, index):
    return tuple(part[index] for part in five)


def step_speeds(now, before, p, wet, coriolis):
    force_east, force_north = gradients(p, wet)
    u, v = now[0][0], now[0][1]
    du = coriolis * v - force_east + 0.2 * spread_of(pick(before, 0), wet)
    dv = -coriolis * u - force_north + 0.2 * spread_of(pick(before, 1), wet)
    return before[0][0] + 0.2 * du * wet[0], before[0][1] + 0.2 * dv * wet[0]


def step_heat_salt(now, before, wet, heating):
    u = (now[0][0], now[1][0], now[2][0])
    v = (now[0][1], now[3][1], now[4][1])
    face = faces(u, v, wet)
    dt = -carried_of(pick(now, 2), face) + 0.2 * spread_of(pick(before, 2), wet) + 3.0 * heating
    ds = -carried_of(pick(now, 3), face) + 0.2 * spread_of(pick(before, 3), wet)
    return before[0][2] + 0.2 * dt * wet[0], before[0][3] + 0.2 * ds * wet[0]


def filtered(now, before, after, wet):
    return now + 0.1 * (before - 2.0 * now + after) * wet


def transported(field, u, v, wet):
    c, e, w, n, s = field
    _, we, ww, wn, ws = wet
    fe, fw, fn, fs = faces(u, v, wet)
    le, lw, ln, ls = 0.2 * we, 0.2 * ww, 0.2 * wn, 0.2 * ws
    own = (le + fe) + (lw - fw) + (ln + fn) + (ls - fs)
    return (le - fe) * e + (lw + fw) * w + (ln - fn) * n + (ls + fs) * s - own * c


def mixed(c, kappa):
    down = kappa * (levels(c, -1) - c)
    return down - levels(down, 1)


def growth_of(nitrate, ammonium, small, large, temp, light):
    rate = jnp.exp(0.06 * temp) * (light / (light + 0.5))
    both = jnp.abs(nitrate) + jnp.abs(ammonium)
    return 0.6 * rate * small / (0.2 + both), 0.9 * rate * large / (0.8 + both)


def reactions(c, temp, light):
    nn, na = jnp.abs(c[0]), jnp.abs(c[1])
    small, large = growth_of(c[0], c[1], c[2], c[3], temp, light)
    sn, sa, ln, la = small * nn, small * na, large * nn, large * na
    graze = 0.8 * c[4] / (1.0 + jnp.abs(c[2]) + jnp.abs(c[3]))
    gs, gl = graze * c[2], graze * c[3]
    remin = 0.3 * c[5] + 0.1 * c[6]
    nitrify = 0.2 * c[1]
    return jnp.stack(
        [
            nitrify - sn - ln,
            remin + 0.1 * c[4] - nitrify - sa - la,
            sn + sa - gs - 0.1 * c[2],
            ln + la - gl - 0.1 * c[3],
            0.7 * (gs + gl) - 0.1 * c[4] - 0.15 * c[4],
            0.1 * c[2] + 0.3 * gs - 0.3 * c[5],
            0.1 * c[3] + 0.15 * c[4] + 0.3 * gl - 0.1 * c[6],
            1.3 * (sn + sa + ln + la) - (remin + 2.0 * nitrify),
        ]
    )


def plant_reactions(c, temp, light):
    both = jnp.abs(c[0]) + jnp.abs(c[1])
    small, large = growth_of(c[0], c[1], c[2], c[3], temp, light)
    graze = 0.8 * c[4] / (1.0 + jnp.abs(c[2]) + jnp.abs(c[3]))
    return jnp.stack([small * both - graze * c[2] - 0.1 * c[2], large * both - graze * c[3] - 0.1 * c[3]])


def row_edges(strip):
    slot = iota(1) % 4
    return jnp.where(slot == 2, lanes(strip, 64), strip)


def around(columns, edges, col):
    lane = iota(1)
    c = columns(col)
    edge = lanes(edges, LANES - 2 - 4 * (col - 1))
    north = lanes(jnp.where(lane == 0, edge, c), -1)
    south = lanes(jnp.where(lane == LANES - 1, edge, c), 1)
    return c, columns(col + 1), columns(col - 1), north, south


def around_strip(strip):
    return strip, lanes(strip, -4), lanes(strip, 4), lanes(strip, -1), lanes(strip, 1)


def wet_faces(wet):
    c, e, w, n, s = wet
    return c, c * e, c * w, c * n, c * s


def speeds_of(now):
    return (now[0][0], now[1][0], now[2][0]), (now[0][1], now[3][1], now[4][1])


class Guarded:
    def __init__(self, copy, sends, receives):
        self.copy, self.sends, self.receives = copy, sends, receives

    def start(self):
        pl.when(self.sends)(self.copy.start)

    def wait_send(self):
        pl.when(self.sends)(self.copy.wait_send)

    def wait_recv(self):
        pl.when(self.receives)(self.copy.wait_recv)


def kernel(
    gy_size, gx_size, state, irr, land, bottom, out,
    raw, irr_v, land_v, bottom_v, mine, other, packs, pairs, corners_in, rows_in, strip, edges, strip_o, edges_o,
    wet, press, next_d, next_t, nedges,
    load_sem, send_sem, recv_sem, hello, intro,
):
    comp, gy, gx = (lax.axis_index(a) for a in ("comp", "gy", "gx"))
    east, west = lax.rem(gx + 1, gx_size), lax.rem(gx + gx_size - 1, gx_size)
    up, down = lax.rem(gy + 1, gy_size), lax.rem(gy + gy_size - 1, gy_size)
    twin = 1 - comp
    eastern = [(c, y, east) for y in (up, down, gy) for c in (comp, twin)]
    western = [(c, y, west) for y in (up, down, gy) for c in (comp, twin)]

    loads = [
        pltpu.make_async_copy(src, dst, load_sem.at[i])
        for i, (src, dst) in enumerate([(state, raw), (irr, irr_v), (land, land_v), (bottom, bottom_v)])
    ]
    for load in loads:
        load.start()

    run = gx_size // 2
    last, foremost = lax.rem(gx, run) == run - 1, lax.rem(gx, run) == 0

    barrier = pltpu.get_barrier_semaphore()
    for target in western + [(twin, gy, gx)]:
        pl.semaphore_signal(barrier, inc=1, device_id=target, device_id_type=MESH)

    @pl.when(jnp.logical_not(last))
    def _():
        pl.semaphore_signal(barrier, inc=1, device_id=(0, up, gx), device_id_type=MESH)

    by_barrier = jnp.logical_and(comp == 0, jnp.logical_not(last))
    pl.semaphore_wait(barrier, jnp.where(by_barrier, 9, 7))

    @pl.when(by_barrier)
    def _():
        pl.semaphore_signal(intro, inc=1, device_id=(0, down, gx), device_id_type=MESH)

    for place, target in zip((1, 1, 0, 0, 2, 2), eastern):
        pl.semaphore_signal(hello.at[place], inc=1, device_id=target, device_id_type=MESH)
    for load in loads:
        load.wait()

    lane, k = iota(1), iota(0)
    slot, quad = lane % 4, lane // 4
    blank = jnp.zeros((LEV, LANES), jnp.float32)

    for x in (2, 3, 0, 1):
        is_wet = (land_v[x : x + 1, :] == 1) & (k < bottom_v[x : x + 1, :])
        mine[8, OWN + x] = jnp.where(is_wet, jnp.broadcast_to(irr_v[x : x + 1, :], (LEV, LANES)), 0.0)
        for f in range(8):
            mine[f, OWN + x] = raw[pl.ds(f * 32 + x, 8, stride=4), :]

    def remote(index, src, dst, target):
        return pltpu.make_async_remote_copy(
            src_ref=src, dst_ref=dst, send_sem=send_sem.at[index], recv_sem=recv_sem.at[index],
            device_id=target, device_id_type=MESH,
        )

    ways = [(SW, 0, up, east), (SE, 0, up, west), (NW, 1, down, east), (NE, 1, down, west)]
    no_south, no_north = gy == 0, gy == gy_size - 1
    inside = [(gy < gy_size - 1, gy > 0), (gy > 0, gy < gy_size - 1)]
    same_corners = [
        Guarded(remote(s, packs.at[p], corners_in.at[0, s], (comp, y, x)), *inside[p]) for s, p, y, x in ways
    ]
    twin_corners = [
        Guarded(remote(4 + s, packs.at[p], corners_in.at[1, s], (twin, y, x)), *inside[p]) for s, p, y, x in ways
    ]

    @pl.when(no_south)
    def _():
        corners_in[:, SW : SE + 1] = jnp.zeros((2, 2, LEV, LANES), jnp.float32)

    @pl.when(no_north)
    def _():
        corners_in[:, NW : NE + 1] = jnp.zeros((2, 2, LEV, LANES), jnp.float32)

    row_sends = [
        remote(8 + 2 * p + c, pairs.at[p], rows_in.at[p], (c, y, gx)) for p, y in ((0, up), (1, down)) for c in (0, 1)
    ]
    same_cols = [
        remote(12, mine.at[:, 4:6], mine.at[:, 0:2], (comp, gy, east)),
        remote(13, mine.at[:, 2:4], mine.at[:, 6:8], (comp, gy, west)),
    ]
    flow_cols = [
        remote(14, mine.at[0:8, 4:6], other.at[0:8, 0:2], (twin, gy, east)),
        remote(15, mine.at[0:8, 2:4], other.at[0:8, 6:8], (twin, gy, west)),
    ]
    plant_cols = [
        remote(14, mine.at[2:4, 5:6], other.at[2:4, 1:2], (twin, gy, east)),
        remote(15, mine.at[2:4, 2:3], other.at[2:4, 6:7], (twin, gy, west)),
    ]
    flow_own = remote(16, mine.at[0:8, 2:6], other.at[0:8, 2:6], (twin, gy, gx))
    plant_own = remote(16, mine.at[0:5, 2:6], other.at[0:5, 2:6], (twin, gy, gx))
    pack_own = remote(17, packs, pairs.at[:, 1], (twin, gy, gx))

    dyn_east = [same_corners[SW], twin_corners[SW], same_corners[NW], twin_corners[NW], same_cols[0], flow_cols[0]]
    dyn_west = [same_corners[SE], twin_corners[SE], same_corners[NE], twin_corners[NE], same_cols[1], flow_cols[1]]
    trc_east = [same_corners[SW], same_corners[NW], same_cols[0], plant_cols[0]]
    trc_west = [same_corners[SE], same_corners[NE], same_cols[1], plant_cols[1]]

    def start(copies):
        for copy in copies:
            copy.start()

    def arrived(copies):
        for copy in copies:
            copy.wait_recv()

    def sent(copies):
        for copy in copies:
            copy.wait_send()

    @pl.when(comp == 0)
    def _():
        start([flow_cols[0], same_cols[0]])

    @pl.when(comp == 1)
    def _():
        start([plant_cols[0], same_cols[0]])

    rows, lit_rows = blank, blank
    for x in range(4):
        for f in range(8):
            rows = jnp.where(quad == 4 * f + x, lanes(mine[f, OWN + x], 16 * f + 4 * x + 2), rows)
        lit_rows = jnp.where(quad == x, lanes(mine[8, OWN + x], 4 * x + 2), lit_rows)
    packs[0] = jnp.where(slot < 2, rows, lanes(lit_rows, 2))
    packs[1] = jnp.where(slot < 2, lanes(lit_rows, -2), rows)

    low = lane < 64
    inner = (lane % 64 >= 4) & (lane % 64 < 20)

    def keep(ref, edge_ref, f, value):
        ref[f] = value
        edge_ref[f] = row_edges(value)

    def lit_part(value, southern):
        return jnp.where(no_south if southern else no_north, 0.0, lanes(value, -2 if southern else 2))

    def other_rows_of(fields):
        result = blank
        for x in range(4):
            for f in fields:
                result = jnp.where(quad == 4 * f + x, lanes(other[f, OWN + x], 16 * f + 4 * x + 2), result)
        return result

    def start_strips(me, plants_only):
        def halves_of(own_rows, south, north):
            south = jnp.where(slot < 2, south, own_rows)
            north = lanes(jnp.where(slot < 2, own_rows, north), 64)
            return jnp.where(low, south, north), jnp.where(low, north, south)

        def put(ref, edge_ref, f, half, by):
            keep(ref, edge_ref, f, jnp.where(inner, lanes(half, by), 0.0))

        south, north = rows_in[0, me], rows_in[1, me]
        south_o, north_o = rows_in[0, 1 - me], rows_in[1, 1 - me]
        first, last = halves_of(rows, south, north)
        lit_first, _ = halves_of(lit_rows, lit_part(south, True), lit_part(north, False))
        put(strip, edges, 8, lit_first, 4)
        fields = (2, 3) if plants_only else range(8)
        halves = (first, last)
        halves_o = halves_of(other_rows_of(fields), south_o, north_o)
        for f in range(8):
            put(strip, edges, f, halves[f // 4], 4 - 16 * f)
        for f in fields:
            put(strip_o, edges_o, f, halves_o[f // 4], 4 - 16 * f)

    def add_corners(is_east, plants_only):
        left = 32 * is_east
        there = lane % 64 // 4 == 5 * is_east
        first = (lane >= left) & (lane < 64 + left)

        def halves_of(south, north):
            south, north = lanes(south, left), lanes(north, 64 + left)
            return jnp.where(first, south, north), jnp.where(first, north, south)

        def put(ref, edge_ref, f, half, by):
            keep(ref, edge_ref, f, jnp.where(there, lanes(half, by), ref[f]))

        south, north = corners_in[0, is_east], corners_in[0, 2 + is_east]
        lit_half, _ = halves_of(lit_part(south, True), lit_part(north, False))
        put(strip, edges, 8, lit_half, -12)
        halves = halves_of(south, north)
        for f in range(8):
            put(strip, edges, f, halves[f // 4], -12 - 16 * f)
        if not plants_only:
            halves_o = halves_of(corners_in[1, is_east], corners_in[1, 2 + is_east])
            for f in range(8):
                put(strip_o, edges_o, f, halves_o[f // 4], -12 - 16 * f)

    def wet_strip():
        return (strip[8] > 0).astype(jnp.float32)

    def wet_at(col, wet_edges):
        return wet_faces(around(lambda c: wet[0, c], wet_edges, col))

    first_row = gy * LANES
    coriolis_main = 0.3 + 0.4 * (first_row + lane).astype(jnp.float32) / float(gy_size * LANES)
    strip_row = first_row + slot + jnp.where(low, -2, LANES - 2)
    coriolis_strip = 0.3 + 0.4 * strip_row.astype(jnp.float32) / float(gy_size * LANES)

    def store_out(f, col, value):
        out[pl.ds(f * 32 + col - OWN, 8, stride=4), :] = value

    def full_step(now, before, p, wets, coriolis, heating):
        u, v = step_speeds(now, before, p, wets, coriolis)
        t, s = step_heat_salt(now, before, wets, heating)
        after = jnp.stack([u, v, t, s])
        return after, filtered(now[0], before[0], after, wets[0])

    def tracer_step(c, u, v, wets, temp, salt, lit):
        kappa = mixing_of(temp, salt, wets[0])
        light = light_of(c[0][2], c[0][3], lit)
        change = transported(c, u, v, wets) + mixed(c[0], kappa) + reactions(c[0], temp, light)
        return c[0] + 0.1 * change * wets[0]

    def dyn_strip():
        dry = wet_strip()
        p = around_strip(pressure_of(strip[2], strip[3], dry))
        heat = heating_of(strip_o[2], strip_o[3], strip[8], dry)
        now, before = around_strip(strip[0:4]), around_strip(strip[4:8])
        after, filt = full_step(now, before, p, wet_faces(around_strip(dry)), coriolis_strip, heat)
        nedges[0:4], nedges[4:8] = row_edges(after), row_edges(filt)
        nedges[8] = row_edges(pressure_of(after[2], after[3], dry))

    def dyn_first(col, wet_edges, press_edges):
        wets = wet_at(col, wet_edges)
        now = around(lambda c: mine[0:4, c], edges[0:4], col)
        before = around(lambda c: mine[4:8, c], edges[4:8], col)
        p = around(lambda c: press[0, c], press_edges, col)
        heat = heating_of(other[2, col], other[3, col], mine[8, col], wets[0])
        after, filt = full_step(now, before, p, wets, coriolis_main, heat)
        next_d[0:4, col], next_d[4:8, col] = after, filt
        press[1, col] = pressure_of(after[2], after[3], wets[0])

        if OWN <= col < OWN + 4:
            c = other[0:5, col]
            plants = around(lambda c: other[2:4, c], edges_o[2:4], col)
            kappa = mixing_of(now[0][2], now[0][3], wets[0])
            light = light_of(c[2], c[3], mine[8, col])
            change = transported(plants, *speeds_of(now), wets) + mixed(plants[0], kappa)
            change = change + plant_reactions(c, now[0][2], light)
            next_t[2:4, col] = plants[0] + 0.1 * change * wets[0]

    def dyn_second(col, wet_edges):
        wets = wet_at(col, wet_edges)
        now = around(lambda c: next_d[0:4, c], nedges[0:4], col)
        before = around(lambda c: next_d[4:8, c], nedges[4:8], col)
        p = around(lambda c: press[1, c], nedges[8], col)
        heat = heating_of(next_t[2, col], next_t[3, col], mine[8, col], wets[0])
        after, filt = full_step(now, before, p, wets, coriolis_main, heat)
        for f in range(4):
            store_out(f, col, after[f])
            store_out(4 + f, col, filt[f])

    def trc_strip():
        dry = wet_strip()
        wets = wet_faces(around_strip(dry))
        p = around_strip(pressure_of(strip_o[2], strip_o[3], dry))
        now, before = around_strip(strip_o[0:4]), around_strip(strip_o[4:6])
        u, v = step_speeds(now, before, p, wets, coriolis_strip)
        nedges[8], nedges[9] = row_edges(u), row_edges(v)
        c = around_strip(strip[0:8])
        nedges[0:8] = row_edges(tracer_step(c, *speeds_of(now), wets, strip_o[2], strip_o[3], strip[8]))

    def trc_first(col, wet_edges, press_edges):
        wets = wet_at(col, wet_edges)
        now = around(lambda c: other[0:4, c], edges_o[0:4], col)
        before = around(lambda c: other[4:8, c], edges_o[4:8], col)
        p = around(lambda c: press[0, c], press_edges, col)
        next_d[0, col], next_d[1, col] = step_speeds(now, before, p, wets, coriolis_main)
        c = around(lambda c: mine[0:8, c], edges[0:8], col)
        if OWN <= col < OWN + 4:
            heat = heating_of(c[0][2], c[0][3], mine[8, col], wets[0])
            next_d[2, col], next_d[3, col] = step_heat_salt(now, before, wets, heat)
        next_t[0:8, col] = tracer_step(c, *speeds_of(now), wets, now[0][2], now[0][3], mine[8, col])

    def trc_second(col, wet_edges):
        c = around(lambda c: next_t[0:8, c], nedges[0:8], col)
        u = around(lambda c: next_d[0, c], nedges[8], col)
        v = around(lambda c: next_d[1, c], nedges[9], col)
        new = tracer_step(
            c, u[:3], (v[0], v[3], v[4]), wet_at(col, wet_edges), next_d[2, col], next_d[3, col], mine[8, col]
        )
        for f in range(8):
            store_out(f, col, new[f])

    def phases(me, own_in, east_in, west_in, flow, flow_strip, first, at_strip, second):
        inputs = [own_in, row_sends[me], row_sends[2 + me]], east_in, west_in
        for it, (new, todo) in enumerate([(range(2, 6), (3, 4)), ((6, 7), (5, 6)), ((0, 1), (2, 1))]):
            arrived(inputs[it])
            if it == 0:
                start_strips(me, me == 0)
            else:
                add_corners(2 - it, me == 0)
            dry = wet_strip()
            wet_edges = row_edges(dry)
            press_edges = row_edges(pressure_of(flow_strip[2], flow_strip[3], dry))
            for col in new:
                is_wet = (mine[8, col] > 0).astype(jnp.float32)
                wet[0, col] = is_wet
                press[0, col] = pressure_of(flow[2, col], flow[3, col], is_wet)
            for col in todo:
                first(col, wet_edges, press_edges)
            if it > 0:
                at_strip()
                for col in (6 - 2 * it, 7 - 2 * it):
                    second(col, wet_edges)

    @pl.when(comp == 0)
    def _():
        start(dyn_east[:4] + [flow_own])
        pairs[0, 0] = packs[0]
        pairs[1, 0] = packs[1]
        arrived([pack_own])
        pl.semaphore_wait(intro, 1)
        start(row_sends)
        pl.semaphore_wait(hello.at[2], 2)
        start([flow_cols[1], same_cols[1]])
        pl.semaphore_wait(hello.at[0], 2)
        pl.semaphore_wait(hello.at[1], 2)
        start(dyn_west[:4])
        east_in = [same_corners[SE], same_corners[NE], same_cols[1], plant_cols[1]]
        west_in = [same_corners[SW], same_corners[NW], same_cols[0], plant_cols[0]]
        phases(0, plant_own, east_in, west_in, mine, strip, dyn_first, dyn_strip, dyn_second)
        sent(dyn_east + [flow_own] + row_sends + dyn_west)

    @pl.when(comp == 1)
    def _():
        start(trc_east[:2] + [pack_own, plant_own])
        pl.semaphore_wait(hello.at[2], 2)
        start(trc_west[2:])
        pl.semaphore_wait(hello.at[0], 2)
        pl.semaphore_wait(hello.at[1], 2)
        start(trc_west[:2])

        @pl.when(foremost)
        def _():
            pl.semaphore_signal(intro, inc=1, device_id=(0, gy, west), device_id_type=MESH)

        east_in = [same_corners[SE], same_corners[NE], twin_corners[SE], twin_corners[NE], same_cols[1], flow_cols[1]]
        west_in = [same_corners[SW], same_corners[NW], twin_corners[SW], twin_corners[NW], same_cols[0], flow_cols[0]]
        phases(1, flow_own, east_in, west_in, other, strip_o, trc_first, trc_strip, trc_second)
        sent([pack_own] + trc_east + [plant_own] + trc_west)


def solution(mesh):
    gy_size, gx_size = mesh.shape["gy"], mesh.shape["gx"]

    def local(ocean_state, irradiance, land_mask, bottom_level):
        rows = ocean_state.size // LANES
        anywhere = pl.BlockSpec(memory_space=pl.ANY)
        f32 = jnp.float32
        operands = (ocean_state.reshape(rows, LANES), irradiance, land_mask, bottom_level)
        result = pl.pallas_call(
            functools.partial(kernel, gy_size, gx_size),
            out_shape=jax.ShapeDtypeStruct((rows, LANES), f32),
            in_specs=[anywhere] * 4,
            out_specs=pl.BlockSpec(memory_space=pltpu.VMEM),
            scratch_shapes=[
                pltpu.VMEM((rows, LANES), f32),
                pltpu.VMEM((4, LANES), f32),
                pltpu.VMEM((4, LANES), jnp.int32),
                pltpu.VMEM((4, LANES), jnp.int32),
                pltpu.VMEM((9, 8, LEV, LANES), f32),
                pltpu.VMEM((8, 8, LEV, LANES), f32),
                pltpu.VMEM((2, LEV, LANES), f32),
                pltpu.VMEM((2, 2, LEV, LANES), f32),
                pltpu.VMEM((2, 4, LEV, LANES), f32),
                pltpu.VMEM((2, 2, LEV, LANES), f32),
                pltpu.VMEM((9, LEV, LANES), f32),
                pltpu.VMEM((9, LEV, LANES), f32),
                pltpu.VMEM((8, LEV, LANES), f32),
                pltpu.VMEM((8, LEV, LANES), f32),
                pltpu.VMEM((1, 8, LEV, LANES), f32),
                pltpu.VMEM((2, 8, LEV, LANES), f32),
                pltpu.VMEM((8, 8, LEV, LANES), f32),
                pltpu.VMEM((8, 8, LEV, LANES), f32),
                pltpu.VMEM((10, LEV, LANES), f32),
                pltpu.SemaphoreType.DMA((4,)),
                pltpu.SemaphoreType.DMA((18,)),
                pltpu.SemaphoreType.DMA((18,)),
                pltpu.SemaphoreType.REGULAR((3,)),
                pltpu.SemaphoreType.REGULAR,
            ],
            compiler_params=pltpu.CompilerParams(
                collective_id=0, has_side_effects=True, vmem_limit_bytes=8 * 1024 * 1024
            ),
            name="coupled_steps",
        )(*[pltpu.with_memory_space_constraint(a, pltpu.HBM) for a in operands])
        return result.reshape(ocean_state.shape)

    return jax.shard_map(
        local,
        mesh=mesh,
        in_specs=(P("comp", None, "gx", "gy"), P("gx", "gy"), P("gx", "gy"), P("gx", "gy")),
        out_specs=P("comp", None, "gx", "gy"),
        check_vma=False,
    )
```
